32 devices in a mesh: sub: 8 (over z, core), slab: 4 (over y, x).
Axes of the slice: x: 2, y: 2, z: 4, core: 2. Of those that a mesh axis runs over, the one named last changes fastest.
Arguments:
- interface_rhs: float32 [8, 4, 3, 8, 3, 128], P('sub', 'slab'), may hold values from -180 to 180
- order: int32 [8, 4, 3, 768], P('sub', 'slab'), may hold values from 0 to 767, each once within a row
- inverse_rr: bfloat16 [8, 4, 3, 768, 768], P('sub', 'slab'), may hold values from -1 to 6, as said below
- corner_response: bfloat16 [8, 4, 3, 8, 768], P('sub', 'slab'), may hold values from -1.5 to 1.5
- corners: int32 [8, 4, 3, 8], P('sub', 'slab'), may hold values from 0 to 95, as said below
- coarse_factor: float32 [96, 96], P('slab'), may hold values from -1 to 2, as said below
Outputs:
- multipliers: float32 [8, 4, 3, 8, 3, 128], P('sub', 'slab')
- residual: float32 [8, 4, 3, 8, 3, 128], P('sub', 'slab')
The draws below stay inside these ranges and needn't reach their ends.
Inputs may be any that keep to these rules, and one draw needn't show every extreme that they name: `corners`: each subdomain lists the numbers of its corner vertices at the offsets (0,0,0), (0,0,1), (0,1,0), (0,1,1), (1,0,0), (1,0,1), (1,1,0), (1,1,1) along the three grid dimensions; the vertices of the periodic grid of subdomains carry the numbers 0 to 95, each once, and all subdomains that meet at a vertex list its number. `coarse_factor`: lower triangular with a positive diagonal. `inverse_rr`: each subdomain's matrix is symmetric and positive definite.
All inputs are finite; a program needn't handle non-finite values.
Results may differ from the reference program's by a relative error of at most 0.014.
Values sent between devices are 32-bit elements; how exact they have to be, the bound alone decides.
No kernel may reach another device: no remote copies, remote signals or barrier semaphores. Data moves between devices by JAX's collectives and lax.ppermute only.
A program may use at most 128 MiB of HBM per device.

```python
import math
import jax
import jax.numpy as jnp
from jax import lax

FACE = 128
RHS = 8
ITERS = 3
NSX = 8
NSY = 4
NSZ = 3
NCOARSE = 96


def draw_interface_rhs(key, part):
    key = jax.random.fold_in(key, 5)
    subkeys = jax.random.split(key, 3)
    full_shape = (NSX, NSY, NSZ, RHS, 3, FACE)
    block_scale = jnp.exp(jax.random.uniform(subkeys[0], (NSX, NSY, NSZ, RHS, 1, 1), jnp.float32, 0.0, math.log(10.0)))
    slot_scale = jnp.exp(jax.random.uniform(subkeys[1], (1, 1, 1, 1, 3, FACE), jnp.float32, 0.0, math.log(10.0)))
    first_pos = jnp.arange(NSX, dtype=jnp.float32).reshape(NSX, 1, 1, 1, 1, 1)
    second_pos = jnp.arange(NSY, dtype=jnp.float32).reshape(1, NSY, 1, 1, 1, 1)
    trend = (1.0 + 2.0 * first_pos / NSX) * (1.0 + 2.0 * second_pos / NSY)
    base = jnp.clip(jax.random.normal(subkeys[2], full_shape, jnp.float32), -6.0, 6.0)
    return base * block_scale * slot_scale * trend / 30.0


def draw_inverse_rr(key, part):
    key = jax.random.fold_in(key, 9)
    local_size = 6 * FACE
    subdomains = NSX * NSY * NSZ
    limit = 1.5 / local_size ** 0.5
    rows_idx = jnp.arange(local_size).reshape(local_size, 1)
    cols_idx = jnp.arange(local_size).reshape(1, local_size)
    identity = (rows_idx == cols_idx).astype(jnp.float32)

    def one_matrix(index):
        sub_key = jax.random.fold_in(key, index)
        first_key, second_key = jax.random.split(sub_key)
        raw = jax.random.uniform(first_key, (local_size, local_size), jnp.float32, -limit, limit)
        symmetric = (raw + raw.T) * 0.70710678
        diagonal = jnp.exp(jax.random.uniform(second_key, (local_size,), jnp.float32, math.log(3.0), math.log(6.0)))
        matrix = symmetric * (1.0 - identity) + diagonal.reshape(1, local_size) * identity
        return matrix.astype(jnp.bfloat16)
    stacked = lax.map(one_matrix, jnp.arange(subdomains))
    return stacked.reshape(NSX, NSY, NSZ, local_size, local_size)


def draw_corners(key, part):
    key = jax.random.fold_in(key, 11)
    numbering = jax.random.permutation(key, NCOARSE).astype(jnp.int32).reshape(NSX, NSY, NSZ)
    listed = []
    for first_off in (0, 1):
        for second_off in (0, 1):
            for third_off in (0, 1):
                listed.append(jnp.roll(numbering, (-first_off, -second_off, -third_off), axis=(0, 1, 2)))
    return jnp.stack(listed, axis=-1).astype(jnp.int32)


def draw_coarse_factor(key, part):
    key = jax.random.fold_in(key, 7)
    subkeys = jax.random.split(key, 2)
    limit = 0.7 / NCOARSE ** 0.5
    diagonal = jnp.exp(jax.random.uniform(subkeys[0], (NCOARSE,), jnp.float32, 0.0, math.log(2.0)))
    lower_part = jax.random.uniform(subkeys[1], (NCOARSE, NCOARSE), jnp.float32, -limit, limit)
    return jnp.tril(lower_part, -1) + jnp.diag(diagonal)


def shard_levels(key, extent, cuts, least, top_value):
    level = 1.0
    for axis_at, shards_of in cuts:
        steps = jax.random.uniform(jax.random.fold_in(jax.random.fold_in(key, 6), axis_at), (shards_of,), jnp.float32, least / len(cuts), top_value / len(cuts))
        level = level * jnp.repeat(jnp.exp(steps), extent[axis_at] // shards_of).reshape((-1,) + (1,) * (len(extent) - 1 - axis_at))
    return level


def gaussian(own_key, shape, deviation, bound, shards=(), kind=jnp.bfloat16):
    loudness = shard_levels(own_key, shape, shards, -0.22, 0.18) if shards else 1.0
    array = jax.random.normal(own_key, shape, jnp.float32) * deviation * loudness
    return jnp.minimum(jnp.maximum(array, -bound), bound).astype(kind)


def setup_inputs(seed: int = 0) -> dict:
    keys = jax.random.split(jax.random.key(seed), 7)
    interface_rhs = draw_interface_rhs(jax.random.fold_in(keys[6], 71), 0)
    order = jax.vmap(lambda own: jax.random.permutation(own, 6 * FACE))(jax.random.split(keys[1], NSX * NSY * NSZ)).reshape((NSX, NSY, NSZ, 6 * FACE)).astype(jnp.int32)
    inverse_rr = draw_inverse_rr(jax.random.fold_in(keys[6], 71), 0)
    corner_response = gaussian(keys[3], (NSX, NSY, NSZ, 8, 6 * FACE), (3.0 / (6 * FACE) ** 0.5), 1.5, ((0, 8), (1, 4)))
    corners = draw_corners(jax.random.fold_in(keys[6], 71), 0)
    coarse_factor = draw_coarse_factor(jax.random.fold_in(keys[6], 71), 0)
    return {"interface_rhs": interface_rhs, "order": order, "inverse_rr": inverse_rr, "corner_response": corner_response, "corners": corners, "coarse_factor": coarse_factor}


def faces_in(lagrange):
    back_faces = jnp.stack([jnp.roll(lagrange[..., 0, :], 1, axis=0), jnp.roll(lagrange[..., 1, :], 1, axis=1), jnp.roll(lagrange[..., 2, :], 1, axis=2)], axis=-2)
    return jnp.concatenate([-back_faces, lagrange], axis=-2)

def interface_operator(lagrange, order, unorder, inverse_rr, corner_response, corners, coarse_factor):
    nsx, nsy, nsz, samples, three_dirs, face_size = lagrange.shape
    subdomains = nsx * nsy * nsz
    local_size = 6 * face_size
    canonical = faces_in(lagrange).reshape(subdomains, samples, local_size)
    local_values = jnp.take_along_axis(canonical, order.reshape(subdomains, 1, local_size), axis=2).astype(jnp.bfloat16)
    matrices = inverse_rr.reshape(subdomains, local_size, local_size)
    responses = corner_response.reshape(subdomains, 8, local_size)

    def per_subdomain(operands):
        vector, matrix, reply = operands
        solved = jnp.dot(vector.astype(jnp.float32), matrix.astype(jnp.float32), preferred_element_type=jnp.float32)
        terms = jnp.dot(vector.astype(jnp.float32), reply.T.astype(jnp.float32), preferred_element_type=jnp.float32)
        return (solved, terms)
    local_solution, corner_terms = lax.map(per_subdomain, (local_values, matrices, responses))
    corner_ids = corners.reshape(subdomains * 8).astype(jnp.int32)
    flat_terms = corner_terms.transpose(0, 2, 1).reshape(subdomains * 8, samples)
    coarse_rhs = jnp.zeros((coarse_factor.shape[0], samples), jnp.float32).at[corner_ids].add(flat_terms)
    coarse = jax.scipy.linalg.cho_solve((coarse_factor, True), coarse_rhs)
    picked = coarse[corner_ids].reshape(subdomains, 8, samples)
    lifted = local_solution + jnp.einsum('skr,skl->srl', picked, responses.astype(jnp.float32), precision=lax.Precision.HIGHEST)
    placed = jnp.take_along_axis(lifted, unorder.reshape(subdomains, 1, local_size), axis=2)
    placed = placed.reshape(nsx, nsy, nsz, samples, 6, face_size)
    ahead_faces = jnp.stack([jnp.roll(placed[..., 0, :], -1, axis=0), jnp.roll(placed[..., 1, :], -1, axis=1), jnp.roll(placed[..., 2, :], -1, axis=2)], axis=-2)
    return placed[..., 3:, :] - ahead_faces

def reference(interface_rhs, order, inverse_rr, corner_response, corners, coarse_factor):
    unorder = jnp.argsort(order, axis=-1).astype(jnp.int32)
    sum_dims = (0, 1, 2, 4, 5)
    multipliers = jnp.zeros_like(interface_rhs)
    residual = interface_rhs
    direction = interface_rhs
    norm_now = jnp.sum(residual * residual, axis=sum_dims)
    for iteration in range(ITERS):
        image = interface_operator(direction, order, unorder, inverse_rr, corner_response, corners, coarse_factor)
        step_size = norm_now / jnp.sum(direction * image, axis=sum_dims)
        step_wide = step_size[:, None, None]
        multipliers = multipliers + step_wide * direction
        residual = residual - step_wide * image
        norm_next = jnp.sum(residual * residual, axis=sum_dims)
        direction = residual + (norm_next / norm_now)[:, None, None] * direction
        norm_now = norm_next
    return (multipliers, residual)
```

```python
import functools

import jax
import jax.numpy as jnp
from jax import lax
from jax.experimental import pallas as pl
from jax.experimental.pallas import tpu as pltpu
from jax.sharding import PartitionSpec as P

ITERS = 3
F32 = jnp.float32
LANES = 128
CORNERS = 8
SIDES = 6
BACK_X, AHEAD_X, BACK_Y, AHEAD_Y = range(4)


def lane_iota():
    return lax.broadcasted_iota(jnp.int32, (8, LANES), 1)


def pick_lanes(tiles, high, low):
    out = None
    for number, tile in enumerate(tiles):
        moved = jnp.take_along_axis(tile, low, axis=1, mode="promise_in_bounds")
        out = moved if out is None else jnp.where(high == number, moved, out)
    return out


def two_parts(value):
    upper = value.astype(jnp.bfloat16)
    lower = (value - upper.astype(F32)).astype(jnp.bfloat16)
    return jnp.concatenate([upper, lower], axis=0)


def lane_sum(tile):
    return jnp.sum(tile, axis=1, keepdims=True)


def order_tiles(order_ref, z):
    high, low = [], []
    for block in range(SIDES):
        row = order_ref[z : z + 1, block * LANES : (block + 1) * LANES]
        row = jnp.broadcast_to(row, (8, LANES))
        high.append(lax.shift_right_logical(row, 7))
        low.append(lax.bitwise_and(row, LANES - 1))
    return high, low


def prepare_kernel(nz, corners_ref, order_ref, response_ref, high_ref, low_ref, faces_ref, ids_ref):
    response = response_ref[...].astype(F32)
    lane = lane_iota()
    lane_square = lax.broadcasted_iota(jnp.int32, (LANES, LANES), 1)
    ids = jnp.zeros((8, LANES), jnp.int32)
    for z in range(nz):
        total = jnp.zeros((16, SIDES * LANES), F32)
        for block in range(SIDES):
            row = order_ref[z : z + 1, block * LANES : (block + 1) * LANES]
            column = jnp.broadcast_to(row, (LANES, LANES)).T
            hot = jnp.concatenate(
                [
                    jnp.where(column == lane_square + side * LANES, 1.0, 0.0).astype(jnp.bfloat16)
                    for side in range(SIDES)
                ],
                axis=1,
            )
            places = jnp.concatenate([lane.astype(F32), jnp.full((8, LANES), block, F32)], axis=0)
            total += jnp.dot(places.astype(jnp.bfloat16), hot, preferred_element_type=F32)
        own = [response[z][:, side * LANES : (side + 1) * LANES] for side in range(SIDES)]
        for side in range(SIDES):
            span = slice(side * LANES, (side + 1) * LANES)
            low = total[:8, span].astype(jnp.int32)
            high = total[8:, span].astype(jnp.int32)
            low_ref[z * SIDES + side] = low
            high_ref[z * SIDES + side] = high
            faces_ref[z * SIDES + side] = pick_lanes(own, high, low)
        for corner in range(CORNERS):
            ids = jnp.where(lane == z * CORNERS + corner, corners_ref[z, corner], ids)
    ids_ref[...] = ids


def factor_kernel(count, factor_ref, inverse_ref, square):
    size = square.shape[0]
    row = lax.broadcasted_iota(jnp.int32, (size, size), 0)
    column = lax.broadcasted_iota(jnp.int32, (size, size), 1)
    square[...] = jnp.where(row == column, 1.0, 0.0)
    square[0:count, 0:count] = factor_ref[...]
    factor = square[...]
    inverse = jnp.where(row == column, 1.0 / factor, 0.0)
    width = 1
    while width < count:
        below = (row // (2 * width) == column // (2 * width)) & (row // width > column // width)
        part = jnp.where(below, factor, 0.0)
        inner = jnp.dot(part, inverse, precision=lax.Precision.HIGHEST, preferred_element_type=F32)
        inverse = inverse - jnp.dot(
            inverse, inner, precision=lax.Precision.HIGHEST, preferred_element_type=F32
        )
        width *= 2
    both = lax.dot_general(
        inverse,
        inverse,
        (((0,), (0,)), ((), ())),
        precision=lax.Precision.HIGHEST,
        preferred_element_type=F32,
    )
    inverse_ref[...] = jnp.where((row < count) & (column < count), both, 0.0)


def send_side(nz, parity_ref, axis, faces, outs):
    even = parity_ref[axis] == 0
    first, second = outs
    for z in range(nz):
        up, down = faces[z * SIDES + 3 + axis], faces[z * SIDES + axis]
        first[z] = jnp.where(even, up, down)
        second[z] = jnp.where(even, down, up)


def local_part(nz, ncoarse, residual, image, refs):
    (order_ref, matrix_ref, response_ref, corners_ref, high_ref, low_ref, faces_ref, sums_ref) = refs
    own, back = residual
    lane = lane_iota()
    energy = jnp.zeros((8, LANES), F32)
    parts = []
    faces = [None] * (nz * SIDES)
    for z in range(nz):
        sides = [
            -back[z],
            -back[nz + z],
            -own[((z - 1) % nz) * 3 + 2],
            own[z * 3],
            own[z * 3 + 1],
            own[z * 3 + 2],
        ]
        high, low = order_tiles(order_ref, z)
        vector = jnp.concatenate([pick_lanes(sides, high[s], low[s]) for s in range(SIDES)], axis=1)
        parts.append(two_parts(vector))
        solved = jnp.dot(parts[z], matrix_ref[z], preferred_element_type=F32)
        solved = solved[:8] + solved[8:]
        tiles = [solved[:, s * LANES : (s + 1) * LANES] for s in range(SIDES)]
        for s in range(SIDES):
            energy += tiles[s] * vector[:, s * LANES : (s + 1) * LANES]
            face = pick_lanes(tiles, high_ref[z * SIDES + s], low_ref[z * SIDES + s])
            faces[z * SIDES + s] = face
            faces_ref[z * SIDES + s] = face
    response = response_ref[...]
    terms = []
    for z in range(nz):
        both = lax.dot_general(
            parts[z], response[z], (((1,), (1,)), ((), ())), preferred_element_type=F32
        )
        terms.append(both[:8] + both[8:])
    norm = jnp.zeros((8, LANES), F32)
    cross = jnp.zeros((8, LANES), F32)
    for at in range(nz * 3):
        norm += own[at] * own[at]
        if image is not None:
            cross += own[at] * image[at]
    numbers = (lane_sum(norm), lane_sum(cross), lane_sum(energy))
    for block in range(sums_ref.shape[0]):
        where = lane + block * LANES
        tile = jnp.zeros((8, LANES), F32)
        for z in range(nz):
            for corner in range(CORNERS):
                tile += jnp.where(where == corners_ref[z, corner], terms[z][:, corner : corner + 1], 0.0)
        for at, number in enumerate(numbers):
            tile += jnp.where(where == ncoarse + at, number, 0.0)
        sums_ref[block] = tile
    return faces


def start_kernel(
    nz, ncoarse, parity_ref, corners_ref, rhs_ref, back_x_ref, back_y_ref, order_ref, matrix_ref,
    response_ref, high_ref, low_ref, response_faces_ref, ids_ref,
    residual_ref, faces_ref, sums_ref, x_first, x_second, y_first, y_second,
):
    own = [rhs_ref[z][:, d, :] for z in range(nz) for d in range(3)]
    back = [back_x_ref[z][:, 0, :] for z in range(nz)] + [back_y_ref[z][:, 1, :] for z in range(nz)]
    for at, tile in enumerate(own + back):
        residual_ref[at] = tile
    refs = (order_ref, matrix_ref, response_ref, corners_ref, high_ref, low_ref, faces_ref, sums_ref)
    faces = local_part(nz, ncoarse, (own, back), None, refs)
    numbers = ids_ref[...].astype(F32)
    responses = [response_faces_ref[at] for at in range(nz * SIDES)]
    for axis, outs in ((0, (x_first, x_second)), (1, (y_first, y_second))):
        send_side(nz, parity_ref, axis, faces, outs)
        send_side(nz, parity_ref, axis, responses, [out.at[nz : 2 * nz] for out in outs])
        for out in outs:
            out[2 * nz] = numbers


def step_kernel(first, last, nz, ncoarse, *refs):
    refs = list(refs)

    def take(count):
        taken = refs[:count]
        del refs[:count]
        return taken

    parity_ref, corners_ref, sums_ref, inverse_ref = take(4)
    received = take(4)
    faces_ref, response_faces_ref, residual_ref = take(3)
    if first:
        (ids_ref,) = take(1)
    else:
        ids_ref, near_ref, image_ref, direction_ref, multipliers_ref, scalars_ref = take(6)
    if not last:
        order_ref, matrix_ref, response_ref, high_ref, low_ref = take(5)
        (out_residual, out_image, out_direction, out_multipliers, out_scalars, out_faces, out_sums) = take(7)
        sends = take(4)
        if first:
            out_ids, out_near = take(2)
    else:
        out_multipliers, out_residual = take(2)

    even_x, even_y = parity_ref[0] == 0, parity_ref[1] == 0
    lane = lane_iota()

    def ahead_and_back(at):
        x_first, x_second, y_first, y_second = [ref[at] for ref in received]
        return {
            AHEAD_X: jnp.where(even_x, x_first, x_second),
            BACK_X: jnp.where(even_x, x_second, x_first),
            AHEAD_Y: jnp.where(even_y, y_first, y_second),
            BACK_Y: jnp.where(even_y, y_second, y_first),
        }

    near_faces, near_responses = {}, {}
    for z in range(nz):
        for side, tile in ahead_and_back(z).items():
            near_faces[side, z] = tile
    if first:
        ids = ids_ref[...]
        for side, tile in ahead_and_back(2 * nz).items():
            shift = nz * CORNERS * (side + 1)
            moved = pltpu.roll(tile, shift, axis=1).astype(jnp.int32)
            ids = jnp.where((lane >= shift) & (lane < shift + nz * CORNERS), moved, ids)
        out_ids[...] = ids
        for z in range(nz):
            for side, tile in ahead_and_back(nz + z).items():
                near_responses[side, z] = tile
                out_near[side * nz + z] = tile
    else:
        ids = ids_ref[...]
        for z in range(nz):
            for side in range(4):
                near_responses[side, z] = near_ref[side * nz + z]

    sums = [sums_ref[block] for block in range(sums_ref.shape[0])]
    coarse = jnp.dot(
        jnp.concatenate(sums, axis=1),
        inverse_ref[...],
        precision=lax.Precision.HIGHEST,
        preferred_element_type=F32,
    )
    coarse = [coarse[:, b * LANES : (b + 1) * LANES] for b in range(coarse.shape[1] // LANES)]
    energy = sum(lane_sum(a * b) for a, b in zip(sums, coarse))

    def number(at):
        block, place = divmod(ncoarse + at, LANES)
        return sums[block][:, place : place + 1]

    norm, cross, energy = number(0), number(1), energy + number(2)
    if first:
        curvature = energy
    else:
        last_norm, last_curvature = scalars_ref[0][:, 0:1], scalars_ref[1][:, 0:1]
        ratio = norm / last_norm
        curvature = energy + 2.0 * ratio * cross + ratio * ratio * last_curvature
    step = norm / curvature

    picked = pick_lanes(coarse, lax.shift_right_logical(ids, 7), lax.bitwise_and(ids, LANES - 1))

    def lifted(tile, response, slot):
        for corner in range(CORNERS):
            at = slot * CORNERS + corner
            tile = tile + picked[:, at : at + 1] * response[corner : corner + 1, :]
        return tile

    def own_side(z, side):
        at = z * SIDES + side
        return lifted(faces_ref[at], response_faces_ref[at], z)

    def near_side(side, z):
        return lifted(near_faces[side, z], near_responses[side, z], nz * (side + 1) + z)

    fresh = [None] * (nz * 5)
    third_down = [own_side(z, 2) for z in range(nz)]
    for z in range(nz):
        fresh[z * 3] = own_side(z, 3) - near_side(AHEAD_X, z)
        fresh[z * 3 + 1] = own_side(z, 4) - near_side(AHEAD_Y, z)
        fresh[z * 3 + 2] = own_side(z, 5) - third_down[(z + 1) % nz]
        if not last:
            fresh[nz * 3 + z] = near_side(BACK_X, z) - own_side(z, 0)
            fresh[nz * 4 + z] = near_side(BACK_Y, z) - own_side(z, 1)

    count = nz * 3 if last else nz * 5
    residual, image = [], []
    for at in range(count):
        new_image = fresh[at] if first else fresh[at] + ratio * image_ref[at]
        old_residual = residual_ref[at]
        residual.append(old_residual - step * new_image)
        image.append(new_image)
        if at < nz * 3:
            direction = old_residual if first else old_residual + ratio * direction_ref[at]
            multipliers = step * direction if first else multipliers_ref[at] + step * direction
            if last:
                z, d = divmod(at, 3)
                out_multipliers[z, :, d, :] = multipliers
                out_residual[z, :, d, :] = residual[at]
            else:
                out_direction[at] = direction
                out_multipliers[at] = multipliers
    if last:
        return
    for at in range(count):
        out_residual[at] = residual[at]
        out_image[at] = image[at]
    out_scalars[0] = jnp.broadcast_to(norm, (8, LANES))
    out_scalars[1] = jnp.broadcast_to(curvature, (8, LANES))
    refs = (order_ref, matrix_ref, response_ref, corners_ref, high_ref, low_ref, out_faces, out_sums)
    faces = local_part(nz, ncoarse, (residual[: nz * 3], residual[nz * 3 :]), image, refs)
    send_side(nz, parity_ref, 0, faces, sends[:2])
    send_side(nz, parity_ref, 1, faces, sends[2:])


def tiles(count, kind=F32):
    return jax.ShapeDtypeStruct((count, 8, LANES), kind)


def call(kernel, outs, operands, scalars, flops, scratch=()):
    vmem = pl.BlockSpec(memory_space=pltpu.VMEM)
    smem = pl.BlockSpec(memory_space=pltpu.SMEM)
    return pl.pallas_call(
        kernel,
        out_shape=outs,
        in_specs=[smem] * scalars + [vmem] * (len(operands) - scalars),
        out_specs=[vmem] * len(outs),
        scratch_shapes=scratch,
        compiler_params=pltpu.CompilerParams(vmem_limit_bytes=48 * 2**20),
        cost_estimate=pl.CostEstimate(flops=flops, bytes_accessed=2**20, transcendentals=0),
    )(*operands)


def shifted(value, axis, steps):
    count = lax.axis_size(axis)
    return lax.ppermute(value, axis, [(i, (i + steps) % count) for i in range(count)])


def paired(value, axis, mask):
    return lax.ppermute(value, axis, [(i, i ^ mask) for i in range(lax.axis_size(axis))])


def paired_other(value, axis):
    count = lax.axis_size(axis)
    return lax.ppermute(value, axis, [(i, (i + 1 if i % 2 else i - 1) % count) for i in range(count)])


def exchange(sums, sends):
    lead = sums.shape[0]
    x_first, x_second, y_first, y_second = sends
    got_x_second = paired_other(x_second, "sub")
    got = paired(jnp.concatenate([sums, x_first]), "sub", 1)
    sums, got_x_first = sums + got[:lead], got[lead:]
    got = paired(jnp.concatenate([sums, y_first]), "slab", 1)
    sums, got_y_first = sums + got[:lead], got[lead:]
    mask = 2
    if lax.axis_size("slab") == 4:
        got = paired(jnp.concatenate([sums, y_second]), "slab", 3)
        sums, got_y_second = sums + got[:lead], got[lead:]
        mask = 4
    else:
        got_y_second = paired_other(y_second, "slab")
    while mask < lax.axis_size("slab"):
        sums = sums + paired(sums, "slab", mask)
        mask *= 2
    mask = 2
    while mask < lax.axis_size("sub"):
        sums = sums + paired(sums, "sub", mask)
        mask *= 2
    return sums, [got_x_first, got_x_second, got_y_first, got_y_second]


def coarse_inverse(coarse_factor, width):
    factor = lax.all_gather(coarse_factor, "slab", axis=0, tiled=True)
    count = factor.shape[0]
    if count <= LANES == width:
        return call(
            functools.partial(factor_kernel, count),
            [jax.ShapeDtypeStruct((LANES, LANES), F32)],
            [factor],
            0,
            2**26,
            [pltpu.VMEM((LANES, LANES), F32)],
        )[0]
    inverse = lax.linalg.triangular_solve(
        factor, jnp.eye(count, dtype=F32), left_side=True, lower=True
    )
    both = jnp.dot(inverse.T, inverse, precision=lax.Precision.HIGHEST)
    columns = -(-count // LANES) * LANES
    return jnp.pad(both, ((0, width - count), (0, columns - count)))


def local(interface_rhs, order, inverse_rr, corner_response, corners, coarse_factor):
    nz, samples, dirs, face = interface_rhs.shape[2:]
    ncoarse = coarse_factor.shape[1]
    local_size = SIDES * face
    blocks = -(-(ncoarse + 3) // LANES)
    rhs = interface_rhs.reshape(nz, samples, dirs, face)
    order = order.reshape(nz, local_size)
    matrices = inverse_rr.reshape(nz, local_size, local_size)
    responses = corner_response.reshape(nz, CORNERS, local_size)
    corners = corners.reshape(nz, CORNERS)
    parity = jnp.stack([lax.axis_index("sub") % 2, lax.axis_index("slab") % 2]).astype(jnp.int32)

    back_x = shifted(rhs, "sub", 1)
    back_y = shifted(rhs, "slab", 1)
    inverse = coarse_inverse(coarse_factor, blocks * LANES)
    tables = nz * SIDES
    high, low, response_faces, ids = call(
        functools.partial(prepare_kernel, nz),
        [tiles(tables, jnp.int32), tiles(tables, jnp.int32), tiles(tables),
         jax.ShapeDtypeStruct((8, LANES), jnp.int32)],
        [corners, order, responses],
        1,
        2**26,
    )
    own = [order, matrices, responses, high, low]
    residual, faces, sums, *sends = call(
        functools.partial(start_kernel, nz, ncoarse),
        [tiles(nz * 5), tiles(tables), tiles(blocks)] + [tiles(2 * nz + 1)] * 4,
        [parity, corners, rhs, back_x, back_y] + own + [response_faces, ids],
        2,
        2**28,
    )
    state = [residual, ids]
    for iteration in range(ITERS):
        first, last = iteration == 0, iteration == ITERS - 1
        sums, received = exchange(sums, sends)
        operands = [parity, corners, sums, inverse] + received + [faces, response_faces] + state
        kernel = functools.partial(step_kernel, first, last, nz, ncoarse)
        if last:
            shape = jax.ShapeDtypeStruct(rhs.shape, F32)
            multipliers, residual = call(kernel, [shape, shape], operands, 2, 2**24)
            break
        outs = [tiles(nz * 5), tiles(nz * 5), tiles(nz * 3), tiles(nz * 3), tiles(2)]
        outs += [tiles(tables), tiles(blocks)] + [tiles(nz)] * 4
        if first:
            outs += [jax.ShapeDtypeStruct((8, LANES), jnp.int32), tiles(nz * 4)]
        results = call(kernel, outs, operands + own, 2, 2**28)
        residual, image, direction, multipliers, scalars, faces, sums = results[:7]
        sends = results[7:11]
        if first:
            ids, near = results[11:]
        state = [residual, ids, near, image, direction, multipliers, scalars]
    return multipliers.reshape(interface_rhs.shape), residual.reshape(interface_rhs.shape)


def solution(mesh):
    in_specs = (
        P("sub", "slab", None, None, None, None),
        P("sub", "slab", None, None),
        P("sub", "slab", None, None, None),
        P("sub", "slab", None, None, None),
        P("sub", "slab", None, None),
        P("slab", None),
    )
    out_specs = (P("sub", "slab", None, None, None, None), P("sub", "slab", None, None, None, None))
    return jax.shard_map(local, mesh=mesh, in_specs=in_specs, out_specs=out_specs, check_vma=False)
```

```python
import functools

import jax
import jax.numpy as jnp
from jax import lax
from jax.experimental import pallas as pl
from jax.experimental.pallas import tpu as pltpu
from jax.sharding import PartitionSpec as P

ITERS = 3
F32 = jnp.float32
LANES = 128
CORNERS = 8
SIDES = 6
BACK_X, AHEAD_X, BACK_Y, AHEAD_Y = range(4)


def lane_iota():
    return lax.broadcasted_iota(jnp.int32, (8, LANES), 1)


def pick_lanes(tiles, high, low):
    out = None
    for number, tile in enumerate(tiles):
        moved = jnp.take_along_axis(tile, low, axis=1, mode="promise_in_bounds")
        out = moved if out is None else jnp.where(high == number, moved, out)
    return out


def two_parts(value):
    upper = value.astype(jnp.bfloat16)
    lower = (value - upper.astype(F32)).astype(jnp.bfloat16)
    return jnp.concatenate([upper, lower], axis=0)


def lane_sum(tile):
    return jnp.sum(tile, axis=1, keepdims=True)


def order_tiles(order_ref, z):
    high, low = [], []
    for block in range(SIDES):
        row = jnp.broadcast_to(order_ref[z, :, block * LANES : (block + 1) * LANES], (8, LANES))
        high.append(lax.shift_right_logical(row, 7))
        low.append(lax.bitwise_and(row, LANES - 1))
    return high, low


def prepare_kernel(
    nz, corners_ref, order_ref, response_ref, matrix_ref, factor_ref,
    high_ref, low_ref, faces_ref, ids_ref, rows_ref,
):
    if rows_ref is not None:
        rows_ref[...] = jnp.zeros_like(rows_ref)
        for at in range(rows_ref.shape[0]):
            rows_ref[at, :, 0 : factor_ref.shape[1]] = factor_ref[at * 8 : (at + 1) * 8, :]
    response = response_ref[...].astype(F32)
    lane = lane_iota()
    lane_square = lax.broadcasted_iota(jnp.int32, (LANES, LANES), 1)
    ids = jnp.zeros((8, LANES), jnp.int32)
    for z in range(nz):
        total = jnp.zeros((16, SIDES * LANES), F32)
        for block in range(SIDES):
            row = order_ref[z, :, block * LANES : (block + 1) * LANES]
            column = jnp.broadcast_to(row, (LANES, LANES)).T
            hot = jnp.concatenate(
                [
                    jnp.where(column == lane_square + side * LANES, 1.0, 0.0).astype(jnp.bfloat16)
                    for side in range(SIDES)
                ],
                axis=1,
            )
            places = jnp.concatenate([lane.astype(F32), jnp.full((8, LANES), block, F32)], axis=0)
            total += jnp.dot(places.astype(jnp.bfloat16), hot, preferred_element_type=F32)
        own = [response[z][:, side * LANES : (side + 1) * LANES] for side in range(SIDES)]
        for side in range(SIDES):
            span = slice(side * LANES, (side + 1) * LANES)
            low = total[:8, span].astype(jnp.int32)
            high = total[8:, span].astype(jnp.int32)
            low_ref[z * SIDES + side] = low
            high_ref[z * SIDES + side] = high
            faces_ref[z * SIDES + side] = pick_lanes(own, high, low)
        for corner in range(CORNERS):
            ids = jnp.where(lane == z * CORNERS + corner, corners_ref[z, 0, corner], ids)
    ids_ref[...] = ids


def factor_kernel(count, place_ref, *refs):
    *blocks, inverse_ref, square = refs
    size = square.shape[0]
    row = lax.broadcasted_iota(jnp.int32, (size, size), 0)
    column = lax.broadcasted_iota(jnp.int32, (size, size), 1)
    square[...] = jnp.where(row == column, 1.0, 0.0)
    for mask, block in zip((0, 1, 3, 2), blocks):
        tall = block.shape[0] * 8
        start = lax.bitwise_xor(place_ref[2], mask) * tall
        for at in range(block.shape[0]):
            square[pl.ds(pl.multiple_of(start + at * 8, 8), 8), :] = block[at]
    square[...] = jnp.where(row < count, square[...], jnp.where(row == column, 1.0, 0.0))
    factor = square[...]
    inverse = jnp.where(row == column, 1.0 / factor, 0.0)
    width = 1
    while width < count:
        below = (row // (2 * width) == column // (2 * width)) & (row // width > column // width)
        part = jnp.where(below, factor, 0.0)
        inner = jnp.dot(part, inverse, precision=lax.Precision.HIGHEST, preferred_element_type=F32)
        inverse = inverse - jnp.dot(
            inverse, inner, precision=lax.Precision.HIGHEST, preferred_element_type=F32
        )
        width *= 2
    both = lax.dot_general(
        inverse,
        inverse,
        (((0,), (0,)), ((), ())),
        precision=lax.Precision.HIGHEST,
        preferred_element_type=F32,
    )
    inverse_ref[...] = jnp.where((row < count) & (column < count), both, 0.0)


def send_side(nz, parity_ref, axis, faces, outs):
    even = parity_ref[axis] == 0
    first, second = outs
    for z in range(nz):
        up, down = faces[z * SIDES + 3 + axis], faces[z * SIDES + axis]
        first[z] = jnp.where(even, up, down)
        second[z] = jnp.where(even, down, up)


def local_part(nz, ncoarse, residual, image, refs):
    (order_ref, matrix_ref, response_ref, corners_ref, high_ref, low_ref, faces_ref, sums_ref) = refs
    own, back = residual
    lane = lane_iota()
    energy = jnp.zeros((8, LANES), F32)
    parts = []
    faces = [None] * (nz * SIDES)
    for z in range(nz):
        sides = [
            -back[z],
            -back[nz + z],
            -own[((z - 1) % nz) * 3 + 2],
            own[z * 3],
            own[z * 3 + 1],
            own[z * 3 + 2],
        ]
        high, low = order_tiles(order_ref, z)
        vector = jnp.concatenate([pick_lanes(sides, high[s], low[s]) for s in range(SIDES)], axis=1)
        parts.append(two_parts(vector))
        solved = jnp.dot(parts[z], matrix_ref[z], preferred_element_type=F32)
        solved = solved[:8] + solved[8:]
        tiles = [solved[:, s * LANES : (s + 1) * LANES] for s in range(SIDES)]
        for s in range(SIDES):
            energy += tiles[s] * vector[:, s * LANES : (s + 1) * LANES]
            face = pick_lanes(tiles, high_ref[z * SIDES + s], low_ref[z * SIDES + s])
            faces[z * SIDES + s] = face
            faces_ref[z * SIDES + s] = face
    response = response_ref[...]
    terms = []
    for z in range(nz):
        both = lax.dot_general(
            parts[z], response[z], (((1,), (1,)), ((), ())), preferred_element_type=F32
        )
        terms.append(both[:8] + both[8:])
    norm = jnp.zeros((8, LANES), F32)
    cross = jnp.zeros((8, LANES), F32)
    for at in range(nz * 3):
        norm += own[at] * own[at]
        if image is not None:
            cross += own[at] * image[at]
    numbers = (lane_sum(norm), lane_sum(cross), lane_sum(energy))
    for block in range(sums_ref.shape[0]):
        where = lane + block * LANES
        tile = jnp.zeros((8, LANES), F32)
        for z in range(nz):
            for corner in range(CORNERS):
                tile += jnp.where(where == corners_ref[z, 0, corner], terms[z][:, corner : corner + 1], 0.0)
        for at, number in enumerate(numbers):
            tile += jnp.where(where == ncoarse + at, number, 0.0)
        sums_ref[block] = tile
    return faces


def start_kernel(
    nz, ncoarse, parity_ref, corners_ref, rhs_ref, back_x_ref, back_y_ref, order_ref, matrix_ref,
    response_ref, high_ref, low_ref, response_faces_ref, ids_ref,
    residual_ref, faces_ref, sums_ref, x_first, x_second, y_first, y_second,
):
    own = [rhs_ref[at] for at in range(nz * 3)]
    back = [back_x_ref[z * 3] for z in range(nz)] + [back_y_ref[z * 3 + 1] for z in range(nz)]
    for at, tile in enumerate(own + back):
        residual_ref[at] = tile
    refs = (order_ref, matrix_ref, response_ref, corners_ref, high_ref, low_ref, faces_ref, sums_ref)
    faces = local_part(nz, ncoarse, (own, back), None, refs)
    numbers = ids_ref[...].astype(F32)
    responses = [response_faces_ref[at] for at in range(nz * SIDES)]
    for axis, outs in ((0, (x_first, x_second)), (1, (y_first, y_second))):
        send_side(nz, parity_ref, axis, faces, outs)
        send_side(nz, parity_ref, axis, responses, [out.at[nz : 2 * nz] for out in outs])
        for out in outs:
            out[2 * nz] = numbers


def step_kernel(first, last, nz, ncoarse, *refs):
    refs = list(refs)

    def take(count):
        taken = refs[:count]
        del refs[:count]
        return taken

    parity_ref, corners_ref, sums_ref, inverse_ref = take(4)
    received = take(4)
    faces_ref, response_faces_ref, residual_ref = take(3)
    if first:
        (ids_ref,) = take(1)
    else:
        ids_ref, near_ref, image_ref, direction_ref, multipliers_ref, scalars_ref = take(6)
    if not last:
        order_ref, matrix_ref, response_ref, high_ref, low_ref = take(5)
        (out_residual, out_image, out_direction, out_multipliers, out_scalars, out_faces, out_sums) = take(7)
        sends = take(4)
        if first:
            out_ids, out_near = take(2)
    else:
        out_multipliers, out_residual = take(2)

    even_x, even_y = parity_ref[0] == 0, parity_ref[1] == 0
    lane = lane_iota()

    def ahead_and_back(at):
        x_first, x_second, y_first, y_second = [ref[at] for ref in received]
        return {
            AHEAD_X: jnp.where(even_x, x_first, x_second),
            BACK_X: jnp.where(even_x, x_second, x_first),
            AHEAD_Y: jnp.where(even_y, y_first, y_second),
            BACK_Y: jnp.where(even_y, y_second, y_first),
        }

    near_faces, near_responses = {}, {}
    for z in range(nz):
        for side, tile in ahead_and_back(z).items():
            near_faces[side, z] = tile
    if first:
        ids = ids_ref[...]
        for side, tile in ahead_and_back(2 * nz).items():
            shift = nz * CORNERS * (side + 1)
            moved = pltpu.roll(tile, shift, axis=1).astype(jnp.int32)
            ids = jnp.where((lane >= shift) & (lane < shift + nz * CORNERS), moved, ids)
        out_ids[...] = ids
        for z in range(nz):
            for side, tile in ahead_and_back(nz + z).items():
                near_responses[side, z] = tile
                out_near[side * nz + z] = tile
    else:
        ids = ids_ref[...]
        for z in range(nz):
            for side in range(4):
                near_responses[side, z] = near_ref[side * nz + z]

    sums = [sums_ref[block] for block in range(sums_ref.shape[0])]
    coarse = jnp.dot(
        jnp.concatenate(sums, axis=1),
        inverse_ref[...],
        precision=lax.Precision.HIGHEST,
        preferred_element_type=F32,
    )
    coarse = [coarse[:, b * LANES : (b + 1) * LANES] for b in range(coarse.shape[1] // LANES)]
    energy = sum(lane_sum(a * b) for a, b in zip(sums, coarse))

    def number(at):
        block, place = divmod(ncoarse + at, LANES)
        return sums[block][:, place : place + 1]

    norm, cross, energy = number(0), number(1), energy + number(2)
    if first:
        curvature = energy
    else:
        last_norm, last_curvature = scalars_ref[0][:, 0:1], scalars_ref[1][:, 0:1]
        ratio = norm / last_norm
        curvature = energy + 2.0 * ratio * cross + ratio * ratio * last_curvature
    step = norm / curvature

    picked = pick_lanes(coarse, lax.shift_right_logical(ids, 7), lax.bitwise_and(ids, LANES - 1))

    def lifted(tile, response, slot):
        for corner in range(CORNERS):
            at = slot * CORNERS + corner
            tile = tile + picked[:, at : at + 1] * response[corner : corner + 1, :]
        return tile

    def own_side(z, side):
        at = z * SIDES + side
        return lifted(faces_ref[at], response_faces_ref[at], z)

    def near_side(side, z):
        return lifted(near_faces[side, z], near_responses[side, z], nz * (side + 1) + z)

    fresh = [None] * (nz * 5)
    third_down = [own_side(z, 2) for z in range(nz)]
    for z in range(nz):
        fresh[z * 3] = own_side(z, 3) - near_side(AHEAD_X, z)
        fresh[z * 3 + 1] = own_side(z, 4) - near_side(AHEAD_Y, z)
        fresh[z * 3 + 2] = own_side(z, 5) - third_down[(z + 1) % nz]
        if not last:
            fresh[nz * 3 + z] = near_side(BACK_X, z) - own_side(z, 0)
            fresh[nz * 4 + z] = near_side(BACK_Y, z) - own_side(z, 1)

    count = nz * 3 if last else nz * 5
    residual, image = [], []
    for at in range(count):
        new_image = fresh[at] if first else fresh[at] + ratio * image_ref[at]
        old_residual = residual_ref[at]
        residual.append(old_residual - step * new_image)
        image.append(new_image)
        if at < nz * 3:
            direction = old_residual if first else old_residual + ratio * direction_ref[at]
            multipliers = step * direction if first else multipliers_ref[at] + step * direction
            if last:
                out_multipliers[at] = multipliers
                out_residual[at] = residual[at]
            else:
                out_direction[at] = direction
                out_multipliers[at] = multipliers
    if last:
        return
    for at in range(count):
        out_residual[at] = residual[at]
        out_image[at] = image[at]
    out_scalars[0] = jnp.broadcast_to(norm, (8, LANES))
    out_scalars[1] = jnp.broadcast_to(curvature, (8, LANES))
    refs = (order_ref, matrix_ref, response_ref, corners_ref, high_ref, low_ref, out_faces, out_sums)
    faces = local_part(nz, ncoarse, (residual[: nz * 3], residual[nz * 3 :]), image, refs)
    send_side(nz, parity_ref, 0, faces, sends[:2])
    send_side(nz, parity_ref, 1, faces, sends[2:])


def tiles(count, kind=F32):
    return jax.ShapeDtypeStruct((count, 8, LANES), kind)


def call(kernel, outs, operands, scalars, flops, scratch=()):
    vmem = pl.BlockSpec(memory_space=pltpu.VMEM)
    smem = pl.BlockSpec(memory_space=pltpu.SMEM)
    return pl.pallas_call(
        kernel,
        out_shape=outs,
        in_specs=[smem] * scalars + [vmem] * (len(operands) - scalars),
        out_specs=[vmem] * len(outs),
        scratch_shapes=scratch,
        compiler_params=pltpu.CompilerParams(vmem_limit_bytes=48 * 2**20),
        cost_estimate=pl.CostEstimate(flops=flops, bytes_accessed=2**20, transcendentals=0),
    )(*operands)


def shifted(value, axis, steps):
    count = lax.axis_size(axis)
    return lax.ppermute(value, axis, [(i, (i + steps) % count) for i in range(count)])


def paired(value, axis, mask):
    return lax.ppermute(value, axis, [(i, i ^ mask) for i in range(lax.axis_size(axis))])


def paired_other(value, axis):
    count = lax.axis_size(axis)
    return lax.ppermute(value, axis, [(i, (i + 1 if i % 2 else i - 1) % count) for i in range(count)])


def exchange(sums, sends, rows=None):
    lead = sums.shape[0]
    x_first, x_second, y_first, y_second = sends
    near = x_first.shape[0]
    blocks = []
    if lax.axis_size("slab") == 4:
        extra = [] if rows is None else [rows]
        got = paired(jnp.concatenate([sums, y_first] + extra), "slab", 1)
        sums, got_y_first = sums + got[:lead], got[lead : lead + near]
        extra += [] if rows is None else [got[lead + near :]]
        got = paired(jnp.concatenate([sums, y_second] + extra), "slab", 3)
        sums, got_y_second = sums + got[:lead], got[lead : lead + near]
        if rows is not None:
            count = rows.shape[0]
            blocks = extra + [got[lead + near : lead + near + count], got[lead + near + count :]]
    else:
        got_y_first, got_y_second = paired(y_first, "slab", 1), paired_other(y_second, "slab")
        sums = doubled(sums, "slab", 1)
    got = paired(jnp.concatenate([sums, x_first]), "sub", 1)
    sums, got_x_first = sums + got[:lead], got[lead:]
    got = paired_other(jnp.concatenate([sums, x_second]), "sub")
    got_x_second = got[lead:]
    if lax.axis_size("sub") == 8:
        beside, opposite = got[:lead], paired(sums, "sub", 4)
        sums = sums + opposite + (beside + paired(beside, "sub", 1))
    else:
        sums = doubled(sums, "sub", 2)
    return sums, [got_x_first, got_x_second, got_y_first, got_y_second], blocks


def doubled(sums, axis, mask):
    while mask < lax.axis_size(axis):
        sums = sums + paired(sums, axis, mask)
        mask *= 2
    return sums


def coarse_inverse(coarse_factor, width):
    factor = lax.all_gather(coarse_factor, "slab", axis=0, tiled=True)
    count = factor.shape[0]
    inverse = lax.linalg.triangular_solve(
        factor, jnp.eye(count, dtype=F32), left_side=True, lower=True
    )
    both = jnp.dot(inverse.T, inverse, precision=lax.Precision.HIGHEST)
    columns = -(-count // LANES) * LANES
    return jnp.pad(both, ((0, width - count), (0, columns - count)))


def local(interface_rhs, order, inverse_rr, corner_response, corners, coarse_factor):
    nz, samples, dirs, face = interface_rhs.shape[2:]
    ncoarse = coarse_factor.shape[1]
    local_size = SIDES * face
    blocks = -(-(ncoarse + 3) // LANES)
    rhs = interface_rhs.transpose(0, 1, 2, 4, 3, 5).reshape(nz * dirs, samples, face)
    order = order.reshape(nz, 1, local_size)
    matrices = inverse_rr.reshape(nz, local_size, local_size)
    responses = corner_response.reshape(nz, CORNERS, local_size)
    corners = corners.reshape(nz, 1, CORNERS)
    place = lax.axis_index("slab")
    parity = jnp.stack([lax.axis_index("sub") % 2, place % 2, place]).astype(jnp.int32)

    back_x = shifted(rhs, "sub", 1)
    back_y = shifted(rhs, "slab", 1)
    riding = blocks == 1 and lax.axis_size("slab") == 4 and coarse_factor.shape[0] % 8 == 0
    tables = nz * SIDES
    rows = coarse_factor.shape[0] // 8 if riding else 1
    high, low, response_faces, ids, rows = call(
        functools.partial(prepare_kernel, nz),
        [tiles(tables, jnp.int32), tiles(tables, jnp.int32), tiles(tables),
         jax.ShapeDtypeStruct((8, LANES), jnp.int32), tiles(rows)],
        [corners, order, responses, matrices, coarse_factor[: rows * 8, :LANES]],
        1,
        2**30,
    )
    own = [order, matrices, responses, high, low]
    residual, faces, sums, *sends = call(
        functools.partial(start_kernel, nz, ncoarse),
        [tiles(nz * 5), tiles(tables), tiles(blocks)] + [tiles(2 * nz + 1)] * 4,
        [parity, corners, rhs, back_x, back_y] + own + [response_faces, ids],
        2,
        2**30,
    )
    state = [residual, ids]
    for iteration in range(ITERS):
        first, last = iteration == 0, iteration == ITERS - 1
        sums, received, factor = exchange(sums, sends, rows if first and riding else None)
        if first and riding:
            square = jax.ShapeDtypeStruct((LANES, LANES), F32)
            inverse = call(
                functools.partial(factor_kernel, ncoarse), [square], [parity] + factor, 1, 3 * 2**30,
                [pltpu.VMEM(square.shape, F32)],
            )[0]
        elif first:
            inverse = coarse_inverse(coarse_factor, blocks * LANES)
        operands = [parity, corners, sums, inverse] + received + [faces, response_faces] + state
        kernel = functools.partial(step_kernel, first, last, nz, ncoarse)
        if last:
            multipliers, residual = call(kernel, [tiles(nz * 3)] * 2, operands, 2, 2**30)
            break
        outs = [tiles(nz * 5), tiles(nz * 5), tiles(nz * 3), tiles(nz * 3), tiles(2)]
        outs += [tiles(tables), tiles(blocks)] + [tiles(nz)] * 4
        if first:
            outs += [jax.ShapeDtypeStruct((8, LANES), jnp.int32), tiles(nz * 4)]
        results = call(kernel, outs, operands + own, 2, 2**31)
        residual, image, direction, multipliers, scalars, faces, sums = results[:7]
        sends = results[7:11]
        if first:
            ids, near = results[11:]
        state = [residual, ids, near, image, direction, multipliers, scalars]

    def placed(value):
        value = value.reshape(interface_rhs.shape[:3] + (dirs, samples, face))
        return value.transpose(0, 1, 2, 4, 3, 5)

    return placed(multipliers), placed(residual)


def solution(mesh):
    in_specs = (
        P("sub", "slab", None, None, None, None),
        P("sub", "slab", None, None),
        P("sub", "slab", None, None, None),
        P("sub", "slab", None, None, None),
        P("sub", "slab", None, None),
        P("slab", None),
    )
    out_specs = (P("sub", "slab", None, None, None, None), P("sub", "slab", None, None, None, None))
    return jax.shard_map(local, mesh=mesh, in_specs=in_specs, out_specs=out_specs, check_vma=False)
```

```python
import functools

import jax
import jax.numpy as jnp
from jax import lax
from jax.experimental import pallas as pl
from jax.experimental.pallas import tpu as pltpu
from jax.sharding import PartitionSpec as P

ITERS = 3
F32 = jnp.float32
LANES = 128
CORNERS = 8
SIDES = 6
BACK_X, AHEAD_X, BACK_Y, AHEAD_Y = range(4)
PARITY, PLACE, CORNER = 0, 2, 3


def lane_iota():
    return lax.broadcasted_iota(jnp.int32, (8, LANES), 1)


def pick_lanes(tiles, high, low):
    out = None
    for number, tile in enumerate(tiles):
        moved = jnp.take_along_axis(tile, low, axis=1, mode="promise_in_bounds")
        out = moved if out is None else jnp.where(high == number, moved, out)
    return out


def two_parts(value):
    upper = value.astype(jnp.bfloat16)
    lower = (value - upper.astype(F32)).astype(jnp.bfloat16)
    return jnp.concatenate([upper, lower], axis=0)


def lane_sum(tile):
    return jnp.sum(tile, axis=1, keepdims=True)


def order_tiles(order_ref, z):
    high, low = [], []
    for block in range(SIDES):
        row = jnp.broadcast_to(order_ref[z, :, block * LANES : (block + 1) * LANES], (8, LANES))
        high.append(lax.shift_right_logical(row, 7))
        low.append(lax.bitwise_and(row, LANES - 1))
    return high, low


def prepare_kernel(
    nz, order_hbm, response_hbm, matrix_hbm, factor_hbm,
    order_ref, response_ref, matrix_ref, high_ref, low_ref, faces_ref, rows_ref,
    factor_ref, done,
):
    pairs = (
        (order_hbm, order_ref),
        (response_hbm, response_ref),
        (matrix_hbm, matrix_ref),
        (factor_hbm, factor_ref),
    )
    copies = [pltpu.make_async_copy(*pair, done.at[at]) for at, pair in enumerate(pairs)]
    for copy in copies:
        copy.start()
    for at in (0, 1, 3):
        copies[at].wait()
    rows_ref[...] = jnp.zeros_like(rows_ref)
    for at in range(rows_ref.shape[0]):
        rows_ref[at, :, 0 : factor_ref.shape[1]] = factor_ref[at * 8 : (at + 1) * 8, :]
    response = response_ref[...].astype(F32)
    lane = lane_iota()
    lane_square = lax.broadcasted_iota(jnp.int32, (LANES, LANES), 1)
    for z in range(nz):
        total = jnp.zeros((16, SIDES * LANES), F32)
        for block in range(SIDES):
            row = order_ref[z, :, block * LANES : (block + 1) * LANES]
            column = jnp.broadcast_to(row, (LANES, LANES)).T
            hot = jnp.concatenate(
                [
                    jnp.where(column == lane_square + side * LANES, 1.0, 0.0).astype(jnp.bfloat16)
                    for side in range(SIDES)
                ],
                axis=1,
            )
            places = jnp.concatenate([lane.astype(F32), jnp.full((8, LANES), block, F32)], axis=0)
            total += jnp.dot(places.astype(jnp.bfloat16), hot, preferred_element_type=F32)
        own = [response[z][:, side * LANES : (side + 1) * LANES] for side in range(SIDES)]
        for side in range(SIDES):
            span = slice(side * LANES, (side + 1) * LANES)
            low = total[:8, span].astype(jnp.int32)
            high = total[8:, span].astype(jnp.int32)
            low_ref[z * SIDES + side] = low
            high_ref[z * SIDES + side] = high
            faces_ref[z * SIDES + side] = pick_lanes(own, high, low)
    copies[2].wait()


def factor_kernel(count, place_ref, *refs):
    *blocks, inverse_ref, square = refs
    size = square.shape[0]
    row = lax.broadcasted_iota(jnp.int32, (size, size), 0)
    column = lax.broadcasted_iota(jnp.int32, (size, size), 1)
    square[...] = jnp.where(row == column, 1.0, 0.0)
    for mask, block in zip((0, 1, 3, 2), blocks):
        tall = block.shape[0] * 8
        start = lax.bitwise_xor(place_ref[PLACE], mask) * tall
        for at in range(block.shape[0]):
            square[pl.ds(pl.multiple_of(start + at * 8, 8), 8), :] = block[at]
    square[...] = jnp.where(row < count, square[...], jnp.where(row == column, 1.0, 0.0))
    factor = square[...]
    inverse = jnp.where(row == column, 1.0 / factor, 0.0)
    width = 1
    while width < count:
        below = (row // (2 * width) == column // (2 * width)) & (row // width > column // width)
        part = jnp.where(below, factor, 0.0)
        inner = jnp.dot(part, inverse, precision=lax.Precision.HIGHEST, preferred_element_type=F32)
        inverse = inverse - jnp.dot(
            inverse, inner, precision=lax.Precision.HIGHEST, preferred_element_type=F32
        )
        width *= 2
    both = lax.dot_general(
        inverse,
        inverse,
        (((0,), (0,)), ((), ())),
        precision=lax.Precision.HIGHEST,
        preferred_element_type=F32,
    )
    inverse_ref[...] = jnp.where((row < count) & (column < count), both, 0.0)


def send_side(nz, scalar_ref, axis, faces, outs):
    even = scalar_ref[PARITY + axis] == 0
    first, second = outs
    for z in range(nz):
        up, down = faces[z * SIDES + 3 + axis], faces[z * SIDES + axis]
        first[z] = jnp.where(even, up, down)
        second[z] = jnp.where(even, down, up)


def local_part(nz, ncoarse, residual, image, refs):
    (order_ref, matrix_ref, response_ref, scalar_ref, high_ref, low_ref, faces_ref, sums_ref) = refs
    own, back = residual
    lane = lane_iota()
    energy = jnp.zeros((8, LANES), F32)
    parts = []
    faces = [None] * (nz * SIDES)
    for z in range(nz):
        sides = [
            -back[z],
            -back[nz + z],
            -own[((z - 1) % nz) * 3 + 2],
            own[z * 3],
            own[z * 3 + 1],
            own[z * 3 + 2],
        ]
        high, low = order_tiles(order_ref, z)
        vector = jnp.concatenate([pick_lanes(sides, high[s], low[s]) for s in range(SIDES)], axis=1)
        parts.append(two_parts(vector))
        solved = jnp.dot(parts[z], matrix_ref[z], preferred_element_type=F32)
        solved = solved[:8] + solved[8:]
        tiles = [solved[:, s * LANES : (s + 1) * LANES] for s in range(SIDES)]
        for s in range(SIDES):
            energy += tiles[s] * vector[:, s * LANES : (s + 1) * LANES]
            face = pick_lanes(tiles, high_ref[z * SIDES + s], low_ref[z * SIDES + s])
            faces[z * SIDES + s] = face
            faces_ref[z * SIDES + s] = face
    response = response_ref[...]
    terms = []
    for z in range(nz):
        both = lax.dot_general(
            parts[z], response[z], (((1,), (1,)), ((), ())), preferred_element_type=F32
        )
        terms.append(both[:8] + both[8:])
    norm = jnp.zeros((8, LANES), F32)
    cross = jnp.zeros((8, LANES), F32)
    for at in range(nz * 3):
        norm += own[at] * own[at]
        if image is not None:
            cross += own[at] * image[at]
    numbers = (lane_sum(norm), lane_sum(cross), lane_sum(energy))
    blocks = -(-(ncoarse + 3) // LANES)
    for block in range(blocks):
        where = lane + block * LANES
        tile = jnp.zeros((8, LANES), F32)
        for z in range(nz):
            for corner in range(CORNERS):
                tile += jnp.where(where == scalar_ref[CORNER + z * CORNERS + corner], terms[z][:, corner : corner + 1], 0.0)
        for at, number in enumerate(numbers):
            tile += jnp.where(where == ncoarse + at, number, 0.0)
        for copy in range(0, sums_ref.shape[0], blocks):
            sums_ref[copy + block] = tile
    return faces


def start_kernel(
    nz, ncoarse, scalar_ref, rhs_ref, back_x_ref, back_y_ref, order_ref, matrix_ref,
    response_ref, high_ref, low_ref, response_faces_ref,
    residual_ref, ids_ref, faces_ref, sums_ref, x_first, x_second, y_first, y_second,
):
    own = [rhs_ref[at] for at in range(nz * 3)]
    back = [back_x_ref[z * 3] for z in range(nz)] + [back_y_ref[z * 3 + 1] for z in range(nz)]
    for at, tile in enumerate(own + back):
        residual_ref[at] = tile
    refs = (order_ref, matrix_ref, response_ref, scalar_ref, high_ref, low_ref, faces_ref, sums_ref)
    faces = local_part(nz, ncoarse, (own, back), None, refs)
    lane = lane_iota()
    ids = jnp.zeros((8, LANES), jnp.int32)
    for at in range(nz * CORNERS):
        ids = jnp.where(lane == at, scalar_ref[CORNER + at], ids)
    ids_ref[...] = ids
    numbers = ids.astype(F32)
    responses = [response_faces_ref[at] for at in range(nz * SIDES)]
    for axis, outs in ((0, (x_first, x_second)), (1, (y_first, y_second))):
        send_side(nz, scalar_ref, axis, faces, outs)
        send_side(nz, scalar_ref, axis, responses, [out.at[nz : 2 * nz] for out in outs])
        for out in outs:
            out[2 * nz] = numbers


def step_kernel(first, last, nz, ncoarse, *refs):
    refs = list(refs)

    def take(count):
        taken = refs[:count]
        del refs[:count]
        return taken

    scalar_ref, sums_ref, inverse_ref = take(3)
    received = take(2 if last else 4)
    faces_ref, response_faces_ref, residual_ref = take(3)
    if first:
        (ids_ref,) = take(1)
    else:
        ids_ref, near_ref, image_ref, direction_ref, multipliers_ref, scalars_ref = take(6)
    if not last:
        order_ref, matrix_ref, response_ref, high_ref, low_ref = take(5)
        (out_residual, out_image, out_direction, out_multipliers, out_scalars, out_faces, out_sums) = take(7)
        sends = take(len(refs) - (2 if first else 0))
        if first:
            out_ids, out_near = take(2)
    else:
        out_multipliers, out_residual = take(2)

    even_x, even_y = scalar_ref[PARITY] == 0, scalar_ref[PARITY + 1] == 0
    lane = lane_iota()

    def ahead_and_back(at):
        if last:
            return {AHEAD_X: received[0][at], AHEAD_Y: received[1][at]}
        x_first, x_second, y_first, y_second = [ref[at] for ref in received]
        return {
            AHEAD_X: jnp.where(even_x, x_first, x_second),
            BACK_X: jnp.where(even_x, x_second, x_first),
            AHEAD_Y: jnp.where(even_y, y_first, y_second),
            BACK_Y: jnp.where(even_y, y_second, y_first),
        }

    near_faces, near_responses = {}, {}
    for z in range(nz):
        for side, tile in ahead_and_back(z).items():
            near_faces[side, z] = tile
    if first:
        ids = ids_ref[...]
        for side, tile in ahead_and_back(2 * nz).items():
            shift = nz * CORNERS * (side + 1)
            moved = pltpu.roll(tile, shift, axis=1).astype(jnp.int32)
            ids = jnp.where((lane >= shift) & (lane < shift + nz * CORNERS), moved, ids)
        out_ids[...] = ids
        for z in range(nz):
            for side, tile in ahead_and_back(nz + z).items():
                near_responses[side, z] = tile
                out_near[side * nz + z] = tile
    else:
        ids = ids_ref[...]
        for z in range(nz):
            for side in (AHEAD_X, AHEAD_Y) if last else range(4):
                near_responses[side, z] = near_ref[side * nz + z]

    blocks = inverse_ref.shape[0] // LANES
    sums = [sums_ref[block] for block in range(blocks)]
    for copy in range(blocks, sums_ref.shape[0], blocks):
        sums = [total + sums_ref[copy + block] for block, total in enumerate(sums)]
    coarse = jnp.dot(
        jnp.concatenate(sums, axis=1),
        inverse_ref[...],
        precision=lax.Precision.HIGHEST,
        preferred_element_type=F32,
    )
    coarse = [coarse[:, b * LANES : (b + 1) * LANES] for b in range(coarse.shape[1] // LANES)]
    energy = sum(lane_sum(a * b) for a, b in zip(sums, coarse))

    def number(at):
        block, place = divmod(ncoarse + at, LANES)
        return sums[block][:, place : place + 1]

    norm, cross, energy = number(0), number(1), energy + number(2)
    if first:
        curvature = energy
    else:
        last_norm, last_curvature = scalars_ref[0][:, 0:1], scalars_ref[1][:, 0:1]
        ratio = norm / last_norm
        curvature = energy + 2.0 * ratio * cross + ratio * ratio * last_curvature
    step = norm / curvature

    picked = pick_lanes(coarse, lax.shift_right_logical(ids, 7), lax.bitwise_and(ids, LANES - 1))

    def lifted(tile, response, slot):
        for corner in range(CORNERS):
            at = slot * CORNERS + corner
            tile = tile + picked[:, at : at + 1] * response[corner : corner + 1, :]
        return tile

    def own_side(z, side):
        at = z * SIDES + side
        return lifted(faces_ref[at], response_faces_ref[at], z)

    def near_side(side, z):
        return lifted(near_faces[side, z], near_responses[side, z], nz * (side + 1) + z)

    fresh = [None] * (nz * 5)
    third_down = [own_side(z, 2) for z in range(nz)]
    for z in range(nz):
        fresh[z * 3] = own_side(z, 3) - near_side(AHEAD_X, z)
        fresh[z * 3 + 1] = own_side(z, 4) - near_side(AHEAD_Y, z)
        fresh[z * 3 + 2] = own_side(z, 5) - third_down[(z + 1) % nz]
        if not last:
            fresh[nz * 3 + z] = near_side(BACK_X, z) - own_side(z, 0)
            fresh[nz * 4 + z] = near_side(BACK_Y, z) - own_side(z, 1)

    count = nz * 3 if last else nz * 5
    residual, image = [], []
    for at in range(count):
        new_image = fresh[at] if first else fresh[at] + ratio * image_ref[at]
        old_residual = residual_ref[at]
        residual.append(old_residual - step * new_image)
        image.append(new_image)
        if at < nz * 3:
            direction = old_residual if first else old_residual + ratio * direction_ref[at]
            multipliers = step * direction if first else multipliers_ref[at] + step * direction
            if last:
                out_multipliers[at] = multipliers
                out_residual[at] = residual[at]
            else:
                out_direction[at] = direction
                out_multipliers[at] = multipliers
    if last:
        return
    for at in range(count):
        out_residual[at] = residual[at]
        out_image[at] = image[at]
    out_scalars[0] = jnp.broadcast_to(norm, (8, LANES))
    out_scalars[1] = jnp.broadcast_to(curvature, (8, LANES))
    refs = (order_ref, matrix_ref, response_ref, scalar_ref, high_ref, low_ref, out_faces, out_sums)
    faces = local_part(nz, ncoarse, (residual[: nz * 3], residual[nz * 3 :]), image, refs)
    if len(sends) == 2:
        for axis, out in enumerate(sends):
            for z in range(nz):
                out[z] = faces[z * SIDES + axis]
    else:
        send_side(nz, scalar_ref, 0, faces, sends[:2])
        send_side(nz, scalar_ref, 1, faces, sends[2:])


def tiles(count, kind=F32):
    return jax.ShapeDtypeStruct((count, 8, LANES), kind)


def like(value):
    return jax.ShapeDtypeStruct(value.shape, value.dtype)


def call(kernel, outs, operands, first_space, flops, scratch=()):
    vmem = pl.BlockSpec(memory_space=pltpu.VMEM)
    specs = [pl.BlockSpec(memory_space=first_space)] + [vmem] * (len(operands) - 1)
    if first_space == pltpu.HBM:
        specs = [pl.BlockSpec(memory_space=pltpu.HBM)] * len(operands)
        operands = [pltpu.with_memory_space_constraint(x, pltpu.HBM) for x in operands]
    return pl.pallas_call(
        kernel,
        out_shape=outs,
        in_specs=specs,
        out_specs=[vmem] * len(outs),
        scratch_shapes=scratch,
        compiler_params=pltpu.CompilerParams(vmem_limit_bytes=48 * 2**20),
        cost_estimate=pl.CostEstimate(flops=flops, bytes_accessed=2**20, transcendentals=0),
    )(*operands)


def shifted(value, axis, steps):
    count = lax.axis_size(axis)
    return lax.ppermute(value, axis, [(i, (i + steps) % count) for i in range(count)])


def paired(value, axis, mask):
    return lax.ppermute(value, axis, [(i, i ^ mask) for i in range(lax.axis_size(axis))])


def paired_other(value, axis):
    count = lax.axis_size(axis)
    return lax.ppermute(value, axis, [(i, (i + 1 if i % 2 else i - 1) % count) for i in range(count)])


def exchange_first(sums, sends, rows):
    lead = sums.shape[0]
    x_first, x_second, y_first, y_second = sends
    near = x_first.shape[0]
    blocks = []
    if lax.axis_size("slab") == 4:
        first = paired(jnp.concatenate([sums, y_first, rows]), "slab", 1)
        second = paired(jnp.concatenate([sums, y_second, rows]), "slab", 3)
        other = paired(jnp.concatenate([sums, rows]), "slab", 2)
        sums = sums + first[:lead] + (second[:lead] + other[:lead])
        blocks = [rows, first[lead + near :], second[lead + near :], other[lead:]]
        got_y_first, got_y_second = first[lead : lead + near], second[lead : lead + near]
    else:
        got_y_first, got_y_second = paired(y_first, "slab", 1), paired_other(y_second, "slab")
        sums = doubled(sums, "slab", 1)
    got = paired(jnp.concatenate([sums, x_first]), "sub", 1)
    sums, got_x_first = sums + got[:lead], got[lead:]
    got = paired_other(jnp.concatenate([sums, x_second]), "sub")
    got_x_second = got[lead:]
    if lax.axis_size("sub") == 8:
        beside, opposite = got[:lead], paired(sums, "sub", 4)
        sums = sums + opposite + (beside + paired(beside, "sub", 1))
    else:
        sums = doubled(sums, "sub", 2)
    return sums, [got_x_first, got_x_second, got_y_first, got_y_second], blocks


def exchange(sums, sends, spread):
    if spread:
        sums = lax.all_to_all(sums, ("sub", "slab"), 0, 0, tiled=True)
    else:
        sums = doubled(doubled(sums, "slab", 1), "sub", 1)
    if len(sends) == 2:
        return sums, [shifted(sends[0], "sub", -1), shifted(sends[1], "slab", -1)]
    x_first, x_second, y_first, y_second = sends
    return sums, [
        paired(x_first, "sub", 1),
        paired_other(x_second, "sub"),
        paired(y_first, "slab", 1),
        paired_other(y_second, "slab"),
    ]


def doubled(sums, axis, mask):
    while mask < lax.axis_size(axis):
        sums = sums + paired(sums, axis, mask)
        mask *= 2
    return sums


def coarse_inverse(coarse_factor, width):
    factor = lax.all_gather(coarse_factor, "slab", axis=0, tiled=True)
    count = factor.shape[0]
    inverse = lax.linalg.triangular_solve(
        factor, jnp.eye(count, dtype=F32), left_side=True, lower=True
    )
    both = jnp.dot(inverse.T, inverse, precision=lax.Precision.HIGHEST)
    columns = -(-count // LANES) * LANES
    return jnp.pad(both, ((0, width - count), (0, columns - count)))


def local(interface_rhs, order, inverse_rr, corner_response, corners, coarse_factor):
    nz, samples, dirs, face = interface_rhs.shape[2:]
    ncoarse = coarse_factor.shape[1]
    local_size = SIDES * face
    blocks = -(-(ncoarse + 3) // LANES)
    rhs = interface_rhs.transpose(0, 1, 2, 4, 3, 5).reshape(nz * dirs, samples, face)
    order = order.reshape(nz, 1, local_size)
    matrices = inverse_rr.reshape(nz, local_size, local_size)
    responses = corner_response.reshape(nz, CORNERS, local_size)
    place = lax.axis_index("slab")
    scalars = jnp.stack([lax.axis_index("sub") % 2, place % 2, place]).astype(jnp.int32)
    scalars = jnp.concatenate([scalars, corners.reshape(nz * CORNERS)])

    back_x = shifted(rhs, "sub", 1)
    back_y = shifted(rhs, "slab", 1)
    devices = lax.axis_size("sub") * lax.axis_size("slab")
    riding = blocks == 1 and lax.axis_size("slab") == 4 and coarse_factor.shape[0] % 8 == 0
    spread = blocks * devices <= 64
    copies = devices if spread else 1
    tables = nz * SIDES
    rows = coarse_factor.shape[0] // 8 if riding else 1
    part = coarse_factor[: rows * 8, :LANES]
    order, responses, matrices, high, low, response_faces, rows = call(
        functools.partial(prepare_kernel, nz),
        [like(order), like(responses), like(matrices), tiles(tables, jnp.int32),
         tiles(tables, jnp.int32), tiles(tables), tiles(rows)],
        [order, responses, matrices, part],
        pltpu.HBM,
        2**30,
        [pltpu.VMEM(part.shape, F32), pltpu.SemaphoreType.DMA((4,))],
    )
    own = [order, matrices, responses, high, low]
    residual, ids, faces, sums, *sends = call(
        functools.partial(start_kernel, nz, ncoarse),
        [tiles(nz * 5), jax.ShapeDtypeStruct((8, LANES), jnp.int32), tiles(tables), tiles(blocks)]
        + [tiles(2 * nz + 1)] * 4,
        [scalars, rhs, back_x, back_y] + own + [response_faces],
        pltpu.SMEM,
        2**30,
    )
    state = [residual, ids]
    for iteration in range(ITERS):
        first, last = iteration == 0, iteration == ITERS - 1
        if first:
            sums, received, factor = exchange_first(sums, sends, rows)
        else:
            sums, received = exchange(sums, sends, spread)
        if first and riding:
            square = jax.ShapeDtypeStruct((LANES, LANES), F32)
            inverse = call(
                functools.partial(factor_kernel, ncoarse), [square], [scalars] + factor,
                pltpu.SMEM, 3 * 2**30, [pltpu.VMEM(square.shape, F32)],
            )[0]
        elif first:
            inverse = coarse_inverse(coarse_factor, blocks * LANES)
        operands = [scalars, sums, inverse] + received + [faces, response_faces] + state
        kernel = functools.partial(step_kernel, first, last, nz, ncoarse)
        if last:
            outs = [tiles(nz * 3)] * 2
            multipliers, residual = call(kernel, outs, operands, pltpu.SMEM, 2**30)
            break
        outs = [tiles(nz * 5), tiles(nz * 5), tiles(nz * 3), tiles(nz * 3), tiles(2)]
        outs += [tiles(tables), tiles(blocks * copies)]
        sides = 2 if iteration == ITERS - 2 else 4
        outs += [tiles(nz)] * sides
        if first:
            outs += [jax.ShapeDtypeStruct((8, LANES), jnp.int32), tiles(nz * 4)]
        results = call(kernel, outs, operands + own, pltpu.SMEM, 2**31)
        residual, image, direction, multipliers, step, faces, sums = results[:7]
        sends = results[7 : 7 + sides]
        if first:
            ids, near = results[7 + sides :]
        state = [residual, ids, near, image, direction, multipliers, step]

    def placed(value):
        value = value.reshape(interface_rhs.shape[:3] + (dirs, samples, face))
        return value.transpose(0, 1, 2, 4, 3, 5)

    return placed(multipliers), placed(residual)


def solution(mesh):
    in_specs = (
        P("sub", "slab", None, None, None, None),
        P("sub", "slab", None, None),
        P("sub", "slab", None, None, None),
        P("sub", "slab", None, None, None),
        P("sub", "slab", None, None),
        P("slab", None),
    )
    out_specs = (P("sub", "slab", None, None, None, None), P("sub", "slab", None, None, None, None))
    return jax.shard_map(local, mesh=mesh, in_specs=in_specs, out_specs=out_specs, check_vma=False)
```

```python
import functools

import jax
import jax.numpy as jnp
from jax import lax
from jax.experimental import pallas as pl
from jax.experimental.pallas import tpu as pltpu
from jax.sharding import PartitionSpec as P

ITERS = 3
F32 = jnp.float32
LANES = 128
CORNERS = 8
WIDE = 256
SIDES = 6
BACK_X, AHEAD_X, BACK_Y, AHEAD_Y = range(4)
PARITY, PLACE = 0, 2


def upper_blocks(size):
    return [(i, j) for i in range(size // WIDE) for j in range(i, size // WIDE)]


def symmetric_dot(vector, matrix_ref, z):
    size = vector.shape[1]
    kept = upper_blocks(size)
    parts = [vector[:, at : at + WIDE] for at in range(0, size, WIDE)]
    outs = [None] * len(parts)
    for at, (i, j) in enumerate(kept):
        block = matrix_ref[z * len(kept) + at]
        terms = [(j, jnp.dot(parts[i], block, preferred_element_type=F32))]
        if i != j:
            turned = (((1,), (1,)), ((), ()))
            terms.append((i, lax.dot_general(parts[j], block, turned, preferred_element_type=F32)))
        for to, term in terms:
            outs[to] = term if outs[to] is None else outs[to] + term
    return jnp.concatenate(outs, axis=1)


def lane_iota():
    return lax.broadcasted_iota(jnp.int32, (8, LANES), 1)


def pick_lanes(tiles, high, low):
    out = None
    for number, tile in enumerate(tiles):
        moved = jnp.take_along_axis(tile, low, axis=1, mode="promise_in_bounds")
        out = moved if out is None else jnp.where(high == number, moved, out)
    return out


def two_parts(value):
    upper = value.astype(jnp.bfloat16)
    lower = (value - upper.astype(F32)).astype(jnp.bfloat16)
    return jnp.concatenate([upper, lower], axis=0)


def lane_sum(tile):
    return jnp.sum(tile, axis=1, keepdims=True)


def order_tiles(order_ref, z):
    high, low = [], []
    for block in range(SIDES):
        row = jnp.broadcast_to(order_ref[z, :, block * LANES : (block + 1) * LANES], (8, LANES))
        high.append(lax.shift_right_logical(row, 7))
        low.append(lax.bitwise_and(row, LANES - 1))
    return high, low


def prepare_kernel(
    nz, order_hbm, response_hbm, factor_hbm, corners_hbm, matrix_hbm,
    order_ref, slots_ref, vertex_ref, ids_ref, matrix_ref, place_ref, faces_ref, rows_ref,
    response_ref, factor_ref, corners_ref, done,
):
    pairs = [(order_hbm, order_ref), (response_hbm, response_ref), (factor_hbm, factor_ref)]
    pairs.append((corners_hbm, corners_ref))
    small = len(pairs)
    for z in range(nz):
        for i, j in upper_blocks(matrix_hbm.shape[1]):
            block = matrix_hbm.at[z, pl.ds(i * WIDE, WIDE), pl.ds(j * WIDE, WIDE)]
            pairs.append((block, matrix_ref.at[len(pairs) - small]))
    copies = [pltpu.make_async_copy(*pair, done.at[at]) for at, pair in enumerate(pairs)]
    for copy in copies:
        copy.start()
    for copy in copies[:small]:
        copy.wait()
    rows_ref[...] = jnp.zeros_like(rows_ref)
    for at in range(rows_ref.shape[0]):
        rows_ref[at, :, 0 : factor_ref.shape[1]] = factor_ref[at * 8 : (at + 1) * 8, :]
    response = response_ref[...].astype(F32)
    lane = lane_iota()
    lane_square = lax.broadcasted_iota(jnp.int32, (LANES, LANES), 1)
    ids_ref[...] = jnp.zeros_like(ids_ref)
    for z in range(nz):
        ids_ref[:, z * CORNERS : (z + 1) * CORNERS] = jnp.broadcast_to(corners_ref[z], (8, CORNERS))
    slots = slots_ref.shape[0]
    column = jnp.broadcast_to(ids_ref[0:1, :], (LANES, LANES)).T[:slots]
    for at in range(0, vertex_ref.shape[1], LANES):
        hot = jnp.where(column == lane_square[:slots] + at, 1.0, 0.0)
        vertex_ref[:, at : at + LANES] = hot.astype(jnp.bfloat16)
    pieces = [response[z] for z in range(nz)]
    if slots > nz * CORNERS:
        pieces.append(jnp.zeros((slots - nz * CORNERS, response.shape[2]), F32))
    slots_ref[...] = jnp.concatenate(pieces, axis=0).astype(jnp.bfloat16)
    for z in range(nz):
        total = jnp.zeros((16, SIDES * LANES), F32)
        for block in range(SIDES):
            row = order_ref[z, :, block * LANES : (block + 1) * LANES]
            column = jnp.broadcast_to(row, (LANES, LANES)).T
            hot = jnp.concatenate(
                [
                    jnp.where(column == lane_square + side * LANES, 1.0, 0.0).astype(jnp.bfloat16)
                    for side in range(SIDES)
                ],
                axis=1,
            )
            places = jnp.concatenate([lane.astype(F32), jnp.full((8, LANES), block, F32)], axis=0)
            total += jnp.dot(places.astype(jnp.bfloat16), hot, preferred_element_type=F32)
        own = [response[z][:, side * LANES : (side + 1) * LANES] for side in range(SIDES)]
        for side in range(SIDES):
            span = slice(side * LANES, (side + 1) * LANES)
            low = total[:8, span].astype(jnp.int32)
            high = total[8:, span].astype(jnp.int32)
            place_ref[z, :, span] = (high * LANES + low)[0:1]
            faces_ref[z * SIDES + side] = pick_lanes(own, high, low)
    for copy in copies[small:]:
        copy.wait()


def factor_kernel(count, mark_ref, *refs):
    *blocks, inverse_ref, square = refs
    size = square.shape[0]
    row = lax.broadcasted_iota(jnp.int32, (size, size), 0)
    column = lax.broadcasted_iota(jnp.int32, (size, size), 1)
    place = mark_ref[PLACE]
    tall = blocks[0].shape[0]
    for at in range(4 * tall):
        tile = blocks[0][at % tall]
        for mask, block in zip((1, 3, 2), blocks[1:]):
            tile = jnp.where(lax.bitwise_xor(place, mask) == at // tall, block[at % tall], tile)
        square[at * 8 : (at + 1) * 8, :] = tile
    square[4 * tall * 8 :, :] = jnp.zeros((size - 4 * tall * 8, LANES), F32)
    square[...] = jnp.where(row < count, square[...], jnp.where(row == column, 1.0, 0.0))
    factor = square[...]
    lane = lane_iota()
    sub = lax.broadcasted_iota(jnp.int32, (8, LANES), 0)
    corner = lax.bitwise_and(lane, LANES - 8)
    tile = jnp.zeros((8, LANES), F32)
    for at in range(0, size, 8):
        tile = jnp.where(corner == at, factor[at : at + 8, :], tile)
    solved = jnp.where(lane - corner == sub, 1.0, 0.0)
    for q in range(8):
        wide = jnp.take_along_axis(tile, corner + q, axis=1, mode="promise_in_bounds")
        row_q = solved[q : q + 1, :] / wide[q : q + 1, :]
        solved = jnp.where(sub > q, solved - wide * row_q, jnp.where(sub == q, row_q, solved))
    inverse = jnp.concatenate(
        [jnp.where(corner == at, solved, 0.0) for at in range(0, size, 8)], axis=0
    )
    width = 8
    while width < count:
        lower = [
            slice(at, at + width) for at in range(width, size, 2 * width)
        ]
        below = jnp.where(
            (row // (2 * width) == column // (2 * width)) & (row // width > column // width), factor, 0.0
        )
        part = jnp.concatenate([below[rows] for rows in lower], axis=0)
        inner = jnp.dot(part, inverse, precision=lax.Precision.HIGHEST, preferred_element_type=F32)
        left = jnp.concatenate([inverse[rows] for rows in lower], axis=0)
        none = jnp.zeros((width, size), F32)
        spread = []
        for at in range(len(lower)):
            spread += [none, inner[at * width : (at + 1) * width]]
        change = jnp.dot(
            left, jnp.concatenate(spread, axis=0),
            precision=lax.Precision.HIGHEST, preferred_element_type=F32,
        )
        pieces = []
        for at, rows in enumerate(lower):
            pieces += [
                inverse[rows.start - width : rows.start],
                inverse[rows] - change[at * width : (at + 1) * width],
            ]
        inverse = jnp.concatenate(pieces, axis=0)
        width *= 2
    both = lax.dot_general(
        inverse,
        inverse,
        (((0,), (0,)), ((), ())),
        precision=lax.Precision.HIGHEST,
        preferred_element_type=F32,
    )
    inverse_ref[...] = jnp.where((row < count) & (column < count), both, 0.0)


def send_side(nz, mark_ref, axis, faces, outs):
    even = mark_ref[PARITY + axis] == 0
    first, second = outs
    for z in range(nz):
        up, down = faces[z * SIDES + 3 + axis], faces[z * SIDES + axis]
        first[z] = jnp.where(even, up, down)
        second[z] = jnp.where(even, down, up)


def local_part(nz, ncoarse, residual, image, refs):
    (order_ref, matrix_ref, slots_ref, vertex_ref, place_ref, faces_ref) = refs[:6]
    sums_hbm, sums_ref, done = refs[6:]
    own, back = residual
    lane = lane_iota()
    norm = jnp.zeros((8, LANES), F32)
    cross = jnp.zeros((8, LANES), F32)
    for at in range(nz * 3):
        norm += own[at] * own[at]
        if image is not None:
            cross += own[at] * image[at]
    energy = jnp.zeros((8, LANES), F32)
    parts, results = [], []
    for z in range(nz):
        sides = [
            -back[z],
            -back[nz + z],
            -own[((z - 1) % nz) * 3 + 2],
            own[z * 3],
            own[z * 3 + 1],
            own[z * 3 + 2],
        ]
        high, low = order_tiles(order_ref, z)
        vector = jnp.concatenate([pick_lanes(sides, high[s], low[s]) for s in range(SIDES)], axis=1)
        parts.append(two_parts(vector))
        solved = symmetric_dot(parts[z], matrix_ref, z)
        solved = solved[:8] + solved[8:]
        results.append([solved[:, s * LANES : (s + 1) * LANES] for s in range(SIDES)])
        for s in range(SIDES):
            energy += results[z][s] * vector[:, s * LANES : (s + 1) * LANES]
    numbers = (lane_sum(norm), lane_sum(cross), lane_sum(energy))
    products = lax.dot_general(
        jnp.concatenate(parts, axis=0), slots_ref[...], (((1,), (1,)), ((), ())),
        preferred_element_type=F32,
    )
    slot = lax.broadcasted_iota(jnp.int32, (8, products.shape[1]), 1)
    terms = jnp.zeros(slot.shape, F32)
    for z in range(nz):
        both = products[z * 16 : z * 16 + 8] + products[z * 16 + 8 : z * 16 + 16]
        terms = jnp.where(lax.shift_right_logical(slot, 3) == z, both, terms)
    by_vertex = jnp.dot(two_parts(terms), vertex_ref[...], preferred_element_type=F32)
    by_vertex = by_vertex[:8] + by_vertex[8:]
    blocks = vertex_ref.shape[1] // LANES
    for block in range(blocks):
        where = lane + block * LANES
        tile = by_vertex[:, block * LANES : (block + 1) * LANES]
        for at, number in enumerate(numbers):
            tile += jnp.where(where == ncoarse + at, number, 0.0)
        for copy in range(0, sums_ref.shape[0], blocks):
            sums_ref[copy + block] = tile
    leaving = pltpu.make_async_copy(sums_ref, sums_hbm, done)
    leaving.start()
    faces = []
    for z in range(nz):
        high, low = order_tiles(place_ref, z)
        for s in range(SIDES):
            at = z * SIDES + s
            faces.append(pick_lanes(results[z], high[s], low[s]))
            faces_ref[at] = faces[at]
    return faces, leaving


def start_kernel(
    nz, ncoarse, mark_ref, rhs_ref, back_x_ref, back_y_ref, order_ref, matrix_ref,
    slots_ref, vertex_ref, place_ref, ids_ref, response_faces_ref,
    residual_ref, faces_ref, sums_hbm, x_first, x_second, y_first, y_second, sums_ref, done,
):
    own = [rhs_ref[at] for at in range(nz * 3)]
    back = [back_x_ref[z * 3] for z in range(nz)] + [back_y_ref[z * 3 + 1] for z in range(nz)]
    for at, tile in enumerate(own + back):
        residual_ref[at] = tile
    refs = (order_ref, matrix_ref, slots_ref, vertex_ref, place_ref, faces_ref)
    refs += (sums_hbm, sums_ref, done)
    faces, leaving = local_part(nz, ncoarse, (own, back), None, refs)
    numbers = ids_ref[...].astype(F32)
    responses = [response_faces_ref[at] for at in range(nz * SIDES)]
    for axis, outs in ((0, (x_first, x_second)), (1, (y_first, y_second))):
        send_side(nz, mark_ref, axis, faces, outs)
        send_side(nz, mark_ref, axis, responses, [out.at[nz : 2 * nz] for out in outs])
        for out in outs:
            out[2 * nz] = numbers
    leaving.wait()


def step_kernel(first, last, nz, ncoarse, *refs):
    refs = list(refs)

    def take(count):
        taken = refs[:count]
        del refs[:count]
        return taken

    mark_ref, sums_ref, inverse_ref = take(3)
    received = take(2 if last else 4)[::-1]
    faces_ref, response_faces_ref, residual_ref = take(3)
    if first:
        (ids_ref,) = take(1)
    else:
        ids_ref, near_ref, image_ref, direction_ref, multipliers_ref, scalars_ref = take(6)
    if not last:
        order_ref, matrix_ref, slots_ref, vertex_ref, place_ref = take(5)
        (out_residual, out_image, out_direction, out_multipliers, out_scalars, out_faces, out_sums) = take(7)
        sends = take(len(refs) - (4 if first else 2))
        if first:
            out_ids, out_near = take(2)
        sums_scratch, done = take(2)
    else:
        out_multipliers, out_residual = take(2)

    even_x, even_y = mark_ref[PARITY] == 0, mark_ref[PARITY + 1] == 0
    lane = lane_iota()

    def ahead_and_back(at):
        if last:
            return {AHEAD_X: received[0][at], AHEAD_Y: received[1][at]}
        x_first, x_second, y_first, y_second = [ref[at] for ref in received]
        return {
            AHEAD_X: jnp.where(even_x, x_first, x_second),
            BACK_X: jnp.where(even_x, x_second, x_first),
            AHEAD_Y: jnp.where(even_y, y_first, y_second),
            BACK_Y: jnp.where(even_y, y_second, y_first),
        }

    near_faces, near_responses = {}, {}
    for z in range(nz):
        for side, tile in ahead_and_back(z).items():
            near_faces[side, z] = tile
    if first:
        ids = ids_ref[...]
        for side, tile in ahead_and_back(2 * nz).items():
            shift = nz * CORNERS * (side + 1)
            moved = pltpu.roll(tile, shift, axis=1).astype(jnp.int32)
            ids = jnp.where((lane >= shift) & (lane < shift + nz * CORNERS), moved, ids)
        out_ids[...] = ids
        for z in range(nz):
            for side, tile in ahead_and_back(nz + z).items():
                near_responses[side, z] = tile
                out_near[side * nz + z] = tile
    else:
        ids = ids_ref[...]
        for z in range(nz):
            for side in (AHEAD_X, AHEAD_Y) if last else range(4):
                near_responses[side, z] = near_ref[side * nz + z]

    blocks = inverse_ref.shape[0] // LANES
    sums = [sums_ref[block] for block in range(blocks)]
    for copy in range(blocks, sums_ref.shape[0], blocks):
        sums = [total + sums_ref[copy + block] for block, total in enumerate(sums)]
    coarse = jnp.dot(
        jnp.concatenate(sums, axis=1),
        inverse_ref[...],
        precision=lax.Precision.HIGHEST,
        preferred_element_type=F32,
    )
    coarse = [coarse[:, b * LANES : (b + 1) * LANES] for b in range(coarse.shape[1] // LANES)]
    energy = sum(lane_sum(a * b) for a, b in zip(sums, coarse))

    def number(at):
        block, place = divmod(ncoarse + at, LANES)
        return sums[block][:, place : place + 1]

    norm, cross, energy = number(0), number(1), energy + number(2)
    if first:
        curvature = energy
    else:
        last_norm, last_curvature = scalars_ref[0][:, 0:1], scalars_ref[1][:, 0:1]
        ratio = norm / last_norm
        curvature = energy + 2.0 * ratio * cross + ratio * ratio * last_curvature
    step = norm / curvature

    picked = pick_lanes(coarse, lax.shift_right_logical(ids, 7), lax.bitwise_and(ids, LANES - 1))

    wide = {}

    def lifted(tile, response, slot):
        for corner in range(CORNERS):
            at = slot * CORNERS + corner
            if at not in wide:
                wide[at] = jnp.broadcast_to(picked[:, at : at + 1], (8, LANES))
            tile = tile + wide[at] * response[corner : corner + 1, :]
        return tile

    def own_side(z, side):
        at = z * SIDES + side
        return lifted(faces_ref[at], response_faces_ref[at], z)

    def near_side(side, z):
        return lifted(near_faces[side, z], near_responses[side, z], nz * (side + 1) + z)

    fresh = [None] * (nz * 5)
    third_down = [own_side(z, 2) for z in range(nz)]
    for z in range(nz):
        fresh[z * 3] = own_side(z, 3) - near_side(AHEAD_X, z)
        fresh[z * 3 + 1] = own_side(z, 4) - near_side(AHEAD_Y, z)
        fresh[z * 3 + 2] = own_side(z, 5) - third_down[(z + 1) % nz]
        if not last:
            fresh[nz * 3 + z] = near_side(BACK_X, z) - own_side(z, 0)
            fresh[nz * 4 + z] = near_side(BACK_Y, z) - own_side(z, 1)

    count = nz * 3 if last else nz * 5
    residual, image = [], []
    for at in range(count):
        new_image = fresh[at] if first else fresh[at] + ratio * image_ref[at]
        old_residual = residual_ref[at]
        residual.append(old_residual - step * new_image)
        image.append(new_image)
        if at < nz * 3:
            direction = old_residual if first else old_residual + ratio * direction_ref[at]
            multipliers = step * direction if first else multipliers_ref[at] + step * direction
            if last:
                out_multipliers[at] = multipliers
                out_residual[at] = residual[at]
            else:
                out_direction[at] = direction
                out_multipliers[at] = multipliers
    if last:
        return
    for at in range(count):
        out_residual[at] = residual[at]
        out_image[at] = image[at]
    out_scalars[0] = jnp.broadcast_to(norm, (8, LANES))
    out_scalars[1] = jnp.broadcast_to(curvature, (8, LANES))
    refs = (order_ref, matrix_ref, slots_ref, vertex_ref, place_ref, out_faces)
    refs += (out_sums, sums_scratch, done)
    faces, leaving = local_part(nz, ncoarse, (residual[: nz * 3], residual[nz * 3 :]), image, refs)
    if len(sends) == 2:
        for axis, out in enumerate(sends):
            for z in range(nz):
                out[z] = faces[z * SIDES + axis]
    else:
        send_side(nz, mark_ref, 0, faces, sends[:2])
        send_side(nz, mark_ref, 1, faces, sends[2:])
    leaving.wait()


def tiles(count, kind=F32):
    return jax.ShapeDtypeStruct((count, 8, LANES), kind)


def like(value):
    return jax.ShapeDtypeStruct(value.shape, value.dtype)


def call(kernel, outs, operands, first_space, flops, scratch=(), hbm=(), hbm_out=None):
    limit = 16 * 2**20 if max(x.size for x in operands) < 2**21 else 48 * 2**20
    vmem = pl.BlockSpec(memory_space=pltpu.VMEM)
    specs = [pl.BlockSpec(memory_space=first_space)] + [vmem] * (len(operands) - 1)
    operands = list(operands)
    for at in hbm:
        specs[at] = pl.BlockSpec(memory_space=pltpu.HBM)
        operands[at] = pltpu.with_memory_space_constraint(operands[at], pltpu.HBM)
    return pl.pallas_call(
        kernel,
        out_shape=outs,
        in_specs=specs,
        out_specs=[
            pl.BlockSpec(memory_space=pltpu.HBM) if at == hbm_out else vmem for at in range(len(outs))
        ],
        scratch_shapes=scratch,
        compiler_params=pltpu.CompilerParams(vmem_limit_bytes=limit),
        cost_estimate=pl.CostEstimate(flops=flops, bytes_accessed=2**20, transcendentals=0),
    )(*operands)


def shifted(value, axis, steps):
    count = lax.axis_size(axis)
    return lax.ppermute(value, axis, [(i, (i + steps) % count) for i in range(count)])


def paired(value, axis, mask):
    return lax.ppermute(value, axis, [(i, i ^ mask) for i in range(lax.axis_size(axis))])


def paired_other(value, axis):
    count = lax.axis_size(axis)
    return lax.ppermute(value, axis, [(i, (i + 1 if i % 2 else i - 1) % count) for i in range(count)])


def summed(sums, spread):
    if spread:
        return lax.all_to_all(sums, ("sub", "slab"), 0, 0, tiled=True)
    return doubled(doubled(sums, "slab", 1), "sub", 1)


def exchange(sums, sends, spread, rows=None):
    x_first, x_second, y_first, y_second = sends
    near = y_first.shape[0]
    blocks = []
    if rows is not None:
        y_first, y_second = jnp.concatenate([y_first, rows]), jnp.concatenate([y_second, rows])
    sums = summed(sums, spread)
    got_y_second, got_y_first = paired_other(y_second, "slab"), paired(y_first, "slab", 1)
    if rows is not None:
        blocks = [rows, got_y_first[near:], got_y_second[near:], paired(rows, "slab", 2)]
        got_y_first, got_y_second = got_y_first[:near], got_y_second[:near]
    got_x_second, got_x_first = paired_other(x_second, "sub"), paired(x_first, "sub", 1)
    return sums, [got_x_first, got_x_second, got_y_first, got_y_second], blocks


def exchange_last(sums, sends, spread):
    sums = summed(sums, spread)
    return sums, [shifted(sends[0], "sub", -1), shifted(sends[1], "slab", -1)]


def doubled(sums, axis, mask):
    while mask < lax.axis_size(axis):
        sums = sums + paired(sums, axis, mask)
        mask *= 2
    return sums


def coarse_inverse(coarse_factor, width):
    factor = lax.all_gather(coarse_factor, "slab", axis=0, tiled=True)
    count = factor.shape[0]
    inverse = lax.linalg.triangular_solve(
        factor, jnp.eye(count, dtype=F32), left_side=True, lower=True
    )
    both = jnp.dot(inverse.T, inverse, precision=lax.Precision.HIGHEST)
    columns = -(-count // LANES) * LANES
    return jnp.pad(both, ((0, width - count), (0, columns - count)))


def local(interface_rhs, order, inverse_rr, corner_response, corners, coarse_factor):
    nz, samples, dirs, face = interface_rhs.shape[2:]
    ncoarse = coarse_factor.shape[1]
    local_size = SIDES * face
    blocks = -(-(ncoarse + 3) // LANES)
    rhs = interface_rhs.transpose(0, 1, 2, 4, 3, 5).reshape(nz * dirs, samples, face)
    order = order.reshape(nz, 1, local_size)
    matrices = inverse_rr.reshape(nz, local_size, local_size)
    responses = corner_response.reshape(nz, CORNERS, local_size)
    place = lax.axis_index("slab")
    marks = jnp.stack([lax.axis_index("sub") % 2, place % 2, place]).astype(jnp.int32)
    marks = jnp.broadcast_to(marks[:, None, None], (3, 8, LANES))

    back_x = shifted(rhs, "sub", 1)
    back_y = shifted(rhs, "slab", 1)
    devices = lax.axis_size("sub") * lax.axis_size("slab")
    riding = blocks == 1 and lax.axis_size("slab") == 4 and coarse_factor.shape[0] % 8 == 0
    spread = blocks * devices <= 64
    copies = devices if spread else 1
    tables = nz * SIDES
    rows = coarse_factor.shape[0] // 8 if riding else 1
    part = coarse_factor[: rows * 8, :LANES]
    kept = nz * len(upper_blocks(local_size))
    kept = jax.ShapeDtypeStruct((kept, WIDE, WIDE), matrices.dtype)
    slots = -(-nz * CORNERS // 16) * 16
    order, slots, vertex, ids, matrices, unorder, response_faces, rows = call(
        functools.partial(prepare_kernel, nz),
        [like(order), jax.ShapeDtypeStruct((slots, local_size), jnp.bfloat16),
         jax.ShapeDtypeStruct((slots, blocks * LANES), jnp.bfloat16),
         jax.ShapeDtypeStruct((8, LANES), jnp.int32), kept, like(order), tiles(tables), tiles(rows)],
        [order, responses, part, corners.reshape(nz, 1, CORNERS), matrices],
        pltpu.HBM,
        2**30,
        [pltpu.VMEM(responses.shape, responses.dtype), pltpu.VMEM(part.shape, F32),
         pltpu.VMEM((nz, 1, CORNERS), jnp.int32), pltpu.SemaphoreType.DMA((4 + kept.shape[0],))],
        range(5),
    )
    own = [order, matrices, slots, vertex, unorder]
    leaving = [pltpu.VMEM((blocks * copies, 8, LANES), F32), pltpu.SemaphoreType.DMA]
    residual, faces, sums, *sends = call(
        functools.partial(start_kernel, nz, ncoarse),
        [tiles(nz * 5), tiles(tables), tiles(blocks * copies)]
        + [tiles(2 * nz + 1)] * 4,
        [marks, rhs, back_x, back_y] + own + [ids, response_faces],
        pltpu.VMEM,
        2**30,
        leaving,
        hbm_out=2,
    )
    state = [residual, ids]

    def invert(factor):
        if not riding:
            return coarse_inverse(coarse_factor, blocks * LANES)
        square = jax.ShapeDtypeStruct((LANES, LANES), F32)
        return call(
            functools.partial(factor_kernel, ncoarse), [square], [marks] + factor,
            pltpu.VMEM, 3 * 2**30, [pltpu.VMEM(square.shape, F32)],
        )[0]

    for iteration in range(ITERS):
        first, last = iteration == 0, iteration == ITERS - 1
        if last:
            sums, received = exchange_last(sums, sends, spread)
        else:
            ride = rows if first and riding else None
            sums, received, factor = exchange(sums, sends, spread, ride)
        if first:
            inverse = invert(factor)
        operands = [marks, sums, inverse] + received[::-1] + [faces, response_faces] + state
        kernel = functools.partial(step_kernel, first, last, nz, ncoarse)
        if last:
            outs = [tiles(nz * 3)] * 2
            multipliers, residual = call(kernel, outs, operands, pltpu.VMEM, 2**30)
            break
        outs = [tiles(nz * 5), tiles(nz * 5), tiles(nz * 3), tiles(nz * 3), tiles(2)]
        sides = 2 if iteration == ITERS - 2 else 4
        outs += [tiles(tables), tiles(blocks * copies)]
        outs += [tiles(nz)] * sides
        if first:
            outs += [jax.ShapeDtypeStruct((8, LANES), jnp.int32), tiles(nz * 4)]
        results = call(kernel, outs, operands + own, pltpu.VMEM, 2**31, leaving, hbm_out=6)
        residual, image, direction, multipliers, step, faces, sums = results[:7]
        sends = results[7 : 7 + sides]
        if first:
            ids, near = results[7 + sides :]
        state = [residual, ids, near, image, direction, multipliers, step]

    def placed(value):
        value = value.reshape(interface_rhs.shape[:3] + (dirs, samples, face))
        return value.transpose(0, 1, 2, 4, 3, 5)

    return placed(multipliers), placed(residual)


def solution(mesh):
    in_specs = (
        P("sub", "slab", None, None, None, None),
        P("sub", "slab", None, None),
        P("sub", "slab", None, None, None),
        P("sub", "slab", None, None, None),
        P("sub", "slab", None, None),
        P("slab", None),
    )
    out_specs = (P("sub", "slab", None, None, None, None), P("sub", "slab", None, None, None, None))
    return jax.shard_map(local, mesh=mesh, in_specs=in_specs, out_specs=out_specs, check_vma=False)
```

```python
import functools

import jax
import jax.numpy as jnp
from jax import lax
from jax.experimental import pallas as pl
from jax.experimental.pallas import tpu as pltpu
from jax.sharding import PartitionSpec as P

ITERS = 3
F32 = jnp.float32
LANES = 128
CORNERS = 8
WIDE = 256
SIDES = 6
BACK_X, AHEAD_X, BACK_Y, AHEAD_Y = range(4)
PARITY, PLACE = 0, 2


def upper_blocks(size):
    return [(i, j) for i in range(size // WIDE) for j in range(i, size // WIDE)]


def symmetric_dot(vector, matrix_ref, z):
    size = vector.shape[1]
    kept = upper_blocks(size)
    parts = [vector[:, at : at + WIDE] for at in range(0, size, WIDE)]
    outs = [None] * len(parts)
    for at, (i, j) in enumerate(kept):
        block = matrix_ref[z * len(kept) + at]
        terms = [(j, jnp.dot(parts[i], block, preferred_element_type=F32))]
        if i != j:
            turned = (((1,), (1,)), ((), ()))
            terms.append((i, lax.dot_general(parts[j], block, turned, preferred_element_type=F32)))
        for to, term in terms:
            outs[to] = term if outs[to] is None else outs[to] + term
    return jnp.concatenate(outs, axis=1)


def lane_iota():
    return lax.broadcasted_iota(jnp.int32, (8, LANES), 1)


def pick_lanes(tiles, high, low):
    out = None
    for number, tile in enumerate(tiles):
        moved = jnp.take_along_axis(tile, low, axis=1, mode="promise_in_bounds")
        out = moved if out is None else jnp.where(high == number, moved, out)
    return out


def two_parts(value):
    upper = value.astype(jnp.bfloat16)
    lower = (value - upper.astype(F32)).astype(jnp.bfloat16)
    return jnp.concatenate([upper, lower], axis=0)


def lane_sum(tile):
    return jnp.sum(tile, axis=1, keepdims=True)


def order_tiles(order_ref, z):
    high, low = [], []
    for block in range(SIDES):
        row = jnp.broadcast_to(order_ref[z, :, block * LANES : (block + 1) * LANES], (8, LANES))
        high.append(lax.shift_right_logical(row, 7))
        low.append(lax.bitwise_and(row, LANES - 1))
    return high, low


def prepare_kernel(
    nz, order_hbm, response_hbm, factor_hbm, corners_hbm, matrix_hbm,
    order_ref, slots_ref, vertex_ref, ids_ref, matrix_ref, place_ref, faces_ref, rows_ref,
    response_ref, factor_ref, corners_ref, done,
):
    pairs = [(order_hbm, order_ref), (response_hbm, response_ref), (factor_hbm, factor_ref)]
    pairs.append((corners_hbm, corners_ref))
    small = len(pairs)
    for z in range(nz):
        for i, j in upper_blocks(matrix_hbm.shape[1]):
            block = matrix_hbm.at[z, pl.ds(i * WIDE, WIDE), pl.ds(j * WIDE, WIDE)]
            pairs.append((block, matrix_ref.at[len(pairs) - small]))
    copies = [pltpu.make_async_copy(*pair, done.at[at]) for at, pair in enumerate(pairs)]
    for copy in copies:
        copy.start()
    for copy in copies[:small]:
        copy.wait()
    rows_ref[...] = jnp.zeros_like(rows_ref)
    for at in range(rows_ref.shape[0]):
        rows_ref[at, :, 0 : factor_ref.shape[1]] = factor_ref[at * 8 : (at + 1) * 8, :]
    response = response_ref[...].astype(F32)
    lane = lane_iota()
    lane_square = lax.broadcasted_iota(jnp.int32, (LANES, LANES), 1)
    ids_ref[...] = jnp.zeros_like(ids_ref)
    for z in range(nz):
        ids_ref[:, z * CORNERS : (z + 1) * CORNERS] = jnp.broadcast_to(corners_ref[z], (8, CORNERS))
    slots = slots_ref.shape[0]
    column = jnp.broadcast_to(ids_ref[0:1, :], (LANES, LANES)).T[:slots]
    for at in range(0, vertex_ref.shape[1], LANES):
        hot = jnp.where(column == lane_square[:slots] + at, 1.0, 0.0)
        vertex_ref[:, at : at + LANES] = hot.astype(jnp.bfloat16)
    pieces = [response[z] for z in range(nz)]
    if slots > nz * CORNERS:
        pieces.append(jnp.zeros((slots - nz * CORNERS, response.shape[2]), F32))
    slots_ref[...] = jnp.concatenate(pieces, axis=0).astype(jnp.bfloat16)
    for z in range(nz):
        total = jnp.zeros((16, SIDES * LANES), F32)
        for block in range(SIDES):
            row = order_ref[z, :, block * LANES : (block + 1) * LANES]
            column = jnp.broadcast_to(row, (LANES, LANES)).T
            hot = jnp.concatenate(
                [
                    jnp.where(column == lane_square + side * LANES, 1.0, 0.0).astype(jnp.bfloat16)
                    for side in range(SIDES)
                ],
                axis=1,
            )
            places = jnp.concatenate([lane.astype(F32), jnp.full((8, LANES), block, F32)], axis=0)
            total += jnp.dot(places.astype(jnp.bfloat16), hot, preferred_element_type=F32)
        own = [response[z][:, side * LANES : (side + 1) * LANES] for side in range(SIDES)]
        for side in range(SIDES):
            span = slice(side * LANES, (side + 1) * LANES)
            low = total[:8, span].astype(jnp.int32)
            high = total[8:, span].astype(jnp.int32)
            place_ref[z, :, span] = (high * LANES + low)[0:1]
            faces_ref[z * SIDES + side] = pick_lanes(own, high, low)
    for copy in copies[small:]:
        copy.wait()


def factor_kernel(count, mark_ref, *refs):
    *blocks, inverse_ref, square = refs
    size = square.shape[0]
    row = lax.broadcasted_iota(jnp.int32, (size, size), 0)
    column = lax.broadcasted_iota(jnp.int32, (size, size), 1)
    place = mark_ref[PLACE]
    tall = blocks[0].shape[0]
    for at in range(4 * tall):
        tile = blocks[0][at % tall]
        for mask, block in zip((1, 3, 2), blocks[1:]):
            tile = jnp.where(lax.bitwise_xor(place, mask) == at // tall, block[at % tall], tile)
        square[at * 8 : (at + 1) * 8, :] = tile
    square[4 * tall * 8 :, :] = jnp.zeros((size - 4 * tall * 8, LANES), F32)
    square[...] = jnp.where(row < count, square[...], jnp.where(row == column, 1.0, 0.0))
    factor = square[...]
    lane = lane_iota()
    sub = lax.broadcasted_iota(jnp.int32, (8, LANES), 0)
    corner = lax.bitwise_and(lane, LANES - 8)
    tile = jnp.zeros((8, LANES), F32)
    for at in range(0, size, 8):
        tile = jnp.where(corner == at, factor[at : at + 8, :], tile)
    solved = jnp.where(lane - corner == sub, 1.0, 0.0)
    for q in range(8):
        wide = jnp.take_along_axis(tile, corner + q, axis=1, mode="promise_in_bounds")
        row_q = solved[q : q + 1, :] / wide[q : q + 1, :]
        solved = jnp.where(sub > q, solved - wide * row_q, jnp.where(sub == q, row_q, solved))
    inverse = jnp.concatenate(
        [jnp.where(corner == at, solved, 0.0) for at in range(0, size, 8)], axis=0
    )
    width = 8
    while width < count:
        lower = [
            slice(at, at + width) for at in range(width, size, 2 * width)
        ]
        below = jnp.where(
            (row // (2 * width) == column // (2 * width)) & (row // width > column // width), factor, 0.0
        )
        part = jnp.concatenate([below[rows] for rows in lower], axis=0)
        inner = jnp.dot(part, inverse, precision=lax.Precision.HIGHEST, preferred_element_type=F32)
        left = jnp.concatenate([inverse[rows] for rows in lower], axis=0)
        none = jnp.zeros((width, size), F32)
        spread = []
        for at in range(len(lower)):
            spread += [none, inner[at * width : (at + 1) * width]]
        change = jnp.dot(
            left, jnp.concatenate(spread, axis=0),
            precision=lax.Precision.HIGHEST, preferred_element_type=F32,
        )
        pieces = []
        for at, rows in enumerate(lower):
            pieces += [
                inverse[rows.start - width : rows.start],
                inverse[rows] - change[at * width : (at + 1) * width],
            ]
        inverse = jnp.concatenate(pieces, axis=0)
        width *= 2
    both = lax.dot_general(
        inverse,
        inverse,
        (((0,), (0,)), ((), ())),
        precision=lax.Precision.HIGHEST,
        preferred_element_type=F32,
    )
    inverse_ref[...] = jnp.where((row < count) & (column < count), both, 0.0)


def send_side(nz, mark_ref, axis, faces, outs):
    even = mark_ref[PARITY + axis] == 0
    first, second = outs
    for z in range(nz):
        up, down = faces[z * SIDES + 3 + axis], faces[z * SIDES + axis]
        first[z] = jnp.where(even, up, down)
        second[z] = jnp.where(even, down, up)


def local_part(nz, ncoarse, residual, image, refs):
    (order_ref, matrix_ref, slots_ref, vertex_ref, place_ref, faces_ref, sums_ref) = refs
    own, back = residual
    lane = lane_iota()
    norm = jnp.zeros((8, LANES), F32)
    cross = jnp.zeros((8, LANES), F32)
    for at in range(nz * 3):
        norm += own[at] * own[at]
        if image is not None:
            cross += own[at] * image[at]
    energy = jnp.zeros((8, LANES), F32)
    parts, results = [], []
    for z in range(nz):
        sides = [
            -back[z],
            -back[nz + z],
            -own[((z - 1) % nz) * 3 + 2],
            own[z * 3],
            own[z * 3 + 1],
            own[z * 3 + 2],
        ]
        high, low = order_tiles(order_ref, z)
        vector = jnp.concatenate([pick_lanes(sides, high[s], low[s]) for s in range(SIDES)], axis=1)
        parts.append(two_parts(vector))
        solved = symmetric_dot(parts[z], matrix_ref, z)
        solved = solved[:8] + solved[8:]
        results.append([solved[:, s * LANES : (s + 1) * LANES] for s in range(SIDES)])
        for s in range(SIDES):
            energy += results[z][s] * vector[:, s * LANES : (s + 1) * LANES]
    numbers = (lane_sum(norm), lane_sum(cross), lane_sum(energy))
    products = lax.dot_general(
        jnp.concatenate(parts, axis=0), slots_ref[...], (((1,), (1,)), ((), ())),
        preferred_element_type=F32,
    )
    slot = lax.broadcasted_iota(jnp.int32, (8, products.shape[1]), 1)
    terms = jnp.zeros(slot.shape, F32)
    for z in range(nz):
        both = products[z * 16 : z * 16 + 8] + products[z * 16 + 8 : z * 16 + 16]
        terms = jnp.where(lax.shift_right_logical(slot, 3) == z, both, terms)
    by_vertex = jnp.dot(two_parts(terms), vertex_ref[...], preferred_element_type=F32)
    by_vertex = by_vertex[:8] + by_vertex[8:]
    blocks = vertex_ref.shape[1] // LANES
    for block in range(blocks):
        where = lane + block * LANES
        tile = by_vertex[:, block * LANES : (block + 1) * LANES]
        for at, number in enumerate(numbers):
            tile += jnp.where(where == ncoarse + at, number, 0.0)
        for copy in range(0, sums_ref.shape[0], blocks):
            sums_ref[copy + block] = tile
    faces = []
    for z in range(nz):
        high, low = order_tiles(place_ref, z)
        for s in range(SIDES):
            at = z * SIDES + s
            faces.append(pick_lanes(results[z], high[s], low[s]))
            faces_ref[at] = faces[at]
    return faces


def start_kernel(
    nz, ncoarse, mark_ref, rhs_ref, back_x_ref, back_y_ref, order_ref, matrix_ref,
    slots_ref, vertex_ref, place_ref, ids_ref, response_faces_ref,
    residual_ref, faces_ref, sums_ref, x_first, x_second, y_first, y_second,
):
    own = [rhs_ref[at] for at in range(nz * 3)]
    back = [back_x_ref[z * 3] for z in range(nz)] + [back_y_ref[z * 3 + 1] for z in range(nz)]
    for at, tile in enumerate(own + back):
        residual_ref[at] = tile
    refs = (order_ref, matrix_ref, slots_ref, vertex_ref, place_ref, faces_ref, sums_ref)
    faces = local_part(nz, ncoarse, (own, back), None, refs)
    numbers = ids_ref[...].astype(F32)
    responses = [response_faces_ref[at] for at in range(nz * SIDES)]
    for axis, outs in ((0, (x_first, x_second)), (1, (y_first, y_second))):
        send_side(nz, mark_ref, axis, faces, outs)
        send_side(nz, mark_ref, axis, responses, [out.at[nz : 2 * nz] for out in outs])
        for out in outs:
            out[2 * nz] = numbers


def step_kernel(first, last, nz, ncoarse, *refs):
    refs = list(refs)

    def take(count):
        taken = refs[:count]
        del refs[:count]
        return taken

    mark_ref, sums_ref, inverse_ref = take(3)
    received = take(2 if last else 4)[::-1]
    faces_ref, response_faces_ref, residual_ref = take(3)
    if first:
        (ids_ref,) = take(1)
    else:
        ids_ref, near_ref, image_ref, direction_ref, multipliers_ref, scalars_ref = take(6)
    if not last:
        order_ref, matrix_ref, slots_ref, vertex_ref, place_ref = take(5)
        (out_residual, out_image, out_direction, out_multipliers, out_scalars, out_faces, out_sums) = take(7)
        sends = take(len(refs) - (2 if first else 0))
        if first:
            out_ids, out_near = take(2)
    else:
        out_multipliers, out_residual = take(2)

    even_x, even_y = mark_ref[PARITY] == 0, mark_ref[PARITY + 1] == 0
    lane = lane_iota()

    def ahead_and_back(at):
        if last:
            return {AHEAD_X: received[0][at], AHEAD_Y: received[1][at]}
        x_first, x_second, y_first, y_second = [ref[at] for ref in received]
        return {
            AHEAD_X: jnp.where(even_x, x_first, x_second),
            BACK_X: jnp.where(even_x, x_second, x_first),
            AHEAD_Y: jnp.where(even_y, y_first, y_second),
            BACK_Y: jnp.where(even_y, y_second, y_first),
        }

    near_faces, near_responses = {}, {}
    for z in range(nz):
        for side, tile in ahead_and_back(z).items():
            near_faces[side, z] = tile
    if first:
        ids = ids_ref[...]
        for side, tile in ahead_and_back(2 * nz).items():
            shift = nz * CORNERS * (side + 1)
            moved = pltpu.roll(tile, shift, axis=1).astype(jnp.int32)
            ids = jnp.where((lane >= shift) & (lane < shift + nz * CORNERS), moved, ids)
        out_ids[...] = ids
        for z in range(nz):
            for side, tile in ahead_and_back(nz + z).items():
                near_responses[side, z] = tile
                out_near[side * nz + z] = tile
    else:
        ids = ids_ref[...]
        for z in range(nz):
            for side in (AHEAD_X, AHEAD_Y) if last else range(4):
                near_responses[side, z] = near_ref[side * nz + z]

    blocks = inverse_ref.shape[0] // LANES
    sums = [sums_ref[block] for block in range(blocks)]
    for copy in range(blocks, sums_ref.shape[0], blocks):
        sums = [total + sums_ref[copy + block] for block, total in enumerate(sums)]
    coarse = jnp.dot(
        jnp.concatenate(sums, axis=1),
        inverse_ref[...],
        precision=lax.Precision.HIGHEST,
        preferred_element_type=F32,
    )
    coarse = [coarse[:, b * LANES : (b + 1) * LANES] for b in range(coarse.shape[1] // LANES)]
    energy = sum(lane_sum(a * b) for a, b in zip(sums, coarse))

    def number(at):
        block, place = divmod(ncoarse + at, LANES)
        return sums[block][:, place : place + 1]

    norm, cross, energy = number(0), number(1), energy + number(2)
    if first:
        curvature = energy
    else:
        last_norm, last_curvature = scalars_ref[0][:, 0:1], scalars_ref[1][:, 0:1]
        ratio = norm / last_norm
        curvature = energy + 2.0 * ratio * cross + ratio * ratio * last_curvature
    step = norm / curvature

    picked = pick_lanes(coarse, lax.shift_right_logical(ids, 7), lax.bitwise_and(ids, LANES - 1))

    wide = {}

    def lifted(tile, response, slot):
        for corner in range(CORNERS):
            at = slot * CORNERS + corner
            if at not in wide:
                wide[at] = jnp.broadcast_to(picked[:, at : at + 1], (8, LANES))
            tile = tile + wide[at] * response[corner : corner + 1, :]
        return tile

    def own_side(z, side):
        at = z * SIDES + side
        return lifted(faces_ref[at], response_faces_ref[at], z)

    def near_side(side, z):
        return lifted(near_faces[side, z], near_responses[side, z], nz * (side + 1) + z)

    fresh = [None] * (nz * 5)
    third_down = [own_side(z, 2) for z in range(nz)]
    for z in range(nz):
        fresh[z * 3] = own_side(z, 3) - near_side(AHEAD_X, z)
        fresh[z * 3 + 1] = own_side(z, 4) - near_side(AHEAD_Y, z)
        fresh[z * 3 + 2] = own_side(z, 5) - third_down[(z + 1) % nz]
        if not last:
            fresh[nz * 3 + z] = near_side(BACK_X, z) - own_side(z, 0)
            fresh[nz * 4 + z] = near_side(BACK_Y, z) - own_side(z, 1)

    count = nz * 3 if last else nz * 5
    residual, image = [], []
    for at in range(count):
        new_image = fresh[at] if first else fresh[at] + ratio * image_ref[at]
        old_residual = residual_ref[at]
        residual.append(old_residual - step * new_image)
        image.append(new_image)
        if at < nz * 3:
            direction = old_residual if first else old_residual + ratio * direction_ref[at]
            multipliers = step * direction if first else multipliers_ref[at] + step * direction
            if last:
                out_multipliers[at] = multipliers
                out_residual[at] = residual[at]
            else:
                out_direction[at] = direction
                out_multipliers[at] = multipliers
    if last:
        return
    for at in range(count):
        out_residual[at] = residual[at]
        out_image[at] = image[at]
    out_scalars[0] = jnp.broadcast_to(norm, (8, LANES))
    out_scalars[1] = jnp.broadcast_to(curvature, (8, LANES))
    refs = (order_ref, matrix_ref, slots_ref, vertex_ref, place_ref, out_faces, out_sums)
    faces = local_part(nz, ncoarse, (residual[: nz * 3], residual[nz * 3 :]), image, refs)
    if len(sends) == 2:
        for axis, out in enumerate(sends):
            for z in range(nz):
                out[z] = faces[z * SIDES + axis]
    else:
        send_side(nz, mark_ref, 0, faces, sends[:2])
        send_side(nz, mark_ref, 1, faces, sends[2:])


def tiles(count, kind=F32):
    return jax.ShapeDtypeStruct((count, 8, LANES), kind)


def like(value):
    return jax.ShapeDtypeStruct(value.shape, value.dtype)


def call(kernel, outs, operands, first_space, flops, scratch=(), hbm=()):
    limit = 16 * 2**20 if max(x.size for x in operands) < 2**21 else 48 * 2**20
    vmem = pl.BlockSpec(memory_space=pltpu.VMEM)
    specs = [pl.BlockSpec(memory_space=first_space)] + [vmem] * (len(operands) - 1)
    operands = list(operands)
    for at in hbm:
        specs[at] = pl.BlockSpec(memory_space=pltpu.HBM)
        operands[at] = pltpu.with_memory_space_constraint(operands[at], pltpu.HBM)
    return pl.pallas_call(
        kernel,
        out_shape=outs,
        in_specs=specs,
        out_specs=[vmem] * len(outs),
        scratch_shapes=scratch,
        compiler_params=pltpu.CompilerParams(vmem_limit_bytes=limit),
        cost_estimate=pl.CostEstimate(flops=flops, bytes_accessed=2**20, transcendentals=0),
    )(*operands)


def shifted(value, axis, steps):
    count = lax.axis_size(axis)
    return lax.ppermute(value, axis, [(i, (i + steps) % count) for i in range(count)])


def paired(value, axis, mask):
    return lax.ppermute(value, axis, [(i, i ^ mask) for i in range(lax.axis_size(axis))])


def paired_other(value, axis):
    count = lax.axis_size(axis)
    return lax.ppermute(value, axis, [(i, (i + 1 if i % 2 else i - 1) % count) for i in range(count)])


def summed(sums, spread):
    if spread:
        return lax.all_to_all(sums, ("sub", "slab"), 0, 0, tiled=True)
    return doubled(doubled(sums, "slab", 1), "sub", 1)


def exchange(sums, sends, spread, rows=None):
    x_first, x_second, y_first, y_second = sends
    near = y_first.shape[0]
    blocks = []
    if rows is not None:
        y_first, y_second = jnp.concatenate([y_first, rows]), jnp.concatenate([y_second, rows])
    sums = summed(sums, spread)
    got_y_second, got_y_first = paired_other(y_second, "slab"), paired(y_first, "slab", 1)
    if rows is not None:
        blocks = [rows, got_y_first[near:], got_y_second[near:], paired(rows, "slab", 2)]
        got_y_first, got_y_second = got_y_first[:near], got_y_second[:near]
    got_x_second, got_x_first = paired_other(x_second, "sub"), paired(x_first, "sub", 1)
    return sums, [got_x_first, got_x_second, got_y_first, got_y_second], blocks


def exchange_last(sums, sends, spread):
    sums = summed(sums, spread)
    return sums, [shifted(sends[0], "sub", -1), shifted(sends[1], "slab", -1)]


def doubled(sums, axis, mask):
    while mask < lax.axis_size(axis):
        sums = sums + paired(sums, axis, mask)
        mask *= 2
    return sums


def coarse_inverse(coarse_factor, width):
    factor = lax.all_gather(coarse_factor, "slab", axis=0, tiled=True)
    count = factor.shape[0]
    inverse = lax.linalg.triangular_solve(
        factor, jnp.eye(count, dtype=F32), left_side=True, lower=True
    )
    both = jnp.dot(inverse.T, inverse, precision=lax.Precision.HIGHEST)
    columns = -(-count // LANES) * LANES
    return jnp.pad(both, ((0, width - count), (0, columns - count)))


def local(interface_rhs, order, inverse_rr, corner_response, corners, coarse_factor):
    nz, samples, dirs, face = interface_rhs.shape[2:]
    ncoarse = coarse_factor.shape[1]
    local_size = SIDES * face
    blocks = -(-(ncoarse + 3) // LANES)
    rhs = interface_rhs.transpose(0, 1, 2, 4, 3, 5).reshape(nz * dirs, samples, face)
    order = order.reshape(nz, 1, local_size)
    matrices = inverse_rr.reshape(nz, local_size, local_size)
    responses = corner_response.reshape(nz, CORNERS, local_size)
    place = lax.axis_index("slab")
    marks = jnp.stack([lax.axis_index("sub") % 2, place % 2, place]).astype(jnp.int32)
    marks = jnp.broadcast_to(marks[:, None, None], (3, 8, LANES))

    back_x = shifted(rhs, "sub", 1)
    back_y = shifted(rhs, "slab", 1)
    devices = lax.axis_size("sub") * lax.axis_size("slab")
    riding = blocks == 1 and lax.axis_size("slab") == 4 and coarse_factor.shape[0] % 8 == 0
    spread = blocks * devices <= 64
    copies = devices if spread else 1
    tables = nz * SIDES
    rows = coarse_factor.shape[0] // 8 if riding else 1
    part = coarse_factor[: rows * 8, :LANES]
    kept = nz * len(upper_blocks(local_size))
    kept = jax.ShapeDtypeStruct((kept, WIDE, WIDE), matrices.dtype)
    slots = -(-nz * CORNERS // 16) * 16
    order, slots, vertex, ids, matrices, unorder, response_faces, rows = call(
        functools.partial(prepare_kernel, nz),
        [like(order), jax.ShapeDtypeStruct((slots, local_size), jnp.bfloat16),
         jax.ShapeDtypeStruct((slots, blocks * LANES), jnp.bfloat16),
         jax.ShapeDtypeStruct((8, LANES), jnp.int32), kept, like(order), tiles(tables), tiles(rows)],
        [order, responses, part, corners.reshape(nz, 1, CORNERS), matrices],
        pltpu.HBM,
        2**30,
        [pltpu.VMEM(responses.shape, responses.dtype), pltpu.VMEM(part.shape, F32),
         pltpu.VMEM((nz, 1, CORNERS), jnp.int32), pltpu.SemaphoreType.DMA((4 + kept.shape[0],))],
        range(5),
    )
    own = [order, matrices, slots, vertex, unorder]
    residual, faces, sums, *sends = call(
        functools.partial(start_kernel, nz, ncoarse),
        [tiles(nz * 5), tiles(tables), tiles(blocks * copies)]
        + [tiles(2 * nz + 1)] * 4,
        [marks, rhs, back_x, back_y] + own + [ids, response_faces],
        pltpu.VMEM,
        2**30,
    )
    state = [residual, ids]

    def invert(factor):
        if not riding:
            return coarse_inverse(coarse_factor, blocks * LANES)
        square = jax.ShapeDtypeStruct((LANES, LANES), F32)
        return call(
            functools.partial(factor_kernel, ncoarse), [square], [marks] + factor,
            pltpu.VMEM, 2**29, [pltpu.VMEM(square.shape, F32)],
        )[0]

    for iteration in range(ITERS):
        first, last = iteration == 0, iteration == ITERS - 1
        if last:
            sums, received = exchange_last(sums, sends, spread)
        else:
            ride = rows if first and riding else None
            sums, received, factor = exchange(sums, sends, spread, ride)
        if first:
            inverse = invert(factor)
        operands = [marks, sums, inverse] + received[::-1] + [faces, response_faces] + state
        kernel = functools.partial(step_kernel, first, last, nz, ncoarse)
        if last:
            outs = [tiles(nz * 3)] * 2
            multipliers, residual = call(kernel, outs, operands, pltpu.VMEM, 2**30)
            break
        outs = [tiles(nz * 5), tiles(nz * 5), tiles(nz * 3), tiles(nz * 3), tiles(2)]
        sides = 2 if iteration == ITERS - 2 else 4
        outs += [tiles(tables), tiles(blocks * copies)]
        outs += [tiles(nz)] * sides
        if first:
            outs += [jax.ShapeDtypeStruct((8, LANES), jnp.int32), tiles(nz * 4)]
        results = call(kernel, outs, operands + own, pltpu.VMEM, 2**31)
        residual, image, direction, multipliers, step, faces, sums = results[:7]
        sends = results[7 : 7 + sides]
        if first:
            ids, near = results[7 + sides :]
        state = [residual, ids, near, image, direction, multipliers, step]

    def placed(value):
        value = value.reshape(interface_rhs.shape[:3] + (dirs, samples, face))
        return value.transpose(0, 1, 2, 4, 3, 5)

    return placed(multipliers), placed(residual)


def solution(mesh):
    in_specs = (
        P("sub", "slab", None, None, None, None),
        P("sub", "slab", None, None),
        P("sub", "slab", None, None, None),
        P("sub", "slab", None, None, None),
        P("sub", "slab", None, None),
        P("slab", None),
    )
    out_specs = (P("sub", "slab", None, None, None, None), P("sub", "slab", None, None, None, None))
    return jax.shard_map(local, mesh=mesh, in_specs=in_specs, out_specs=out_specs, check_vma=False)
```

```python
import functools

import jax
import jax.numpy as jnp
from jax import lax
from jax.experimental import pallas as pl
from jax.experimental.pallas import tpu as pltpu
from jax.sharding import PartitionSpec as P

ITERS = 3
F32 = jnp.float32
LANES = 128
CORNERS = 8
WIDE = 256
SIDES = 6
BACK_X, AHEAD_X, BACK_Y, AHEAD_Y = range(4)
PARITY, PLACE = 0, 2
PACK = 16
NUMBERS = 3


def upper_blocks(size):
    return [(i, j) for i in range(size // WIDE) for j in range(i, size // WIDE)]


def symmetric_dot(vector, matrix_ref, z):
    size = vector.shape[1]
    kept = upper_blocks(size)
    parts = [vector[:, at : at + WIDE] for at in range(0, size, WIDE)]
    outs = [None] * len(parts)
    for at, (i, j) in enumerate(kept):
        block = matrix_ref[z * len(kept) + at]
        terms = [(j, jnp.dot(parts[i], block, preferred_element_type=F32))]
        if i != j:
            turned = (((1,), (1,)), ((), ()))
            terms.append((i, lax.dot_general(parts[j], block, turned, preferred_element_type=F32)))
        for to, term in terms:
            outs[to] = term if outs[to] is None else outs[to] + term
    return jnp.concatenate(outs, axis=1)


def lane_iota():
    return lax.broadcasted_iota(jnp.int32, (8, LANES), 1)


def pick_lanes(tiles, high, low):
    out = None
    for number, tile in enumerate(tiles):
        moved = jnp.take_along_axis(tile, low, axis=1, mode="promise_in_bounds")
        out = moved if out is None else jnp.where(high == number, moved, out)
    return out


def bf16_parts(value, count):
    parts = []
    for _ in range(count):
        parts.append(value.astype(jnp.bfloat16))
        value = value - parts[-1].astype(F32)
    return jnp.concatenate(parts, axis=0)


def pack_sums(nz, terms, numbers):
    slot = lax.broadcasted_iota(jnp.int32, (terms.shape[1], LANES), 0)
    lane = lax.broadcasted_iota(jnp.int32, slot.shape, 1)
    level = lax.shift_right_logical(slot, 3) + lax.bitwise_and(slot, 1)
    level = jnp.where(level >= nz, level - nz, level)
    vertex = level * 4 + lax.bitwise_and(lax.shift_right_logical(slot, 1), 3)
    hot = (lax.bitwise_and(lane, PACK - 1) == vertex) & (slot < nz * CORNERS)
    wide = jnp.dot(
        two_parts(terms), jnp.where(hot, 1.0, 0.0).astype(jnp.bfloat16), preferred_element_type=F32
    )
    wide = wide[:8] + wide[8:]
    lane = lane_iota()
    for at, number in enumerate(numbers):
        wide = jnp.where(lax.bitwise_and(lane, PACK - 1) == nz * 4 + at, number, wide)
    sample = lax.broadcasted_iota(jnp.int32, (8, LANES), 0)
    return jnp.sum(jnp.where(lane // PACK == sample, wide, 0.0), axis=0, keepdims=True)


def unpack_sums(sums_ref, spread_ref):
    lane = lane_iota()
    place = lax.broadcasted_iota(jnp.int32, (8, LANES), 0) * PACK + lax.bitwise_and(lane, PACK - 1)
    group = LANES // PACK
    tiles = []
    for first in range(0, sums_ref.shape[0], group):
        tile = jnp.zeros((8, LANES), F32)
        for at in range(group):
            row = jnp.broadcast_to(sums_ref[first + at], (8, LANES))
            row = jnp.take_along_axis(row, place, axis=1, mode="promise_in_bounds")
            tile = jnp.where(lane // PACK == at, row, tile)
        tiles.append(tile)
    parts = bf16_parts(jnp.concatenate(tiles, axis=1), 3)
    total = jnp.dot(parts, spread_ref[...], preferred_element_type=F32)
    return total[:8] + (total[8:16] + total[16:])


def own_vertices(nz, ncoarse, ids):
    at = lane_iota() - ncoarse - NUMBERS
    inside = (at >= 0) & (at < PACK)
    at = jnp.where(inside, at, 0)
    slot = jnp.where(at < nz * 4, (at // 4) * CORNERS + lax.bitwise_and(at, 3) * 2, 0)
    vertex = jnp.take_along_axis(ids, slot, axis=1, mode="promise_in_bounds")
    vertex = jnp.where(at < nz * 4, vertex, ncoarse + at - nz * 4)
    vertex = jnp.where(at < nz * 4 + NUMBERS, vertex, -1)
    return jnp.where(inside, vertex.astype(F32), 0.0)


def spread_kernel(ncoarse, sums_ref, spread_ref):
    lane = lane_iota()
    lane_square = lax.broadcasted_iota(jnp.int32, (LANES, LANES), 1)
    place = ncoarse + NUMBERS + lax.bitwise_and(lane, PACK - 1)
    group = LANES // PACK
    for first in range(0, sums_ref.shape[0], group):
        line = jnp.zeros((8, LANES), F32)
        for at in range(group):
            row = jnp.take_along_axis(sums_ref[first + at], place, axis=1, mode="promise_in_bounds")
            line = jnp.where(lane // PACK == at, row, line)
        column = jnp.broadcast_to(line[0:1].astype(jnp.int32), (LANES, LANES)).T
        hot = jnp.where(column == lane_square, 1.0, 0.0).astype(jnp.bfloat16)
        spread_ref[first * PACK : (first + group) * PACK, :] = hot


def two_parts(value):
    upper = value.astype(jnp.bfloat16)
    lower = (value - upper.astype(F32)).astype(jnp.bfloat16)
    return jnp.concatenate([upper, lower], axis=0)


def lane_sum(tile):
    return jnp.sum(tile, axis=1, keepdims=True)


def order_tiles(order_ref, z):
    high, low = [], []
    for block in range(SIDES):
        row = jnp.broadcast_to(order_ref[z, :, block * LANES : (block + 1) * LANES], (8, LANES))
        high.append(lax.shift_right_logical(row, 7))
        low.append(lax.bitwise_and(row, LANES - 1))
    return high, low


def prepare_kernel(
    nz, order_hbm, response_hbm, factor_hbm, corners_hbm, matrix_hbm,
    order_ref, slots_ref, vertex_ref, ids_ref, matrix_ref, place_ref, faces_ref, rows_ref,
    response_ref, factor_ref, corners_ref, done,
):
    pairs = [(order_hbm, order_ref), (response_hbm, response_ref), (factor_hbm, factor_ref)]
    pairs.append((corners_hbm, corners_ref))
    small = len(pairs)
    for z in range(nz):
        for i, j in upper_blocks(matrix_hbm.shape[1]):
            block = matrix_hbm.at[z, pl.ds(i * WIDE, WIDE), pl.ds(j * WIDE, WIDE)]
            pairs.append((block, matrix_ref.at[len(pairs) - small]))
    copies = [pltpu.make_async_copy(*pair, done.at[at]) for at, pair in enumerate(pairs)]
    for copy in copies:
        copy.start()
    for copy in copies[:small]:
        copy.wait()
    rows_ref[...] = jnp.zeros_like(rows_ref)
    for at in range(rows_ref.shape[0]):
        rows_ref[at, :, 0 : factor_ref.shape[1]] = factor_ref[at * 8 : (at + 1) * 8, :]
    response = response_ref[...].astype(F32)
    lane = lane_iota()
    lane_square = lax.broadcasted_iota(jnp.int32, (LANES, LANES), 1)
    ids_ref[...] = jnp.zeros_like(ids_ref)
    for z in range(nz):
        ids_ref[:, z * CORNERS : (z + 1) * CORNERS] = jnp.broadcast_to(corners_ref[z], (8, CORNERS))
    slots = slots_ref.shape[0]
    column = jnp.broadcast_to(ids_ref[0:1, :], (LANES, LANES)).T[:slots]
    for at in range(0, vertex_ref.shape[1], LANES):
        hot = jnp.where(column == lane_square[:slots] + at, 1.0, 0.0)
        vertex_ref[:, at : at + LANES] = hot.astype(jnp.bfloat16)
    pieces = [response[z] for z in range(nz)]
    if slots > nz * CORNERS:
        pieces.append(jnp.zeros((slots - nz * CORNERS, response.shape[2]), F32))
    slots_ref[...] = jnp.concatenate(pieces, axis=0).astype(jnp.bfloat16)
    for z in range(nz):
        total = jnp.zeros((16, SIDES * LANES), F32)
        for block in range(SIDES):
            row = order_ref[z, :, block * LANES : (block + 1) * LANES]
            column = jnp.broadcast_to(row, (LANES, LANES)).T
            hot = jnp.concatenate(
                [
                    jnp.where(column == lane_square + side * LANES, 1.0, 0.0).astype(jnp.bfloat16)
                    for side in range(SIDES)
                ],
                axis=1,
            )
            places = jnp.concatenate([lane.astype(F32), jnp.full((8, LANES), block, F32)], axis=0)
            total += jnp.dot(places.astype(jnp.bfloat16), hot, preferred_element_type=F32)
        own = [response[z][:, side * LANES : (side + 1) * LANES] for side in range(SIDES)]
        for side in range(SIDES):
            span = slice(side * LANES, (side + 1) * LANES)
            low = total[:8, span].astype(jnp.int32)
            high = total[8:, span].astype(jnp.int32)
            place_ref[z, :, span] = (high * LANES + low)[0:1]
            faces_ref[z * SIDES + side] = pick_lanes(own, high, low)
    for copy in copies[small:]:
        copy.wait()


def apart(value, slices, size):
    pieces, at, used = [], 0, 0
    for rows in slices:
        pieces += [jnp.zeros((rows.start - at, size), F32), value[used : used + rows.stop - rows.start]]
        at, used = rows.stop, used + rows.stop - rows.start
    if at < size:
        pieces.append(jnp.zeros((size - at, size), F32))
    return jnp.concatenate(pieces, axis=0)


def factor_kernel(count, mark_ref, *refs):
    *blocks, inverse_ref, square = refs
    size = square.shape[0]
    row = lax.broadcasted_iota(jnp.int32, (size, size), 0)
    column = lax.broadcasted_iota(jnp.int32, (size, size), 1)
    place = mark_ref[PLACE]
    tall = blocks[0].shape[0]
    for at in range(4 * tall):
        tile = blocks[0][at % tall]
        for mask, block in zip((1, 3, 2), blocks[1:]):
            tile = jnp.where(lax.bitwise_xor(place, mask) == at // tall, block[at % tall], tile)
        square[at * 8 : (at + 1) * 8, :] = tile
    square[4 * tall * 8 :, :] = jnp.zeros((size - 4 * tall * 8, LANES), F32)
    square[...] = jnp.where(row < count, square[...], jnp.where(row == column, 1.0, 0.0))
    factor = square[...]
    least = 16
    lane = lax.broadcasted_iota(jnp.int32, (least, LANES), 1)
    sub = lax.broadcasted_iota(jnp.int32, (least, LANES), 0)
    corner = lax.bitwise_and(lane, LANES - least)
    tile = jnp.zeros((least, LANES), F32)
    for at in range(0, size, least):
        tile = jnp.where(corner == at, factor[at : at + least, :], tile)
    diagonal = jnp.take_along_axis(tile, corner + sub, axis=1, mode="promise_in_bounds")
    solved = jnp.where(lane - corner == sub, 1.0 / diagonal, 0.0)
    tile = tile / diagonal
    for q in range(least - 1):
        wide = jnp.take_along_axis(tile, corner + q, axis=1, mode="promise_in_bounds")
        solved = jnp.where(sub > q, solved - wide * solved[q : q + 1, :], solved)
    inverse = jnp.concatenate(
        [jnp.where(corner == at, solved, 0.0) for at in range(0, size, least)], axis=0
    )
    width = least
    while width < count:
        lower = [slice(at, min(at + width, -(-count // 8) * 8)) for at in range(width, count, 2 * width)]
        below = jnp.where(
            (row // (2 * width) == column // (2 * width)) & (row // width > column // width), factor, 0.0
        )
        part = jnp.concatenate([below[rows] for rows in lower], axis=0)
        left = jnp.concatenate([inverse[rows] for rows in lower], axis=0)
        inner = jnp.dot(part, inverse, precision=lax.Precision.HIGHEST, preferred_element_type=F32)
        change = jnp.dot(
            left, apart(inner, lower, size), precision=lax.Precision.HIGHEST, preferred_element_type=F32
        )
        inverse = inverse - apart(change, lower, size)
        width *= 2
    both = lax.dot_general(
        inverse,
        inverse,
        (((0,), (0,)), ((), ())),
        precision=lax.Precision.HIGHEST,
        preferred_element_type=F32,
    )
    inverse_ref[...] = jnp.where((row < count) & (column < count), both, 0.0)


def send_side(nz, mark_ref, axis, faces, outs):
    even = mark_ref[PARITY + axis] == 0
    first, second = outs
    for z in range(nz):
        up, down = faces[z * SIDES + 3 + axis], faces[z * SIDES + axis]
        first[z] = jnp.where(even, up, down)
        second[z] = jnp.where(even, down, up)


def local_part(nz, ncoarse, residual, image, refs, ids=None):
    (order_ref, matrix_ref, slots_ref, vertex_ref, place_ref, faces_ref, sums_ref) = refs
    own, back = residual
    lane = lane_iota()
    norm = jnp.zeros((8, LANES), F32)
    cross = jnp.zeros((8, LANES), F32)
    for at in range(nz * 3):
        norm += own[at] * own[at]
        if image is not None:
            cross += own[at] * image[at]
    energy = jnp.zeros((8, LANES), F32)
    parts, results = [], []
    for z in range(nz):
        sides = [
            -back[z],
            -back[nz + z],
            -own[((z - 1) % nz) * 3 + 2],
            own[z * 3],
            own[z * 3 + 1],
            own[z * 3 + 2],
        ]
        high, low = order_tiles(order_ref, z)
        vector = jnp.concatenate([pick_lanes(sides, high[s], low[s]) for s in range(SIDES)], axis=1)
        parts.append(two_parts(vector))
        solved = symmetric_dot(parts[z], matrix_ref, z)
        solved = solved[:8] + solved[8:]
        results.append([solved[:, s * LANES : (s + 1) * LANES] for s in range(SIDES)])
        for s in range(SIDES):
            energy += results[z][s] * vector[:, s * LANES : (s + 1) * LANES]
    numbers = (lane_sum(norm), lane_sum(cross), lane_sum(energy))
    products = lax.dot_general(
        jnp.concatenate(parts, axis=0), slots_ref[...], (((1,), (1,)), ((), ())),
        preferred_element_type=F32,
    )
    slot = lax.broadcasted_iota(jnp.int32, (8, products.shape[1]), 1)
    terms = jnp.zeros(slot.shape, F32)
    for z in range(nz):
        both = products[z * 16 : z * 16 + 8] + products[z * 16 + 8 : z * 16 + 16]
        terms = jnp.where(lax.shift_right_logical(slot, 3) == z, both, terms)
    if sums_ref.shape[1] == 1:
        row = pack_sums(nz, terms, numbers)
        for copy in range(sums_ref.shape[0]):
            sums_ref[copy] = row
    else:
        by_vertex = jnp.dot(two_parts(terms), vertex_ref[...], preferred_element_type=F32)
        by_vertex = by_vertex[:8] + by_vertex[8:]
        blocks = vertex_ref.shape[1] // LANES
        for block in range(blocks):
            where = lane + block * LANES
            tile = by_vertex[:, block * LANES : (block + 1) * LANES]
            for at, number in enumerate(numbers):
                tile += jnp.where(where == ncoarse + at, number, 0.0)
            if ids is not None:
                tile += own_vertices(nz, ncoarse, ids)
            for copy in range(0, sums_ref.shape[0], blocks):
                sums_ref[copy + block] = tile
    faces = []
    for z in range(nz):
        high, low = order_tiles(place_ref, z)
        for s in range(SIDES):
            at = z * SIDES + s
            faces.append(pick_lanes(results[z], high[s], low[s]))
            faces_ref[at] = faces[at]
    return faces


def start_kernel(
    packed, nz, ncoarse, mark_ref, rhs_ref, back_x_ref, back_y_ref, order_ref, matrix_ref,
    slots_ref, vertex_ref, place_ref, ids_ref, response_faces_ref,
    residual_ref, faces_ref, sums_ref, x_first, x_second, y_first, y_second,
):
    own = [rhs_ref[at] for at in range(nz * 3)]
    back = [back_x_ref[z * 3] for z in range(nz)] + [back_y_ref[z * 3 + 1] for z in range(nz)]
    for at, tile in enumerate(own + back):
        residual_ref[at] = tile
    refs = (order_ref, matrix_ref, slots_ref, vertex_ref, place_ref, faces_ref, sums_ref)
    faces = local_part(nz, ncoarse, (own, back), None, refs, ids_ref[...] if packed else None)
    numbers = ids_ref[...].astype(F32)
    responses = [response_faces_ref[at] for at in range(nz * SIDES)]
    for axis, outs in ((0, (x_first, x_second)), (1, (y_first, y_second))):
        send_side(nz, mark_ref, axis, faces, outs)
        send_side(nz, mark_ref, axis, responses, [out.at[nz : 2 * nz] for out in outs])
        for out in outs:
            out[2 * nz] = numbers


def step_kernel(first, last, nz, ncoarse, *refs):
    refs = list(refs)

    def take(count):
        taken = refs[:count]
        del refs[:count]
        return taken

    mark_ref, sums_ref, inverse_ref = take(3)
    packed = sums_ref.shape[1] == 1
    if packed:
        (spread_ref,) = take(1)
    received = take(2 if last else 4)[::-1]
    faces_ref, response_faces_ref, residual_ref = take(3)
    if first:
        (ids_ref,) = take(1)
    else:
        ids_ref, near_ref, image_ref, direction_ref, multipliers_ref, scalars_ref = take(6)
    if not last:
        order_ref, matrix_ref, slots_ref, vertex_ref, place_ref = take(5)
        (out_residual, out_image, out_direction, out_multipliers, out_scalars, out_faces, out_sums) = take(7)
        sends = take(len(refs) - (2 if first else 0))
        if first:
            out_ids, out_near = take(2)
    else:
        out_multipliers, out_residual = take(2)

    even_x, even_y = mark_ref[PARITY] == 0, mark_ref[PARITY + 1] == 0
    lane = lane_iota()

    def ahead_and_back(at):
        if last:
            return {AHEAD_X: received[0][at], AHEAD_Y: received[1][at]}
        x_first, x_second, y_first, y_second = [ref[at] for ref in received]
        return {
            AHEAD_X: jnp.where(even_x, x_first, x_second),
            BACK_X: jnp.where(even_x, x_second, x_first),
            AHEAD_Y: jnp.where(even_y, y_first, y_second),
            BACK_Y: jnp.where(even_y, y_second, y_first),
        }

    near_faces, near_responses = {}, {}
    for z in range(nz):
        for side, tile in ahead_and_back(z).items():
            near_faces[side, z] = tile
    if first:
        ids = ids_ref[...]
        for side, tile in ahead_and_back(2 * nz).items():
            shift = nz * CORNERS * (side + 1)
            moved = pltpu.roll(tile, shift, axis=1).astype(jnp.int32)
            ids = jnp.where((lane >= shift) & (lane < shift + nz * CORNERS), moved, ids)
        out_ids[...] = ids
        for z in range(nz):
            for side, tile in ahead_and_back(nz + z).items():
                near_responses[side, z] = tile
                out_near[side * nz + z] = tile
    else:
        ids = ids_ref[...]
        for z in range(nz):
            for side in (AHEAD_X, AHEAD_Y) if last else range(4):
                near_responses[side, z] = near_ref[side * nz + z]

    blocks = inverse_ref.shape[0] // LANES
    if packed:
        sums = [unpack_sums(sums_ref, spread_ref)]
    else:
        sums = [sums_ref[block] for block in range(blocks)]
        for copy in range(blocks, sums_ref.shape[0], blocks):
            sums = [total + sums_ref[copy + block] for block, total in enumerate(sums)]
    coarse = jnp.dot(
        jnp.concatenate(sums, axis=1),
        inverse_ref[...],
        precision=lax.Precision.HIGHEST,
        preferred_element_type=F32,
    )
    coarse = [coarse[:, b * LANES : (b + 1) * LANES] for b in range(coarse.shape[1] // LANES)]
    energy = sum(lane_sum(a * b) for a, b in zip(sums, coarse))

    def number(at):
        block, place = divmod(ncoarse + at, LANES)
        return sums[block][:, place : place + 1]

    norm, cross, energy = number(0), number(1), energy + number(2)
    if first:
        curvature = energy
    else:
        last_norm, last_curvature = scalars_ref[0][:, 0:1], scalars_ref[1][:, 0:1]
        ratio = norm / last_norm
        curvature = energy + 2.0 * ratio * cross + ratio * ratio * last_curvature
    step = norm / curvature

    picked = pick_lanes(coarse, lax.shift_right_logical(ids, 7), lax.bitwise_and(ids, LANES - 1))

    wide = {}

    def lifted(tile, response, slot):
        for corner in range(CORNERS):
            at = slot * CORNERS + corner
            if at not in wide:
                wide[at] = jnp.broadcast_to(picked[:, at : at + 1], (8, LANES))
            tile = tile + wide[at] * response[corner : corner + 1, :]
        return tile

    def own_side(z, side):
        at = z * SIDES + side
        return lifted(faces_ref[at], response_faces_ref[at], z)

    def near_side(side, z):
        return lifted(near_faces[side, z], near_responses[side, z], nz * (side + 1) + z)

    fresh = [None] * (nz * 5)
    third_down = [own_side(z, 2) for z in range(nz)]
    for z in range(nz):
        fresh[z * 3] = own_side(z, 3) - near_side(AHEAD_X, z)
        fresh[z * 3 + 1] = own_side(z, 4) - near_side(AHEAD_Y, z)
        fresh[z * 3 + 2] = own_side(z, 5) - third_down[(z + 1) % nz]
        if not last:
            fresh[nz * 3 + z] = near_side(BACK_X, z) - own_side(z, 0)
            fresh[nz * 4 + z] = near_side(BACK_Y, z) - own_side(z, 1)

    count = nz * 3 if last else nz * 5
    residual, image = [], []
    for at in range(count):
        new_image = fresh[at] if first else fresh[at] + ratio * image_ref[at]
        old_residual = residual_ref[at]
        residual.append(old_residual - step * new_image)
        image.append(new_image)
        if at < nz * 3:
            direction = old_residual if first else old_residual + ratio * direction_ref[at]
            multipliers = step * direction if first else multipliers_ref[at] + step * direction
            if last:
                out_multipliers[at] = multipliers
                out_residual[at] = residual[at]
            else:
                out_direction[at] = direction
                out_multipliers[at] = multipliers
    if last:
        return
    for at in range(count):
        out_residual[at] = residual[at]
        out_image[at] = image[at]
    out_scalars[0] = jnp.broadcast_to(norm, (8, LANES))
    out_scalars[1] = jnp.broadcast_to(curvature, (8, LANES))
    refs = (order_ref, matrix_ref, slots_ref, vertex_ref, place_ref, out_faces, out_sums)
    faces = local_part(nz, ncoarse, (residual[: nz * 3], residual[nz * 3 :]), image, refs)
    if len(sends) == 2:
        for axis, out in enumerate(sends):
            for z in range(nz):
                out[z] = faces[z * SIDES + axis]
    else:
        send_side(nz, mark_ref, 0, faces, sends[:2])
        send_side(nz, mark_ref, 1, faces, sends[2:])


def tiles(count, kind=F32):
    return jax.ShapeDtypeStruct((count, 8, LANES), kind)


def like(value):
    return jax.ShapeDtypeStruct(value.shape, value.dtype)


def call(kernel, outs, operands, first_space, flops, scratch=(), hbm=()):
    limit = 16 * 2**20 if max(x.size for x in operands) < 2**21 else 48 * 2**20
    vmem = pl.BlockSpec(memory_space=pltpu.VMEM)
    specs = [pl.BlockSpec(memory_space=first_space)] + [vmem] * (len(operands) - 1)
    operands = list(operands)
    for at in hbm:
        specs[at] = pl.BlockSpec(memory_space=pltpu.HBM)
        operands[at] = pltpu.with_memory_space_constraint(operands[at], pltpu.HBM)
    return pl.pallas_call(
        kernel,
        out_shape=outs,
        in_specs=specs,
        out_specs=[vmem] * len(outs),
        scratch_shapes=scratch,
        compiler_params=pltpu.CompilerParams(vmem_limit_bytes=limit),
        cost_estimate=pl.CostEstimate(flops=flops, bytes_accessed=2**20, transcendentals=0),
    )(*operands)


def shifted(value, axis, steps):
    count = lax.axis_size(axis)
    return lax.ppermute(value, axis, [(i, (i + steps) % count) for i in range(count)])


def paired(value, axis, mask):
    return lax.ppermute(value, axis, [(i, i ^ mask) for i in range(lax.axis_size(axis))])


def paired_other(value, axis):
    count = lax.axis_size(axis)
    return lax.ppermute(value, axis, [(i, (i + 1 if i % 2 else i - 1) % count) for i in range(count)])


def summed(sums, spread):
    if spread:
        return lax.all_to_all(sums, ("sub", "slab"), 0, 0, tiled=True)
    return doubled(doubled(sums, "slab", 1), "sub", 1)


def exchange(sums, sends, spread, rows=None):
    x_first, x_second, y_first, y_second = sends
    near = y_first.shape[0]
    blocks = []
    if rows is not None:
        y_first, y_second = jnp.concatenate([y_first, rows]), jnp.concatenate([y_second, rows])
    sums = summed(sums, spread)
    got_y_second, got_y_first = paired_other(y_second, "slab"), paired(y_first, "slab", 1)
    if rows is not None:
        blocks = [rows, got_y_first[near:], got_y_second[near:], paired(rows, "slab", 2)]
        got_y_first, got_y_second = got_y_first[:near], got_y_second[:near]
    got_x_second, got_x_first = paired_other(x_second, "sub"), paired(x_first, "sub", 1)
    return sums, [got_x_first, got_x_second, got_y_first, got_y_second], blocks


def exchange_last(sums, sends, spread):
    sums = summed(sums, spread)
    return sums, [shifted(sends[0], "sub", -1), shifted(sends[1], "slab", -1)]


def doubled(sums, axis, mask):
    while mask < lax.axis_size(axis):
        sums = sums + paired(sums, axis, mask)
        mask *= 2
    return sums


def coarse_inverse(coarse_factor, width):
    factor = lax.all_gather(coarse_factor, "slab", axis=0, tiled=True)
    count = factor.shape[0]
    inverse = lax.linalg.triangular_solve(
        factor, jnp.eye(count, dtype=F32), left_side=True, lower=True
    )
    both = jnp.dot(inverse.T, inverse, precision=lax.Precision.HIGHEST)
    columns = -(-count // LANES) * LANES
    return jnp.pad(both, ((0, width - count), (0, columns - count)))


def local(interface_rhs, order, inverse_rr, corner_response, corners, coarse_factor):
    nz, samples, dirs, face = interface_rhs.shape[2:]
    ncoarse = coarse_factor.shape[1]
    local_size = SIDES * face
    blocks = -(-(ncoarse + NUMBERS) // LANES)
    rhs = interface_rhs.transpose(0, 1, 2, 4, 3, 5).reshape(nz * dirs, samples, face)
    order = order.reshape(nz, 1, local_size)
    matrices = inverse_rr.reshape(nz, local_size, local_size)
    responses = corner_response.reshape(nz, CORNERS, local_size)
    place = lax.axis_index("slab")
    marks = jnp.stack([lax.axis_index("sub") % 2, place % 2, place]).astype(jnp.int32)
    marks = jnp.broadcast_to(marks[:, None, None], (3, 8, LANES))

    back_x = shifted(rhs, "sub", 1)
    back_y = shifted(rhs, "slab", 1)
    devices = lax.axis_size("sub") * lax.axis_size("slab")
    riding = blocks == 1 and lax.axis_size("slab") == 4 and coarse_factor.shape[0] % 8 == 0
    spread = blocks * devices <= 64
    copies = devices if spread else 1
    packed = spread and riding and devices % (LANES // PACK) == 0
    packed = packed and nz * 4 + NUMBERS <= PACK and ncoarse + NUMBERS + PACK <= LANES
    tables = nz * SIDES
    rows = coarse_factor.shape[0] // 8 if riding else 1
    part = coarse_factor[: rows * 8, :LANES]
    kept = nz * len(upper_blocks(local_size))
    kept = jax.ShapeDtypeStruct((kept, WIDE, WIDE), matrices.dtype)
    slots = -(-nz * CORNERS // 16) * 16
    order, slots, vertex, ids, matrices, unorder, response_faces, rows = call(
        functools.partial(prepare_kernel, nz),
        [like(order), jax.ShapeDtypeStruct((slots, local_size), jnp.bfloat16),
         jax.ShapeDtypeStruct((slots, blocks * LANES), jnp.bfloat16),
         jax.ShapeDtypeStruct((8, LANES), jnp.int32), kept, like(order), tiles(tables), tiles(rows)],
        [order, responses, part, corners.reshape(nz, 1, CORNERS), matrices],
        pltpu.HBM,
        2**30,
        [pltpu.VMEM(responses.shape, responses.dtype), pltpu.VMEM(part.shape, F32),
         pltpu.VMEM((nz, 1, CORNERS), jnp.int32), pltpu.SemaphoreType.DMA((4 + kept.shape[0],))],
        range(5),
    )
    own = [order, matrices, slots, vertex, unorder]
    residual, faces, sums, *sends = call(
        functools.partial(start_kernel, packed, nz, ncoarse),
        [tiles(nz * 5), tiles(tables), tiles(blocks * copies)]
        + [tiles(2 * nz + 1)] * 4,
        [marks, rhs, back_x, back_y] + own + [ids, response_faces],
        pltpu.VMEM,
        2**30,
    )
    state = [residual, ids]

    def invert(factor):
        if not riding:
            return coarse_inverse(coarse_factor, blocks * LANES)
        square = jax.ShapeDtypeStruct((LANES, LANES), F32)
        return call(
            functools.partial(factor_kernel, ncoarse), [square], [marks] + factor,
            pltpu.VMEM, 2**29, [pltpu.VMEM(square.shape, F32)],
        )[0]

    for iteration in range(ITERS):
        first, last = iteration == 0, iteration == ITERS - 1
        if last:
            sums, received = exchange_last(sums, sends, spread)
        else:
            ride = rows if first and riding else None
            sums, received, factor = exchange(sums, sends, spread, ride)
        if first:
            inverse = invert(factor)
        if first and packed:
            wide = jax.ShapeDtypeStruct((devices * PACK, LANES), jnp.bfloat16)
            scatter = call(
                functools.partial(spread_kernel, ncoarse), [wide], [sums], pltpu.VMEM, 2**26
            )
        rows_at = list(scatter) if packed and not first else []
        operands = [marks, sums, inverse] + rows_at + received[::-1] + [faces, response_faces] + state
        kernel = functools.partial(step_kernel, first, last, nz, ncoarse)
        if last:
            outs = [tiles(nz * 3)] * 2
            multipliers, residual = call(kernel, outs, operands, pltpu.VMEM, 2**30)
            break
        outs = [tiles(nz * 5), tiles(nz * 5), tiles(nz * 3), tiles(nz * 3), tiles(2)]
        sides = 2 if iteration == ITERS - 2 else 4
        outs += [tiles(tables), jax.ShapeDtypeStruct((copies, 1, LANES), F32) if packed else tiles(blocks * copies)]
        outs += [tiles(nz)] * sides
        if first:
            outs += [jax.ShapeDtypeStruct((8, LANES), jnp.int32), tiles(nz * 4)]
        results = call(kernel, outs, operands + own, pltpu.VMEM, 2**31)
        residual, image, direction, multipliers, step, faces, sums = results[:7]
        sends = results[7 : 7 + sides]
        if first:
            ids, near = results[7 + sides :]
        state = [residual, ids, near, image, direction, multipliers, step]

    def placed(value):
        value = value.reshape(interface_rhs.shape[:3] + (dirs, samples, face))
        return value.transpose(0, 1, 2, 4, 3, 5)

    return placed(multipliers), placed(residual)


def solution(mesh):
    in_specs = (
        P("sub", "slab", None, None, None, None),
        P("sub", "slab", None, None),
        P("sub", "slab", None, None, None),
        P("sub", "slab", None, None, None),
        P("sub", "slab", None, None),
        P("slab", None),
    )
    out_specs = (P("sub", "slab", None, None, None, None), P("sub", "slab", None, None, None, None))
    return jax.shard_map(local, mesh=mesh, in_specs=in_specs, out_specs=out_specs, check_vma=False)
```

```python
import functools

import jax
import jax.numpy as jnp
from jax import lax
from jax.experimental import pallas as pl
from jax.experimental.pallas import tpu as pltpu
from jax.sharding import PartitionSpec as P

ITERS = 3
F32 = jnp.float32
LANES = 128
CORNERS = 8
WIDE = 256
SIDES = 6
BACK_X, AHEAD_X, BACK_Y, AHEAD_Y = range(4)
PARITY, PLACE = 0, 2
PACK = 16
NUMBERS = 3


def upper_blocks(size):
    return [(i, j) for i in range(size // WIDE) for j in range(i, size // WIDE)]


def symmetric_dot(vector, matrix_ref, z):
    size = vector.shape[1]
    kept = upper_blocks(size)
    parts = [vector[:, at : at + WIDE] for at in range(0, size, WIDE)]
    outs = [None] * len(parts)
    for at, (i, j) in enumerate(kept):
        block = matrix_ref[z * len(kept) + at]
        terms = [(j, jnp.dot(parts[i], block, preferred_element_type=F32))]
        if i != j:
            turned = (((1,), (1,)), ((), ()))
            terms.append((i, lax.dot_general(parts[j], block, turned, preferred_element_type=F32)))
        for to, term in terms:
            outs[to] = term if outs[to] is None else outs[to] + term
    return jnp.concatenate(outs, axis=1)


def lane_iota():
    return lax.broadcasted_iota(jnp.int32, (8, LANES), 1)


def pick_lanes(tiles, high, low):
    out = None
    for number, tile in enumerate(tiles):
        moved = jnp.take_along_axis(tile, low, axis=1, mode="promise_in_bounds")
        out = moved if out is None else jnp.where(high == number, moved, out)
    return out


def bf16_parts(value, count):
    parts = []
    for _ in range(count):
        parts.append(value.astype(jnp.bfloat16))
        value = value - parts[-1].astype(F32)
    return jnp.concatenate(parts, axis=0)


def pack_sums(nz, terms, numbers):
    slot = lax.broadcasted_iota(jnp.int32, (terms.shape[1], LANES), 0)
    lane = lax.broadcasted_iota(jnp.int32, slot.shape, 1)
    level = lax.shift_right_logical(slot, 3) + lax.bitwise_and(slot, 1)
    level = jnp.where(level >= nz, level - nz, level)
    vertex = level * 4 + lax.bitwise_and(lax.shift_right_logical(slot, 1), 3)
    hot = (lax.bitwise_and(lane, PACK - 1) == vertex) & (slot < nz * CORNERS)
    wide = jnp.dot(
        two_parts(terms), jnp.where(hot, 1.0, 0.0).astype(jnp.bfloat16), preferred_element_type=F32
    )
    wide = wide[:8] + wide[8:]
    lane = lane_iota()
    for at, number in enumerate(numbers):
        wide = jnp.where(lax.bitwise_and(lane, PACK - 1) == nz * 4 + at, number, wide)
    sample = lax.broadcasted_iota(jnp.int32, (8, LANES), 0)
    return jnp.sum(jnp.where(lane // PACK == sample, wide, 0.0), axis=0, keepdims=True)


def unpack_sums(sums_ref, spread_ref):
    lane = lane_iota()
    place = lax.broadcasted_iota(jnp.int32, (8, LANES), 0) * PACK + lax.bitwise_and(lane, PACK - 1)
    group = LANES // PACK
    tiles = []
    for first in range(0, sums_ref.shape[0], group):
        tile = jnp.zeros((8, LANES), F32)
        for at in range(group):
            row = jnp.broadcast_to(sums_ref[first + at], (8, LANES))
            row = jnp.take_along_axis(row, place, axis=1, mode="promise_in_bounds")
            tile = jnp.where(lane // PACK == at, row, tile)
        tiles.append(tile)
    parts = bf16_parts(jnp.concatenate(tiles, axis=1), 3)
    total = jnp.dot(parts, spread_ref[...], preferred_element_type=F32)
    return total[:8] + (total[8:16] + total[16:])


def own_vertices(nz, ncoarse, ids):
    at = lane_iota() - ncoarse - NUMBERS
    inside = (at >= 0) & (at < PACK)
    at = jnp.where(inside, at, 0)
    slot = jnp.where(at < nz * 4, (at // 4) * CORNERS + lax.bitwise_and(at, 3) * 2, 0)
    vertex = jnp.take_along_axis(ids, slot, axis=1, mode="promise_in_bounds")
    vertex = jnp.where(at < nz * 4, vertex, ncoarse + at - nz * 4)
    vertex = jnp.where(at < nz * 4 + NUMBERS, vertex, -1)
    return jnp.where(inside, vertex.astype(F32), 0.0)


def spread_kernel(ncoarse, sums_ref, spread_ref):
    lane = lane_iota()
    lane_square = lax.broadcasted_iota(jnp.int32, (LANES, LANES), 1)
    place = ncoarse + NUMBERS + lax.bitwise_and(lane, PACK - 1)
    group = LANES // PACK
    for first in range(0, sums_ref.shape[0], group):
        line = jnp.zeros((8, LANES), F32)
        for at in range(group):
            row = jnp.take_along_axis(sums_ref[first + at], place, axis=1, mode="promise_in_bounds")
            line = jnp.where(lane // PACK == at, row, line)
        column = jnp.broadcast_to(line[0:1].astype(jnp.int32), (LANES, LANES)).T
        hot = jnp.where(column == lane_square, 1.0, 0.0).astype(jnp.bfloat16)
        spread_ref[first * PACK : (first + group) * PACK, :] = hot


def two_parts(value):
    upper = value.astype(jnp.bfloat16)
    lower = (value - upper.astype(F32)).astype(jnp.bfloat16)
    return jnp.concatenate([upper, lower], axis=0)


def lane_sum(tile):
    return jnp.sum(tile, axis=1, keepdims=True)


def order_tiles(order_ref, z):
    high, low = [], []
    for block in range(SIDES):
        row = jnp.broadcast_to(order_ref[z, :, block * LANES : (block + 1) * LANES], (8, LANES))
        high.append(lax.shift_right_logical(row, 7))
        low.append(lax.bitwise_and(row, LANES - 1))
    return high, low


def invert_own_block(rows_ref, place):
    count = rows_ref.shape[0]
    tall = count * 8
    rows = jnp.concatenate([rows_ref[at] for at in range(count)], axis=0)
    lane = lax.broadcasted_iota(jnp.int32, (tall, LANES), 1)
    sub = lax.broadcasted_iota(jnp.int32, (tall, LANES), 0)
    start = jnp.broadcast_to(place, (tall, LANES)) * tall
    block = jnp.take_along_axis(
        rows, jnp.minimum(start + lane, LANES - 1), axis=1, mode="promise_in_bounds"
    )
    diagonal = jnp.take_along_axis(block, sub, axis=1, mode="promise_in_bounds")
    solved = jnp.where(lane == sub, 1.0 / diagonal, 0.0)
    block = block / diagonal
    for q in range(tall - 1):
        solved = jnp.where(sub > q, solved - block[:, q : q + 1] * solved[q : q + 1, :], solved)
    inside = (lane >= start) & (lane < start + tall)
    moved = jnp.take_along_axis(
        solved, jnp.where(inside, lane - start, 0), axis=1, mode="promise_in_bounds"
    )
    rows = jnp.where(inside, moved, rows)
    for at in range(count):
        rows_ref[at] = rows[at * 8 : (at + 1) * 8, :]


def prepare_kernel(
    nz, riding, order_hbm, response_hbm, factor_hbm, corners_hbm, matrix_hbm, mark_ref,
    order_ref, slots_ref, vertex_ref, ids_ref, matrix_ref, place_ref, faces_ref, rows_ref,
    response_ref, factor_ref, corners_ref, done,
):
    pairs = [(order_hbm, order_ref), (response_hbm, response_ref), (factor_hbm, factor_ref)]
    pairs.append((corners_hbm, corners_ref))
    small = len(pairs)
    for z in range(nz):
        for i, j in upper_blocks(matrix_hbm.shape[1]):
            block = matrix_hbm.at[z, pl.ds(i * WIDE, WIDE), pl.ds(j * WIDE, WIDE)]
            pairs.append((block, matrix_ref.at[len(pairs) - small]))
    copies = [pltpu.make_async_copy(*pair, done.at[at]) for at, pair in enumerate(pairs)]
    for copy in copies:
        copy.start()
    for copy in copies[:small]:
        copy.wait()
    rows_ref[...] = jnp.zeros_like(rows_ref)
    for at in range(rows_ref.shape[0]):
        rows_ref[at, :, 0 : factor_ref.shape[1]] = factor_ref[at * 8 : (at + 1) * 8, :]
    if riding:
        invert_own_block(rows_ref, mark_ref[PLACE, 0:1, :])
    response = response_ref[...].astype(F32)
    lane = lane_iota()
    lane_square = lax.broadcasted_iota(jnp.int32, (LANES, LANES), 1)
    ids_ref[...] = jnp.zeros_like(ids_ref)
    for z in range(nz):
        ids_ref[:, z * CORNERS : (z + 1) * CORNERS] = jnp.broadcast_to(corners_ref[z], (8, CORNERS))
    slots = slots_ref.shape[0]
    column = jnp.broadcast_to(ids_ref[0:1, :], (LANES, LANES)).T[:slots]
    for at in range(0, vertex_ref.shape[1], LANES):
        hot = jnp.where(column == lane_square[:slots] + at, 1.0, 0.0)
        vertex_ref[:, at : at + LANES] = hot.astype(jnp.bfloat16)
    pieces = [response[z] for z in range(nz)]
    if slots > nz * CORNERS:
        pieces.append(jnp.zeros((slots - nz * CORNERS, response.shape[2]), F32))
    slots_ref[...] = jnp.concatenate(pieces, axis=0).astype(jnp.bfloat16)
    for z in range(nz):
        total = jnp.zeros((16, SIDES * LANES), F32)
        for block in range(SIDES):
            row = order_ref[z, :, block * LANES : (block + 1) * LANES]
            column = jnp.broadcast_to(row, (LANES, LANES)).T
            hot = jnp.concatenate(
                [
                    jnp.where(column == lane_square + side * LANES, 1.0, 0.0).astype(jnp.bfloat16)
                    for side in range(SIDES)
                ],
                axis=1,
            )
            places = jnp.concatenate([lane.astype(F32), jnp.full((8, LANES), block, F32)], axis=0)
            total += jnp.dot(places.astype(jnp.bfloat16), hot, preferred_element_type=F32)
        own = [response[z][:, side * LANES : (side + 1) * LANES] for side in range(SIDES)]
        for side in range(SIDES):
            span = slice(side * LANES, (side + 1) * LANES)
            low = total[:8, span].astype(jnp.int32)
            high = total[8:, span].astype(jnp.int32)
            place_ref[z, :, span] = (high * LANES + low)[0:1]
            faces_ref[z * SIDES + side] = pick_lanes(own, high, low)
    for copy in copies[small:]:
        copy.wait()


def apart(value, slices, size):
    pieces, at, used = [], 0, 0
    for rows in slices:
        pieces += [jnp.zeros((rows.start - at, size), F32), value[used : used + rows.stop - rows.start]]
        at, used = rows.stop, used + rows.stop - rows.start
    if at < size:
        pieces.append(jnp.zeros((size - at, size), F32))
    return jnp.concatenate(pieces, axis=0)


def factor_kernel(count, mark_ref, *refs):
    *blocks, inverse_ref, square = refs
    size = square.shape[0]
    row = lax.broadcasted_iota(jnp.int32, (size, size), 0)
    column = lax.broadcasted_iota(jnp.int32, (size, size), 1)
    place = mark_ref[PLACE]
    tall = blocks[0].shape[0]
    for at in range(4 * tall):
        tile = blocks[0][at % tall]
        for mask, block in zip((1, 3, 2), blocks[1:]):
            tile = jnp.where(lax.bitwise_xor(place, mask) == at // tall, block[at % tall], tile)
        square[at * 8 : (at + 1) * 8, :] = tile
    square[4 * tall * 8 :, :] = jnp.zeros((size - 4 * tall * 8, LANES), F32)
    square[...] = jnp.where(row < count, square[...], jnp.where(row == column, 1.0, 0.0))
    factor = square[...]
    width = count // 4
    inverse = jnp.where(row // width == column // width, factor, 0.0)
    while width < count:
        lower = [slice(at, min(at + width, -(-count // 8) * 8)) for at in range(width, count, 2 * width)]
        below = jnp.where(
            (row // (2 * width) == column // (2 * width)) & (row // width > column // width), factor, 0.0
        )
        part = jnp.concatenate([below[rows] for rows in lower], axis=0)
        left = jnp.concatenate([inverse[rows] for rows in lower], axis=0)
        inner = jnp.dot(part, inverse, precision=lax.Precision.HIGHEST, preferred_element_type=F32)
        change = jnp.dot(
            left, apart(inner, lower, size), precision=lax.Precision.HIGHEST, preferred_element_type=F32
        )
        inverse = inverse - apart(change, lower, size)
        width *= 2
    both = lax.dot_general(
        inverse,
        inverse,
        (((0,), (0,)), ((), ())),
        precision=lax.Precision.HIGHEST,
        preferred_element_type=F32,
    )
    inverse_ref[...] = jnp.where((row < count) & (column < count), both, 0.0)


def send_side(nz, mark_ref, axis, faces, outs):
    even = mark_ref[PARITY + axis] == 0
    first, second = outs
    for z in range(nz):
        up, down = faces[z * SIDES + 3 + axis], faces[z * SIDES + axis]
        first[z] = jnp.where(even, up, down)
        second[z] = jnp.where(even, down, up)


def local_part(nz, ncoarse, residual, image, refs, ids=None):
    (order_ref, matrix_ref, slots_ref, vertex_ref, place_ref, faces_ref, sums_ref) = refs
    own, back = residual
    lane = lane_iota()
    norm = jnp.zeros((8, LANES), F32)
    cross = jnp.zeros((8, LANES), F32)
    for at in range(nz * 3):
        norm += own[at] * own[at]
        if image is not None:
            cross += own[at] * image[at]
    energy = jnp.zeros((8, LANES), F32)
    parts, results = [], []
    for z in range(nz):
        sides = [
            -back[z],
            -back[nz + z],
            -own[((z - 1) % nz) * 3 + 2],
            own[z * 3],
            own[z * 3 + 1],
            own[z * 3 + 2],
        ]
        high, low = order_tiles(order_ref, z)
        vector = jnp.concatenate([pick_lanes(sides, high[s], low[s]) for s in range(SIDES)], axis=1)
        parts.append(two_parts(vector))
        solved = symmetric_dot(parts[z], matrix_ref, z)
        solved = solved[:8] + solved[8:]
        results.append([solved[:, s * LANES : (s + 1) * LANES] for s in range(SIDES)])
        for s in range(SIDES):
            energy += results[z][s] * vector[:, s * LANES : (s + 1) * LANES]
    numbers = (lane_sum(norm), lane_sum(cross), lane_sum(energy))
    products = lax.dot_general(
        jnp.concatenate(parts, axis=0), slots_ref[...], (((1,), (1,)), ((), ())),
        preferred_element_type=F32,
    )
    slot = lax.broadcasted_iota(jnp.int32, (8, products.shape[1]), 1)
    terms = jnp.zeros(slot.shape, F32)
    for z in range(nz):
        both = products[z * 16 : z * 16 + 8] + products[z * 16 + 8 : z * 16 + 16]
        terms = jnp.where(lax.shift_right_logical(slot, 3) == z, both, terms)
    if sums_ref.shape[1] == 1:
        row = pack_sums(nz, terms, numbers)
        for copy in range(sums_ref.shape[0]):
            sums_ref[copy] = row
    else:
        by_vertex = jnp.dot(two_parts(terms), vertex_ref[...], preferred_element_type=F32)
        by_vertex = by_vertex[:8] + by_vertex[8:]
        blocks = vertex_ref.shape[1] // LANES
        for block in range(blocks):
            where = lane + block * LANES
            tile = by_vertex[:, block * LANES : (block + 1) * LANES]
            for at, number in enumerate(numbers):
                tile += jnp.where(where == ncoarse + at, number, 0.0)
            if ids is not None:
                tile += own_vertices(nz, ncoarse, ids)
            for copy in range(0, sums_ref.shape[0], blocks):
                sums_ref[copy + block] = tile
    faces = []
    for z in range(nz):
        high, low = order_tiles(place_ref, z)
        for s in range(SIDES):
            at = z * SIDES + s
            faces.append(pick_lanes(results[z], high[s], low[s]))
            faces_ref[at] = faces[at]
    return faces


def start_kernel(
    packed, nz, ncoarse, mark_ref, rhs_ref, back_x_ref, back_y_ref, order_ref, matrix_ref,
    slots_ref, vertex_ref, place_ref, ids_ref, response_faces_ref,
    residual_ref, faces_ref, sums_ref, x_first, x_second, y_first, y_second,
):
    own = [rhs_ref[at] for at in range(nz * 3)]
    back = [back_x_ref[z * 3] for z in range(nz)] + [back_y_ref[z * 3 + 1] for z in range(nz)]
    for at, tile in enumerate(own + back):
        residual_ref[at] = tile
    refs = (order_ref, matrix_ref, slots_ref, vertex_ref, place_ref, faces_ref, sums_ref)
    faces = local_part(nz, ncoarse, (own, back), None, refs, ids_ref[...] if packed else None)
    numbers = ids_ref[...].astype(F32)
    responses = [response_faces_ref[at] for at in range(nz * SIDES)]
    for axis, outs in ((0, (x_first, x_second)), (1, (y_first, y_second))):
        send_side(nz, mark_ref, axis, faces, outs)
        send_side(nz, mark_ref, axis, responses, [out.at[nz : 2 * nz] for out in outs])
        for out in outs:
            out[2 * nz] = numbers


def start_order(first, last):
    if last:
        return (0, 1)
    return (3, 2, 1, 0) if first else (1, 3, 0, 2)


def step_kernel(first, last, nz, ncoarse, *refs):
    refs = list(refs)

    def take(count):
        taken = refs[:count]
        del refs[:count]
        return taken

    mark_ref, sums_ref, inverse_ref = take(3)
    packed = sums_ref.shape[1] == 1
    if packed:
        (spread_ref,) = take(1)
    order = start_order(first, last)
    received = [got for _, got in sorted(zip(order, take(len(order))), key=lambda pair: pair[0])]
    faces_ref, response_faces_ref, residual_ref = take(3)
    if first:
        (ids_ref,) = take(1)
    else:
        ids_ref, near_ref, image_ref, direction_ref, multipliers_ref, scalars_ref = take(6)
    if not last:
        order_ref, matrix_ref, slots_ref, vertex_ref, place_ref = take(5)
        (out_residual, out_image, out_direction, out_multipliers, out_scalars, out_faces, out_sums) = take(7)
        sends = take(len(refs) - (2 if first else 0))
        if first:
            out_ids, out_near = take(2)
    else:
        out_multipliers, out_residual = take(2)

    even_x, even_y = mark_ref[PARITY] == 0, mark_ref[PARITY + 1] == 0
    lane = lane_iota()

    def ahead_and_back(at):
        if last:
            return {AHEAD_X: received[0][at], AHEAD_Y: received[1][at]}
        x_first, x_second, y_first, y_second = [ref[at] for ref in received]
        return {
            AHEAD_X: jnp.where(even_x, x_first, x_second),
            BACK_X: jnp.where(even_x, x_second, x_first),
            AHEAD_Y: jnp.where(even_y, y_first, y_second),
            BACK_Y: jnp.where(even_y, y_second, y_first),
        }

    near_faces, near_responses = {}, {}
    for z in range(nz):
        for side, tile in ahead_and_back(z).items():
            near_faces[side, z] = tile
    if first:
        ids = ids_ref[...]
        for side, tile in ahead_and_back(2 * nz).items():
            shift = nz * CORNERS * (side + 1)
            moved = pltpu.roll(tile, shift, axis=1).astype(jnp.int32)
            ids = jnp.where((lane >= shift) & (lane < shift + nz * CORNERS), moved, ids)
        out_ids[...] = ids
        for z in range(nz):
            for side, tile in ahead_and_back(nz + z).items():
                near_responses[side, z] = tile
                out_near[side * nz + z] = tile
    else:
        ids = ids_ref[...]
        for z in range(nz):
            for side in (AHEAD_X, AHEAD_Y) if last else range(4):
                near_responses[side, z] = near_ref[side * nz + z]

    blocks = inverse_ref.shape[0] // LANES
    if packed:
        sums = [unpack_sums(sums_ref, spread_ref)]
    else:
        sums = [sums_ref[block] for block in range(blocks)]
        for copy in range(blocks, sums_ref.shape[0], blocks):
            sums = [total + sums_ref[copy + block] for block, total in enumerate(sums)]
    coarse = jnp.dot(
        jnp.concatenate(sums, axis=1),
        inverse_ref[...],
        precision=lax.Precision.HIGHEST,
        preferred_element_type=F32,
    )
    coarse = [coarse[:, b * LANES : (b + 1) * LANES] for b in range(coarse.shape[1] // LANES)]
    energy = sum(lane_sum(a * b) for a, b in zip(sums, coarse))

    def number(at):
        block, place = divmod(ncoarse + at, LANES)
        return sums[block][:, place : place + 1]

    norm, cross, energy = number(0), number(1), energy + number(2)
    if first:
        curvature = energy
    else:
        last_norm, last_curvature = scalars_ref[0][:, 0:1], scalars_ref[1][:, 0:1]
        ratio = norm / last_norm
        curvature = energy + 2.0 * ratio * cross + ratio * ratio * last_curvature
    step = norm / curvature

    picked = pick_lanes(coarse, lax.shift_right_logical(ids, 7), lax.bitwise_and(ids, LANES - 1))

    wide = {}

    def lifted(tile, response, slot):
        for corner in range(CORNERS):
            at = slot * CORNERS + corner
            if at not in wide:
                wide[at] = jnp.broadcast_to(picked[:, at : at + 1], (8, LANES))
            tile = tile + wide[at] * response[corner : corner + 1, :]
        return tile

    def own_side(z, side):
        at = z * SIDES + side
        return lifted(faces_ref[at], response_faces_ref[at], z)

    def near_side(side, z):
        return lifted(near_faces[side, z], near_responses[side, z], nz * (side + 1) + z)

    fresh = [None] * (nz * 5)
    third_down = [own_side(z, 2) for z in range(nz)]
    for z in range(nz):
        fresh[z * 3] = own_side(z, 3) - near_side(AHEAD_X, z)
        fresh[z * 3 + 1] = own_side(z, 4) - near_side(AHEAD_Y, z)
        fresh[z * 3 + 2] = own_side(z, 5) - third_down[(z + 1) % nz]
        if not last:
            fresh[nz * 3 + z] = near_side(BACK_X, z) - own_side(z, 0)
            fresh[nz * 4 + z] = near_side(BACK_Y, z) - own_side(z, 1)

    count = nz * 3 if last else nz * 5
    residual, image = [], []
    for at in range(count):
        new_image = fresh[at] if first else fresh[at] + ratio * image_ref[at]
        old_residual = residual_ref[at]
        residual.append(old_residual - step * new_image)
        image.append(new_image)
        if at < nz * 3:
            direction = old_residual if first else old_residual + ratio * direction_ref[at]
            multipliers = step * direction if first else multipliers_ref[at] + step * direction
            if last:
                out_multipliers[at] = multipliers
                out_residual[at] = residual[at]
            else:
                out_direction[at] = direction
                out_multipliers[at] = multipliers
    if last:
        return
    for at in range(count):
        out_residual[at] = residual[at]
        out_image[at] = image[at]
    out_scalars[0] = jnp.broadcast_to(norm, (8, LANES))
    out_scalars[1] = jnp.broadcast_to(curvature, (8, LANES))
    refs = (order_ref, matrix_ref, slots_ref, vertex_ref, place_ref, out_faces, out_sums)
    faces = local_part(nz, ncoarse, (residual[: nz * 3], residual[nz * 3 :]), image, refs)
    if len(sends) == 2:
        for axis, out in enumerate(sends):
            for z in range(nz):
                out[z] = faces[z * SIDES + axis]
    else:
        send_side(nz, mark_ref, 0, faces, sends[:2])
        send_side(nz, mark_ref, 1, faces, sends[2:])


def tiles(count, kind=F32):
    return jax.ShapeDtypeStruct((count, 8, LANES), kind)


def like(value):
    return jax.ShapeDtypeStruct(value.shape, value.dtype)


def call(kernel, outs, operands, first_space, flops, scratch=(), hbm=()):
    limit = 16 * 2**20 if max(x.size for x in operands) < 2**21 else 48 * 2**20
    vmem = pl.BlockSpec(memory_space=pltpu.VMEM)
    specs = [pl.BlockSpec(memory_space=first_space)] + [vmem] * (len(operands) - 1)
    operands = list(operands)
    for at in hbm:
        specs[at] = pl.BlockSpec(memory_space=pltpu.HBM)
        operands[at] = pltpu.with_memory_space_constraint(operands[at], pltpu.HBM)
    return pl.pallas_call(
        kernel,
        out_shape=outs,
        in_specs=specs,
        out_specs=[vmem] * len(outs),
        scratch_shapes=scratch,
        compiler_params=pltpu.CompilerParams(vmem_limit_bytes=limit),
        cost_estimate=pl.CostEstimate(flops=flops, bytes_accessed=2**20, transcendentals=0),
    )(*operands)


def shifted(value, axis, steps):
    count = lax.axis_size(axis)
    return lax.ppermute(value, axis, [(i, (i + steps) % count) for i in range(count)])


def paired(value, axis, mask):
    return lax.ppermute(value, axis, [(i, i ^ mask) for i in range(lax.axis_size(axis))])


def paired_other(value, axis):
    count = lax.axis_size(axis)
    return lax.ppermute(value, axis, [(i, (i + 1 if i % 2 else i - 1) % count) for i in range(count)])


def summed(sums, spread):
    if spread:
        return lax.all_to_all(sums, ("sub", "slab"), 0, 0, tiled=True)
    return doubled(doubled(sums, "slab", 1), "sub", 1)


def exchange(sums, sends, spread, rows=None):
    x_first, x_second, y_first, y_second = sends
    near = y_first.shape[0]
    blocks = []
    if rows is not None:
        y_first, y_second = jnp.concatenate([y_first, rows]), jnp.concatenate([y_second, rows])
    sums = summed(sums, spread)
    got_y_second, got_y_first = paired_other(y_second, "slab"), paired(y_first, "slab", 1)
    if rows is not None:
        blocks = [rows, got_y_first[near:], got_y_second[near:], paired(rows, "slab", 2)]
        got_y_first, got_y_second = got_y_first[:near], got_y_second[:near]
    got_x_second, got_x_first = paired_other(x_second, "sub"), paired(x_first, "sub", 1)
    return sums, [got_x_first, got_x_second, got_y_first, got_y_second], blocks


def exchange_last(sums, sends, spread):
    sums = summed(sums, spread)
    return sums, [shifted(sends[0], "sub", -1), shifted(sends[1], "slab", -1)]


def doubled(sums, axis, mask):
    while mask < lax.axis_size(axis):
        sums = sums + paired(sums, axis, mask)
        mask *= 2
    return sums


def coarse_inverse(coarse_factor, width):
    factor = lax.all_gather(coarse_factor, "slab", axis=0, tiled=True)
    count = factor.shape[0]
    inverse = lax.linalg.triangular_solve(
        factor, jnp.eye(count, dtype=F32), left_side=True, lower=True
    )
    both = jnp.dot(inverse.T, inverse, precision=lax.Precision.HIGHEST)
    columns = -(-count // LANES) * LANES
    return jnp.pad(both, ((0, width - count), (0, columns - count)))


def local(interface_rhs, order, inverse_rr, corner_response, corners, coarse_factor):
    nz, samples, dirs, face = interface_rhs.shape[2:]
    ncoarse = coarse_factor.shape[1]
    local_size = SIDES * face
    blocks = -(-(ncoarse + NUMBERS) // LANES)
    rhs = interface_rhs.transpose(0, 1, 2, 4, 3, 5).reshape(nz * dirs, samples, face)
    order = order.reshape(nz, 1, local_size)
    matrices = inverse_rr.reshape(nz, local_size, local_size)
    responses = corner_response.reshape(nz, CORNERS, local_size)
    place = lax.axis_index("slab")
    marks = jnp.stack([lax.axis_index("sub") % 2, place % 2, place]).astype(jnp.int32)
    marks = jnp.broadcast_to(marks[:, None, None], (3, 8, LANES))

    back_x = shifted(rhs, "sub", 1)
    back_y = shifted(rhs, "slab", 1)
    devices = lax.axis_size("sub") * lax.axis_size("slab")
    riding = blocks == 1 and lax.axis_size("slab") == 4 and coarse_factor.shape[0] % 8 == 0
    spread = blocks * devices <= 64
    copies = devices if spread else 1
    packed = spread and riding and devices % (LANES // PACK) == 0
    packed = packed and nz * 4 + NUMBERS <= PACK and ncoarse + NUMBERS + PACK <= LANES
    tables = nz * SIDES
    rows = coarse_factor.shape[0] // 8 if riding else 1
    part = coarse_factor[: rows * 8, :LANES]
    kept = nz * len(upper_blocks(local_size))
    kept = jax.ShapeDtypeStruct((kept, WIDE, WIDE), matrices.dtype)
    slots = -(-nz * CORNERS // 16) * 16
    order, slots, vertex, ids, matrices, unorder, response_faces, rows = call(
        functools.partial(prepare_kernel, nz, riding),
        [like(order), jax.ShapeDtypeStruct((slots, local_size), jnp.bfloat16),
         jax.ShapeDtypeStruct((slots, blocks * LANES), jnp.bfloat16),
         jax.ShapeDtypeStruct((8, LANES), jnp.int32), kept, like(order), tiles(tables), tiles(rows)],
        [order, responses, part, corners.reshape(nz, 1, CORNERS), matrices, marks],
        pltpu.HBM,
        2**30,
        [pltpu.VMEM(responses.shape, responses.dtype), pltpu.VMEM(part.shape, F32),
         pltpu.VMEM((nz, 1, CORNERS), jnp.int32), pltpu.SemaphoreType.DMA((4 + kept.shape[0],))],
        range(5),
    )
    own = [order, matrices, slots, vertex, unorder]
    residual, faces, sums, *sends = call(
        functools.partial(start_kernel, packed, nz, ncoarse),
        [tiles(nz * 5), tiles(tables), tiles(blocks * copies)]
        + [tiles(2 * nz + 1)] * 4,
        [marks, rhs, back_x, back_y] + own + [ids, response_faces],
        pltpu.VMEM,
        2**30,
    )
    state = [residual, ids]

    def invert(factor):
        if not riding:
            return coarse_inverse(coarse_factor, blocks * LANES)
        square = jax.ShapeDtypeStruct((LANES, LANES), F32)
        return call(
            functools.partial(factor_kernel, ncoarse), [square], [marks] + factor,
            pltpu.VMEM, 2**29, [pltpu.VMEM(square.shape, F32)],
        )[0]

    for iteration in range(ITERS):
        first, last = iteration == 0, iteration == ITERS - 1
        if last:
            sums, received = exchange_last(sums, sends, spread)
        else:
            ride = rows if first and riding else None
            sums, received, factor = exchange(sums, sends, spread, ride)
        if first:
            inverse = invert(factor)
        if first and packed:
            wide = jax.ShapeDtypeStruct((devices * PACK, LANES), jnp.bfloat16)
            scatter = call(
                functools.partial(spread_kernel, ncoarse), [wide], [sums], pltpu.VMEM, 2**26
            )
        rows_at = list(scatter) if packed and not first else []
        operands = [marks, sums, inverse] + rows_at + [received[at] for at in start_order(first, last)] + [faces, response_faces] + state
        kernel = functools.partial(step_kernel, first, last, nz, ncoarse)
        if last:
            outs = [tiles(nz * 3)] * 2
            multipliers, residual = call(kernel, outs, operands, pltpu.VMEM, 2**30)
            break
        outs = [tiles(nz * 5), tiles(nz * 5), tiles(nz * 3), tiles(nz * 3), tiles(2)]
        sides = 2 if iteration == ITERS - 2 else 4
        outs += [tiles(tables), jax.ShapeDtypeStruct((copies, 1, LANES), F32) if packed else tiles(blocks * copies)]
        outs += [tiles(nz)] * sides
        if first:
            outs += [jax.ShapeDtypeStruct((8, LANES), jnp.int32), tiles(nz * 4)]
        results = call(kernel, outs, operands + own, pltpu.VMEM, 2**31)
        residual, image, direction, multipliers, step, faces, sums = results[:7]
        sends = results[7 : 7 + sides]
        if first:
            ids, near = results[7 + sides :]
        state = [residual, ids, near, image, direction, multipliers, step]

    def placed(value):
        value = value.reshape(interface_rhs.shape[:3] + (dirs, samples, face))
        return value.transpose(0, 1, 2, 4, 3, 5)

    return placed(multipliers), placed(residual)


def solution(mesh):
    in_specs = (
        P("sub", "slab", None, None, None, None),
        P("sub", "slab", None, None),
        P("sub", "slab", None, None, None),
        P("sub", "slab", None, None, None),
        P("sub", "slab", None, None),
        P("slab", None),
    )
    out_specs = (P("sub", "slab", None, None, None, None), P("sub", "slab", None, None, None, None))
    return jax.shard_map(local, mesh=mesh, in_specs=in_specs, out_specs=out_specs, check_vma=False)
```

```python
import functools

import jax
import jax.numpy as jnp
from jax import lax
from jax.experimental import pallas as pl
from jax.experimental.pallas import tpu as pltpu
from jax.sharding import PartitionSpec as P

ITERS = 3
F32 = jnp.float32
LANES = 128
CORNERS = 8
WIDE = 256
SIDES = 6
BACK_X, AHEAD_X, BACK_Y, AHEAD_Y = range(4)
PARITY, PLACE = 0, 2
PACK = 16
NUMBERS = 3


def upper_blocks(size):
    return [(i, j) for i in range(size // WIDE) for j in range(i, size // WIDE)]


def symmetric_dot(vector, matrix_ref, z):
    size = vector.shape[1]
    kept = upper_blocks(size)
    parts = [vector[:, at : at + WIDE] for at in range(0, size, WIDE)]
    outs = [None] * len(parts)
    for at, (i, j) in enumerate(kept):
        block = matrix_ref[z * len(kept) + at]
        terms = [(j, jnp.dot(parts[i], block, preferred_element_type=F32))]
        if i != j:
            turned = (((1,), (1,)), ((), ()))
            terms.append((i, lax.dot_general(parts[j], block, turned, preferred_element_type=F32)))
        for to, term in terms:
            outs[to] = term if outs[to] is None else outs[to] + term
    return jnp.concatenate(outs, axis=1)


def lane_iota():
    return lax.broadcasted_iota(jnp.int32, (8, LANES), 1)


def pick_lanes(tiles, high, low):
    out = None
    for number, tile in enumerate(tiles):
        moved = jnp.take_along_axis(tile, low, axis=1, mode="promise_in_bounds")
        out = moved if out is None else jnp.where(high == number, moved, out)
    return out


def bf16_parts(value, count):
    parts = []
    for _ in range(count):
        parts.append(value.astype(jnp.bfloat16))
        value = value - parts[-1].astype(F32)
    return jnp.concatenate(parts, axis=0)


def pack_sums(nz, terms, numbers):
    slot = lax.broadcasted_iota(jnp.int32, (terms.shape[1], LANES), 0)
    lane = lax.broadcasted_iota(jnp.int32, slot.shape, 1)
    level = lax.shift_right_logical(slot, 3) + lax.bitwise_and(slot, 1)
    level = jnp.where(level >= nz, level - nz, level)
    vertex = level * 4 + lax.bitwise_and(lax.shift_right_logical(slot, 1), 3)
    hot = (lax.bitwise_and(lane, PACK - 1) == vertex) & (slot < nz * CORNERS)
    wide = jnp.dot(
        two_parts(terms), jnp.where(hot, 1.0, 0.0).astype(jnp.bfloat16), preferred_element_type=F32
    )
    wide = wide[:8] + wide[8:]
    lane = lane_iota()
    for at, number in enumerate(numbers):
        wide = jnp.where(lax.bitwise_and(lane, PACK - 1) == nz * 4 + at, number, wide)
    sample = lax.broadcasted_iota(jnp.int32, (8, LANES), 0)
    return jnp.sum(jnp.where(lane // PACK == sample, wide, 0.0), axis=0, keepdims=True)


def unpack_sums(sums_ref, spread_ref):
    lane = lane_iota()
    place = lax.broadcasted_iota(jnp.int32, (8, LANES), 0) * PACK + lax.bitwise_and(lane, PACK - 1)
    group = LANES // PACK
    tiles = []
    for first in range(0, sums_ref.shape[0], group):
        tile = jnp.zeros((8, LANES), F32)
        for at in range(group):
            row = jnp.broadcast_to(sums_ref[first + at], (8, LANES))
            row = jnp.take_along_axis(row, place, axis=1, mode="promise_in_bounds")
            tile = jnp.where(lane // PACK == at, row, tile)
        tiles.append(tile)
    parts = bf16_parts(jnp.concatenate(tiles, axis=1), 3)
    total = jnp.dot(parts, spread_ref[...], preferred_element_type=F32)
    return total[:8] + (total[8:16] + total[16:])


def own_vertices(nz, ncoarse, ids):
    at = lane_iota() - ncoarse - NUMBERS
    inside = (at >= 0) & (at < PACK)
    at = jnp.where(inside, at, 0)
    slot = jnp.where(at < nz * 4, (at // 4) * CORNERS + lax.bitwise_and(at, 3) * 2, 0)
    vertex = jnp.take_along_axis(ids, slot, axis=1, mode="promise_in_bounds")
    vertex = jnp.where(at < nz * 4, vertex, ncoarse + at - nz * 4)
    vertex = jnp.where(at < nz * 4 + NUMBERS, vertex, -1)
    return jnp.where(inside, vertex.astype(F32), 0.0)


def spread_kernel(ncoarse, sums_ref, spread_ref):
    lane = lane_iota()
    lane_square = lax.broadcasted_iota(jnp.int32, (LANES, LANES), 1)
    place = ncoarse + NUMBERS + lax.bitwise_and(lane, PACK - 1)
    group = LANES // PACK
    for first in range(0, sums_ref.shape[0], group):
        line = jnp.zeros((8, LANES), F32)
        for at in range(group):
            row = jnp.take_along_axis(sums_ref[first + at], place, axis=1, mode="promise_in_bounds")
            line = jnp.where(lane // PACK == at, row, line)
        column = jnp.broadcast_to(line[0:1].astype(jnp.int32), (LANES, LANES)).T
        hot = jnp.where(column == lane_square, 1.0, 0.0).astype(jnp.bfloat16)
        spread_ref[first * PACK : (first + group) * PACK, :] = hot


def two_parts(value):
    upper = value.astype(jnp.bfloat16)
    lower = (value - upper.astype(F32)).astype(jnp.bfloat16)
    return jnp.concatenate([upper, lower], axis=0)


def lane_sum(tile):
    return jnp.sum(tile, axis=1, keepdims=True)


def order_tiles(order_ref, z):
    high, low = [], []
    for block in range(SIDES):
        row = jnp.broadcast_to(order_ref[z, :, block * LANES : (block + 1) * LANES], (8, LANES))
        high.append(lax.shift_right_logical(row, 7))
        low.append(lax.bitwise_and(row, LANES - 1))
    return high, low


def invert_own_block(rows_ref, place):
    count = rows_ref.shape[0]
    tall = count * 8
    rows = jnp.concatenate([rows_ref[at] for at in range(count)], axis=0)
    lane = lax.broadcasted_iota(jnp.int32, (tall, LANES), 1)
    sub = lax.broadcasted_iota(jnp.int32, (tall, LANES), 0)
    start = jnp.broadcast_to(place, (tall, LANES)) * tall
    block = jnp.take_along_axis(
        rows, jnp.minimum(start + lane, LANES - 1), axis=1, mode="promise_in_bounds"
    )
    diagonal = jnp.take_along_axis(block, sub, axis=1, mode="promise_in_bounds")
    solved = jnp.where(lane == sub, 1.0 / diagonal, 0.0)
    block = block / diagonal
    for q in range(tall - 1):
        solved = jnp.where(sub > q, solved - block[:, q : q + 1] * solved[q : q + 1, :], solved)
    inside = (lane >= start) & (lane < start + tall)
    moved = jnp.take_along_axis(
        solved, jnp.where(inside, lane - start, 0), axis=1, mode="promise_in_bounds"
    )
    rows = jnp.where(inside, moved, rows)
    for at in range(count):
        rows_ref[at] = rows[at * 8 : (at + 1) * 8, :]


def prepare_kernel(
    nz, riding, order_hbm, response_hbm, factor_hbm, corners_hbm, matrix_hbm, mark_ref,
    order_ref, slots_ref, vertex_ref, ids_ref, matrix_ref, place_ref, faces_ref, rows_ref,
    response_ref, factor_ref, corners_ref, done,
):
    pairs = [(order_hbm, order_ref), (response_hbm, response_ref), (factor_hbm, factor_ref)]
    pairs.append((corners_hbm, corners_ref))
    small = len(pairs)
    for z in range(nz):
        for i, j in upper_blocks(matrix_hbm.shape[1]):
            block = matrix_hbm.at[z, pl.ds(i * WIDE, WIDE), pl.ds(j * WIDE, WIDE)]
            pairs.append((block, matrix_ref.at[len(pairs) - small]))
    copies = [pltpu.make_async_copy(*pair, done.at[at]) for at, pair in enumerate(pairs)]
    for copy in copies:
        copy.start()
    for copy in copies[:small]:
        copy.wait()
    rows_ref[...] = jnp.zeros_like(rows_ref)
    for at in range(rows_ref.shape[0]):
        rows_ref[at, :, 0 : factor_ref.shape[1]] = factor_ref[at * 8 : (at + 1) * 8, :]
    if riding:
        invert_own_block(rows_ref, mark_ref[PLACE, 0:1, :])
    response = response_ref[...].astype(F32)
    lane = lane_iota()
    lane_square = lax.broadcasted_iota(jnp.int32, (LANES, LANES), 1)
    ids_ref[...] = jnp.zeros_like(ids_ref)
    for z in range(nz):
        ids_ref[:, z * CORNERS : (z + 1) * CORNERS] = jnp.broadcast_to(corners_ref[z], (8, CORNERS))
    slots = slots_ref.shape[0]
    column = jnp.broadcast_to(ids_ref[0:1, :], (LANES, LANES)).T[:slots]
    for at in range(0, vertex_ref.shape[1], LANES):
        hot = jnp.where(column == lane_square[:slots] + at, 1.0, 0.0)
        vertex_ref[:, at : at + LANES] = hot.astype(jnp.bfloat16)
    pieces = [response[z] for z in range(nz)]
    if slots > nz * CORNERS:
        pieces.append(jnp.zeros((slots - nz * CORNERS, response.shape[2]), F32))
    slots_ref[...] = jnp.concatenate(pieces, axis=0).astype(jnp.bfloat16)
    for z in range(nz):
        total = jnp.zeros((16, SIDES * LANES), F32)
        for block in range(SIDES):
            row = order_ref[z, :, block * LANES : (block + 1) * LANES]
            column = jnp.broadcast_to(row, (LANES, LANES)).T
            hot = jnp.concatenate(
                [
                    jnp.where(column == lane_square + side * LANES, 1.0, 0.0).astype(jnp.bfloat16)
                    for side in range(SIDES)
                ],
                axis=1,
            )
            places = jnp.concatenate([lane.astype(F32), jnp.full((8, LANES), block, F32)], axis=0)
            total += jnp.dot(places.astype(jnp.bfloat16), hot, preferred_element_type=F32)
        own = [response[z][:, side * LANES : (side + 1) * LANES] for side in range(SIDES)]
        for side in range(SIDES):
            span = slice(side * LANES, (side + 1) * LANES)
            low = total[:8, span].astype(jnp.int32)
            high = total[8:, span].astype(jnp.int32)
            place_ref[z, :, span] = (high * LANES + low)[0:1]
            faces_ref[z * SIDES + side] = pick_lanes(own, high, low)
    for copy in copies[small:]:
        copy.wait()


def apart(value, slices, size):
    pieces, at, used = [], 0, 0
    for rows in slices:
        pieces += [jnp.zeros((rows.start - at, size), F32), value[used : used + rows.stop - rows.start]]
        at, used = rows.stop, used + rows.stop - rows.start
    if at < size:
        pieces.append(jnp.zeros((size - at, size), F32))
    return jnp.concatenate(pieces, axis=0)


def factor_kernel(count, mark_ref, *refs):
    *blocks, inverse_ref, square = refs
    size = square.shape[0]
    row = lax.broadcasted_iota(jnp.int32, (size, size), 0)
    column = lax.broadcasted_iota(jnp.int32, (size, size), 1)
    place = mark_ref[PLACE]
    tall = blocks[0].shape[0]
    for at in range(4 * tall):
        tile = blocks[0][at % tall]
        for mask, block in zip((1, 3, 2), blocks[1:]):
            tile = jnp.where(lax.bitwise_xor(place, mask) == at // tall, block[at % tall], tile)
        square[at * 8 : (at + 1) * 8, :] = tile
    square[4 * tall * 8 :, :] = jnp.zeros((size - 4 * tall * 8, LANES), F32)
    square[...] = jnp.where(row < count, square[...], jnp.where(row == column, 1.0, 0.0))
    factor = square[...]
    width = count // 4
    inverse = jnp.where(row // width == column // width, factor, 0.0)
    while width < count:
        lower = [slice(at, min(at + width, -(-count // 8) * 8)) for at in range(width, count, 2 * width)]
        below = jnp.where(
            (row // (2 * width) == column // (2 * width)) & (row // width > column // width), factor, 0.0
        )
        part = jnp.concatenate([below[rows] for rows in lower], axis=0)
        left = jnp.concatenate([inverse[rows] for rows in lower], axis=0)
        inner = jnp.dot(part, inverse, precision=lax.Precision.HIGHEST, preferred_element_type=F32)
        change = jnp.dot(
            left, apart(inner, lower, size), precision=lax.Precision.HIGHEST, preferred_element_type=F32
        )
        inverse = inverse - apart(change, lower, size)
        width *= 2
    both = lax.dot_general(
        inverse,
        inverse,
        (((0,), (0,)), ((), ())),
        precision=lax.Precision.HIGHEST,
        preferred_element_type=F32,
    )
    inverse_ref[...] = jnp.where((row < count) & (column < count), both, 0.0)


def send_side(nz, mark_ref, axis, faces, outs):
    even = mark_ref[PARITY + axis] == 0
    first, second = outs
    for z in range(nz):
        up, down = faces[z * SIDES + 3 + axis], faces[z * SIDES + axis]
        first[z] = jnp.where(even, up, down)
        second[z] = jnp.where(even, down, up)


def local_part(nz, ncoarse, residual, image, refs, ids=None):
    (order_ref, matrix_ref, slots_ref, vertex_ref, place_ref, faces_ref, sums_ref) = refs
    own, back = residual
    lane = lane_iota()
    norm = jnp.zeros((8, LANES), F32)
    cross = jnp.zeros((8, LANES), F32)
    for at in range(nz * 3):
        norm += own[at] * own[at]
        if image is not None:
            cross += own[at] * image[at]
    energy = jnp.zeros((8, LANES), F32)
    parts, results = [], []
    for z in range(nz):
        sides = [
            -back[z],
            -back[nz + z],
            -own[((z - 1) % nz) * 3 + 2],
            own[z * 3],
            own[z * 3 + 1],
            own[z * 3 + 2],
        ]
        high, low = order_tiles(order_ref, z)
        vector = jnp.concatenate([pick_lanes(sides, high[s], low[s]) for s in range(SIDES)], axis=1)
        parts.append(two_parts(vector))
        solved = symmetric_dot(parts[z], matrix_ref, z)
        solved = solved[:8] + solved[8:]
        results.append([solved[:, s * LANES : (s + 1) * LANES] for s in range(SIDES)])
        for s in range(SIDES):
            energy += results[z][s] * vector[:, s * LANES : (s + 1) * LANES]
    numbers = (lane_sum(norm), lane_sum(cross), lane_sum(energy))
    products = lax.dot_general(
        jnp.concatenate(parts, axis=0), slots_ref[...], (((1,), (1,)), ((), ())),
        preferred_element_type=F32,
    )
    slot = lax.broadcasted_iota(jnp.int32, (8, products.shape[1]), 1)
    terms = jnp.zeros(slot.shape, F32)
    for z in range(nz):
        both = products[z * 16 : z * 16 + 8] + products[z * 16 + 8 : z * 16 + 16]
        terms = jnp.where(lax.shift_right_logical(slot, 3) == z, both, terms)
    if sums_ref.shape[1] == 1:
        row = pack_sums(nz, terms, numbers)
        for copy in range(sums_ref.shape[0]):
            sums_ref[copy] = row
    else:
        by_vertex = jnp.dot(two_parts(terms), vertex_ref[...], preferred_element_type=F32)
        by_vertex = by_vertex[:8] + by_vertex[8:]
        blocks = vertex_ref.shape[1] // LANES
        for block in range(blocks):
            where = lane + block * LANES
            tile = by_vertex[:, block * LANES : (block + 1) * LANES]
            for at, number in enumerate(numbers):
                tile += jnp.where(where == ncoarse + at, number, 0.0)
            if ids is not None:
                tile += own_vertices(nz, ncoarse, ids)
            for copy in range(0, sums_ref.shape[0], blocks):
                sums_ref[copy + block] = tile
    faces = []
    for z in range(nz):
        high, low = order_tiles(place_ref, z)
        for s in range(SIDES):
            at = z * SIDES + s
            faces.append(pick_lanes(results[z], high[s], low[s]))
            faces_ref[at] = faces[at]
    return faces


def start_kernel(
    packed, nz, ncoarse, mark_ref, rhs_ref, back_x_ref, back_y_ref, order_ref, matrix_ref,
    slots_ref, vertex_ref, place_ref, ids_ref, response_faces_ref,
    residual_ref, faces_ref, sums_ref, x_first, x_second, y_first, y_second,
):
    own = [rhs_ref[at] for at in range(nz * 3)]
    back = [back_x_ref[z * 3] for z in range(nz)] + [back_y_ref[z * 3 + 1] for z in range(nz)]
    for at, tile in enumerate(own + back):
        residual_ref[at] = tile
    refs = (order_ref, matrix_ref, slots_ref, vertex_ref, place_ref, faces_ref, sums_ref)
    faces = local_part(nz, ncoarse, (own, back), None, refs, ids_ref[...] if packed else None)
    numbers = ids_ref[...].astype(F32)
    responses = [response_faces_ref[at] for at in range(nz * SIDES)]
    for axis, outs in ((0, (x_first, x_second)), (1, (y_first, y_second))):
        send_side(nz, mark_ref, axis, faces, outs)
        send_side(nz, mark_ref, axis, responses, [out.at[nz : 2 * nz] for out in outs])
        for out in outs:
            out[2 * nz] = numbers


def start_order(first, last):
    if last:
        return (0, 1)
    return (3, 2, 1, 0) if first else (3, 1, 0, 2)


def lift(tile, response, picked, slot, wide):
    for corner in range(CORNERS):
        at = slot * CORNERS + corner
        if at not in wide:
            wide[at] = jnp.broadcast_to(picked[:, at : at + 1], (8, LANES))
        tile = tile + wide[at] * response[corner : corner + 1, :]
    return tile


def corner_values(coarse, ids):
    return pick_lanes(coarse, lax.shift_right_logical(ids, 7), lax.bitwise_and(ids, LANES - 1))


def near_sides(last):
    return (AHEAD_X, AHEAD_Y) if last else range(4)


def sums_kernel(first, last, nz, ncoarse, *refs):
    refs = list(refs)

    def take(count):
        taken = refs[:count]
        del refs[:count]
        return taken

    sums_ref, inverse_ref = take(2)
    packed = sums_ref.shape[1] == 1
    if packed:
        (spread_ref,) = take(1)
    faces_ref, response_faces_ref, residual_ref, ids_ref = take(4)
    if not first:
        near_ref, scalars_ref = take(2)
    if not first and not last:
        direction_ref, multipliers_ref = take(2)
    out_scalars, out_lifted, out_rest = take(3)
    if not last:
        out_direction, out_multipliers = take(2)

    blocks = inverse_ref.shape[0] // LANES
    if packed:
        sums = [unpack_sums(sums_ref, spread_ref)]
    else:
        sums = [sums_ref[block] for block in range(blocks)]
        for copy in range(blocks, sums_ref.shape[0], blocks):
            sums = [total + sums_ref[copy + block] for block, total in enumerate(sums)]
    coarse = jnp.dot(
        jnp.concatenate(sums, axis=1),
        inverse_ref[...],
        precision=lax.Precision.HIGHEST,
        preferred_element_type=F32,
    )
    coarse = [coarse[:, b * LANES : (b + 1) * LANES] for b in range(coarse.shape[1] // LANES)]
    energy = sum(lane_sum(a * b) for a, b in zip(sums, coarse))

    def number(at):
        block, place = divmod(ncoarse + at, LANES)
        return jnp.broadcast_to(sums[block][:, place : place + 1], (8, LANES))

    norm, cross, energy = number(0), number(1), jnp.broadcast_to(energy, (8, LANES)) + number(2)
    if first:
        ratio, curvature = jnp.zeros_like(norm), energy
    else:
        ratio = norm / scalars_ref[2]
        curvature = energy + 2.0 * ratio * cross + ratio * ratio * scalars_ref[3]
    step = norm / curvature
    for at, value in enumerate((step, ratio, norm, curvature)):
        out_scalars[at] = value

    picked, wide = corner_values(coarse, ids_ref[...]), {}
    for z in range(nz):
        for side in range(SIDES):
            at = z * SIDES + side
            out_lifted[at] = lift(faces_ref[at], response_faces_ref[at], picked, z, wide)
    if first:
        for block, tile in enumerate(coarse):
            out_rest[block] = tile
    else:
        none = jnp.zeros((8, LANES), F32)
        for side in near_sides(last):
            for z in range(nz):
                at = side * nz + z
                out_rest[at] = lift(none, near_ref[at], picked, nz * (side + 1) + z, wide)
    if last:
        return
    for at in range(nz * 3):
        direction = residual_ref[at] if first else residual_ref[at] + ratio * direction_ref[at]
        out_multipliers[at] = step * direction if first else multipliers_ref[at] + step * direction
        out_direction[at] = direction


def faces_kernel(first, last, nz, ncoarse, *refs):
    refs = list(refs)

    def take(count):
        taken = refs[:count]
        del refs[:count]
        return taken

    mark_ref, scalars_ref, lifted_ref, rest_ref = take(4)
    order = start_order(first, last)
    received = [got for _, got in sorted(zip(order, take(len(order))), key=lambda pair: pair[0])]
    (residual_ref,) = take(1)
    if first:
        (ids_ref,) = take(1)
    else:
        (image_ref,) = take(1)
    if not last:
        order_ref, matrix_ref, slots_ref, vertex_ref, place_ref = take(5)
        out_residual, out_image, out_faces, out_sums = take(4)
        sends = take(len(refs) - (2 if first else 0))
        if first:
            out_ids, out_near = take(2)
    else:
        direction_ref, multipliers_ref, out_residual, out_multipliers = take(4)

    even_x, even_y = mark_ref[PARITY] == 0, mark_ref[PARITY + 1] == 0
    lane = lane_iota()

    def ahead_and_back(at):
        if last:
            return {AHEAD_X: received[0][at], AHEAD_Y: received[1][at]}
        x_first, x_second, y_first, y_second = [ref[at] for ref in received]
        return {
            AHEAD_X: jnp.where(even_x, x_first, x_second),
            BACK_X: jnp.where(even_x, x_second, x_first),
            AHEAD_Y: jnp.where(even_y, y_first, y_second),
            BACK_Y: jnp.where(even_y, y_second, y_first),
        }

    near = {}
    for z in range(nz):
        for side, tile in ahead_and_back(z).items():
            near[side, z] = tile
    if first:
        ids = ids_ref[...]
        for side, tile in ahead_and_back(2 * nz).items():
            shift = nz * CORNERS * (side + 1)
            moved = pltpu.roll(tile, shift, axis=1).astype(jnp.int32)
            ids = jnp.where((lane >= shift) & (lane < shift + nz * CORNERS), moved, ids)
        out_ids[...] = ids
        picked = corner_values([rest_ref[block] for block in range(rest_ref.shape[0])], ids)
        wide = {}
        for z in range(nz):
            for side, tile in ahead_and_back(nz + z).items():
                near[side, z] = lift(near[side, z], tile, picked, nz * (side + 1) + z, wide)
                out_near[side * nz + z] = tile
    else:
        for z in range(nz):
            for side in near_sides(last):
                near[side, z] = near[side, z] + rest_ref[side * nz + z]

    def own_side(z, side):
        return lifted_ref[z * SIDES + side]

    fresh = [None] * (nz * 5)
    for z in range(nz):
        fresh[z * 3] = own_side(z, 3) - near[AHEAD_X, z]
        fresh[z * 3 + 1] = own_side(z, 4) - near[AHEAD_Y, z]
        fresh[z * 3 + 2] = own_side(z, 5) - own_side((z + 1) % nz, 2)
        if not last:
            fresh[nz * 3 + z] = near[BACK_X, z] - own_side(z, 0)
            fresh[nz * 4 + z] = near[BACK_Y, z] - own_side(z, 1)

    step, ratio = scalars_ref[0], scalars_ref[1]
    count = nz * 3 if last else nz * 5
    residual, image = [], []
    for at in range(count):
        image.append(fresh[at] if first else fresh[at] + ratio * image_ref[at])
        residual.append(residual_ref[at] - step * image[at])
        out_residual[at] = residual[at]
        if not last:
            out_image[at] = image[at]
    if last:
        for at in range(nz * 3):
            direction = residual_ref[at] + ratio * direction_ref[at]
            out_multipliers[at] = multipliers_ref[at] + step * direction
        return
    refs = (order_ref, matrix_ref, slots_ref, vertex_ref, place_ref, out_faces, out_sums)
    faces = local_part(nz, ncoarse, (residual[: nz * 3], residual[nz * 3 :]), image, refs)
    if len(sends) == 2:
        for axis, out in enumerate(sends):
            for z in range(nz):
                out[z] = faces[z * SIDES + axis]
    else:
        send_side(nz, mark_ref, 0, faces, sends[:2])
        send_side(nz, mark_ref, 1, faces, sends[2:])


def tiles(count, kind=F32):
    return jax.ShapeDtypeStruct((count, 8, LANES), kind)


def like(value):
    return jax.ShapeDtypeStruct(value.shape, value.dtype)


def call(kernel, outs, operands, first_space, flops, scratch=(), hbm=()):
    limit = 16 * 2**20 if max(x.size for x in operands) < 2**21 else 48 * 2**20
    vmem = pl.BlockSpec(memory_space=pltpu.VMEM)
    specs = [pl.BlockSpec(memory_space=first_space)] + [vmem] * (len(operands) - 1)
    operands = list(operands)
    for at in hbm:
        specs[at] = pl.BlockSpec(memory_space=pltpu.HBM)
        operands[at] = pltpu.with_memory_space_constraint(operands[at], pltpu.HBM)
    return pl.pallas_call(
        kernel,
        out_shape=outs,
        in_specs=specs,
        out_specs=[vmem] * len(outs),
        scratch_shapes=scratch,
        compiler_params=pltpu.CompilerParams(vmem_limit_bytes=limit),
        cost_estimate=pl.CostEstimate(flops=flops, bytes_accessed=2**20, transcendentals=0),
    )(*operands)


def shifted(value, axis, steps):
    count = lax.axis_size(axis)
    return lax.ppermute(value, axis, [(i, (i + steps) % count) for i in range(count)])


def paired(value, axis, mask):
    return lax.ppermute(value, axis, [(i, i ^ mask) for i in range(lax.axis_size(axis))])


def paired_other(value, axis):
    count = lax.axis_size(axis)
    return lax.ppermute(value, axis, [(i, (i + 1 if i % 2 else i - 1) % count) for i in range(count)])


def summed(sums, spread):
    if spread:
        return lax.all_to_all(sums, ("sub", "slab"), 0, 0, tiled=True)
    return doubled(doubled(sums, "slab", 1), "sub", 1)


def exchange(sums, sends, spread, rows=None):
    x_first, x_second, y_first, y_second = sends
    near = y_first.shape[0]
    blocks = []
    if rows is not None:
        y_first, y_second = jnp.concatenate([y_first, rows]), jnp.concatenate([y_second, rows])
    sums = summed(sums, spread)
    got_y_second, got_y_first = paired_other(y_second, "slab"), paired(y_first, "slab", 1)
    if rows is not None:
        blocks = [rows, got_y_first[near:], got_y_second[near:], paired(rows, "slab", 2)]
        got_y_first, got_y_second = got_y_first[:near], got_y_second[:near]
    got_x_second, got_x_first = paired_other(x_second, "sub"), paired(x_first, "sub", 1)
    return sums, [got_x_first, got_x_second, got_y_first, got_y_second], blocks


def exchange_last(sums, sends, spread):
    sums = summed(sums, spread)
    return sums, [shifted(sends[0], "sub", -1), shifted(sends[1], "slab", -1)]


def doubled(sums, axis, mask):
    while mask < lax.axis_size(axis):
        sums = sums + paired(sums, axis, mask)
        mask *= 2
    return sums


def coarse_inverse(coarse_factor, width):
    factor = lax.all_gather(coarse_factor, "slab", axis=0, tiled=True)
    count = factor.shape[0]
    inverse = lax.linalg.triangular_solve(
        factor, jnp.eye(count, dtype=F32), left_side=True, lower=True
    )
    both = jnp.dot(inverse.T, inverse, precision=lax.Precision.HIGHEST)
    columns = -(-count // LANES) * LANES
    return jnp.pad(both, ((0, width - count), (0, columns - count)))


def local(interface_rhs, order, inverse_rr, corner_response, corners, coarse_factor):
    nz, samples, dirs, face = interface_rhs.shape[2:]
    ncoarse = coarse_factor.shape[1]
    local_size = SIDES * face
    blocks = -(-(ncoarse + NUMBERS) // LANES)
    rhs = interface_rhs.transpose(0, 1, 2, 4, 3, 5).reshape(nz * dirs, samples, face)
    order = order.reshape(nz, 1, local_size)
    matrices = inverse_rr.reshape(nz, local_size, local_size)
    responses = corner_response.reshape(nz, CORNERS, local_size)
    place = lax.axis_index("slab")
    marks = jnp.stack([lax.axis_index("sub") % 2, place % 2, place]).astype(jnp.int32)
    marks = jnp.broadcast_to(marks[:, None, None], (3, 8, LANES))

    back_x = shifted(rhs, "sub", 1)
    back_y = shifted(rhs, "slab", 1)
    devices = lax.axis_size("sub") * lax.axis_size("slab")
    riding = blocks == 1 and lax.axis_size("slab") == 4 and coarse_factor.shape[0] % 8 == 0
    spread = blocks * devices <= 64
    copies = devices if spread else 1
    packed = spread and riding and devices % (LANES // PACK) == 0
    packed = packed and nz * 4 + NUMBERS <= PACK and ncoarse + NUMBERS + PACK <= LANES
    tables = nz * SIDES
    rows = coarse_factor.shape[0] // 8 if riding else 1
    part = coarse_factor[: rows * 8, :LANES]
    kept = nz * len(upper_blocks(local_size))
    kept = jax.ShapeDtypeStruct((kept, WIDE, WIDE), matrices.dtype)
    slots = -(-nz * CORNERS // 16) * 16
    order, slots, vertex, ids, matrices, unorder, response_faces, rows = call(
        functools.partial(prepare_kernel, nz, riding),
        [like(order), jax.ShapeDtypeStruct((slots, local_size), jnp.bfloat16),
         jax.ShapeDtypeStruct((slots, blocks * LANES), jnp.bfloat16),
         jax.ShapeDtypeStruct((8, LANES), jnp.int32), kept, like(order), tiles(tables), tiles(rows)],
        [order, responses, part, corners.reshape(nz, 1, CORNERS), matrices, marks],
        pltpu.HBM,
        2**30,
        [pltpu.VMEM(responses.shape, responses.dtype), pltpu.VMEM(part.shape, F32),
         pltpu.VMEM((nz, 1, CORNERS), jnp.int32), pltpu.SemaphoreType.DMA((4 + kept.shape[0],))],
        range(5),
    )
    own = [order, matrices, slots, vertex, unorder]
    residual, faces, sums, *sends = call(
        functools.partial(start_kernel, packed, nz, ncoarse),
        [tiles(nz * 5), tiles(tables), tiles(blocks * copies)]
        + [tiles(2 * nz + 1)] * 4,
        [marks, rhs, back_x, back_y] + own + [ids, response_faces],
        pltpu.VMEM,
        2**30,
    )

    def invert(factor):
        if not riding:
            return coarse_inverse(coarse_factor, blocks * LANES)
        square = jax.ShapeDtypeStruct((LANES, LANES), F32)
        return call(
            functools.partial(factor_kernel, ncoarse), [square], [marks] + factor,
            pltpu.VMEM, 2**29, [pltpu.VMEM(square.shape, F32)],
        )[0]

    for iteration in range(ITERS):
        first, last = iteration == 0, iteration == ITERS - 1
        if last:
            sums, received = exchange_last(sums, sends, spread)
        else:
            ride = rows if first and riding else None
            sums, received, factor = exchange(sums, sends, spread, ride)
        if first:
            inverse = invert(factor)
        if first and packed:
            wide = jax.ShapeDtypeStruct((devices * PACK, LANES), jnp.bfloat16)
            scatter = call(
                functools.partial(spread_kernel, ncoarse), [wide], [sums], pltpu.VMEM, 2**26
            )
        rows_at = list(scatter) if packed and not first else []
        kept = [ids] if first else [ids, near, step]
        if not first and not last:
            kept += [direction, multipliers]
        rest = inverse.shape[1] // LANES if first else nz * 4
        outs = [tiles(4), tiles(tables), tiles(rest)] + [tiles(nz * 3)] * (0 if last else 2)
        step, lifted, rest, *moved = call(
            functools.partial(sums_kernel, first, last, nz, ncoarse), outs,
            [sums, inverse] + rows_at + [faces, response_faces, residual] + kept, pltpu.VMEM, 2**29,
        )
        operands = [marks, step, lifted, rest]
        operands += [received[at] for at in start_order(first, last)]
        operands += [residual, ids if first else image]
        kernel = functools.partial(faces_kernel, first, last, nz, ncoarse)
        if last:
            operands += [direction, multipliers]
            residual, multipliers = call(kernel, [tiles(nz * 3)] * 2, operands, pltpu.VMEM, 2**28)
            break
        direction, multipliers = moved
        sides = 2 if iteration == ITERS - 2 else 4
        outs = [tiles(nz * 5), tiles(nz * 5), tiles(tables)]
        outs += [jax.ShapeDtypeStruct((copies, 1, LANES), F32) if packed else tiles(blocks * copies)]
        outs += [tiles(nz)] * sides
        if first:
            outs += [jax.ShapeDtypeStruct((8, LANES), jnp.int32), tiles(nz * 4)]
        results = call(kernel, outs, operands + own, pltpu.VMEM, 2**31)
        residual, image, faces, sums = results[:4]
        sends = results[4 : 4 + sides]
        if first:
            ids, near = results[4 + sides :]

    def placed(value):
        value = value.reshape(interface_rhs.shape[:3] + (dirs, samples, face))
        return value.transpose(0, 1, 2, 4, 3, 5)

    return placed(multipliers), placed(residual)


def solution(mesh):
    in_specs = (
        P("sub", "slab", None, None, None, None),
        P("sub", "slab", None, None),
        P("sub", "slab", None, None, None),
        P("sub", "slab", None, None, None),
        P("sub", "slab", None, None),
        P("slab", None),
    )
    out_specs = (P("sub", "slab", None, None, None, None), P("sub", "slab", None, None, None, None))
    return jax.shard_map(local, mesh=mesh, in_specs=in_specs, out_specs=out_specs, check_vma=False)
```
